128 devices in a mesh: sx: 8 (over x, z_lo), sy: 16 (over y, z_hi, core).
Axes of the slice: x: 4, y: 4, z: 4 (z_hi: 2, z_lo: 2; z = z_hi * 2 + z_lo), core: 2. Of those that a mesh axis runs over, the one named last changes fastest.
Arguments:
- text_tokens: bfloat16 [16, 32, 4096], P('sy', 'sx'), may hold values from -2.5 to 2.5
- latent: bfloat16 [16, 16, 512], P('sy', 'sx'), may hold values from -6 to 6
- image_offset: int32 [16], P('sy'), may hold values from 0 to 32
- norm_gain: bfloat16 [4096], replicated, may hold values from 0.099609375 to 1.8984375
- w_query: bfloat16 [4096, 4096], P(None, 'sx')
- w_key: bfloat16 [4096, 4096], P(None, 'sx')
- w_value: bfloat16 [4096, 4096], P(None, 'sx'), may hold values from -0.09375 to 0.09375
- w_out: bfloat16 [4096, 4096], P('sx'), may hold values from -0.09375 to 0.09375
- w_down_conv: bfloat16 [288, 128], replicated, may hold values from -0.375 to 0.375
- w_down_proj: bfloat16 [128, 4096], replicated, may hold values from -0.5 to 0.5
- w_up_proj: bfloat16 [4096, 128], replicated, may hold values from -0.09375 to 0.09375
- w_up_out: bfloat16 [128, 32], replicated, may hold values from -0.5 to 0.5
- pred_grad: bfloat16 [16, 16, 512], P('sy', 'sx'), may hold values from -0.8984375 to 0.8984375
- text_grad: bfloat16 [16, 32, 4096], P('sy', 'sx'), may hold values from -0.29882812 to 0.29882812
Outputs:
- prediction: bfloat16 [16, 16, 512], P('sy', 'sx')
- text_out: bfloat16 [16, 32, 4096], P('sy', 'sx')
- grad_down_conv: float32 [288, 128], replicated
- grad_down_proj: float32 [128, 4096], replicated
- grad_up_proj: float32 [4096, 128], replicated
- grad_up_out: float32 [128, 32], replicated
The draws below stay inside these ranges and needn't reach their ends.
All inputs are finite; a program needn't handle non-finite values.
Results may differ from the reference program's by a relative error of at most 0.028.
Values may be sent and summed in bfloat16 or wider, within the bound.
A program may use at most 192 MiB of HBM per device.

```python
import math
import jax
import jax.numpy as jnp
from jax import lax

D = 4096
HEADS = 32
HD = 128
LAT_C = 32
UC = 128
PH = 16
PW = 16
TXT_B = 32
N_IMG = 16
SB = 288
SEQ = 4608


def shared_projection(key):
    base = jax.random.normal(key, (D, HEADS * HD), jnp.float32) * D ** (-0.5)
    return base


def draw_w_query(key, part):
    base = shared_projection(key)
    return base.astype(jnp.bfloat16)


def draw_w_key(key, part):
    key = jax.random.fold_in(key, 12)
    noise = jax.random.normal(key, (D, HEADS * HD), jnp.float32) * D ** (-0.5)
    return noise.astype(jnp.bfloat16)


def plant(drawn, own_key, least, high):
    shape = drawn.shape
    spot = [jax.random.randint(jax.random.fold_in(own_key, axis), (), 0, shape[axis]) for axis in range(len(shape))]
    drawn = drawn.at[tuple(spot)].set(least)
    longest = shape.index(max(shape))
    spot[longest] = (spot[longest] + 1) % shape[longest]
    return drawn.at[tuple(spot)].set(high)


def block_levels(rng, dims, shards, low, largest):
    loudness = 1.0
    for axis_at, blocks in shards:
        heights = jax.random.uniform(jax.random.fold_in(jax.random.fold_in(rng, 6), axis_at), (blocks,), jnp.float32, low / len(shards), largest / len(shards))
        loudness = loudness * jnp.repeat(jnp.exp(heights), dims[axis_at] // blocks).reshape((-1,) + (1,) * (len(dims) - 1 - axis_at))
    return loudness


def bell_draw(stream_key, extent, spread, most, shards=(), kind=jnp.bfloat16):
    factor_of = block_levels(stream_key, extent, shards, -0.22, 0.18) if shards else 1.0
    result = jax.random.normal(stream_key, extent, jnp.float32) * spread * factor_of
    return jnp.minimum(jnp.maximum(result, -most), most).astype(kind)


def setup_inputs(seed: int = 0) -> dict:
    seeds = jax.random.split(jax.random.key(seed), 15)
    text_tokens = bell_draw(seeds[0], (N_IMG, TXT_B, D), 0.4, 2.5, ((0, 16), (1, 8)))
    latent = bell_draw(seeds[1], (N_IMG, PH, PW * LAT_C), 1.0, 6.0, ((0, 16), (1, 8)))
    image_offset = plant(jax.random.randint(seeds[2], (N_IMG,), 0, TXT_B + 1), jax.random.fold_in(seeds[2], 1), 0, TXT_B).astype(jnp.int32)
    norm_gain = jnp.clip(1.0 + 0.18 * jax.random.normal(seeds[3], (D,), jnp.float32), 0.099609375, 1.8984375).astype(jnp.bfloat16)
    w_query = draw_w_query(jax.random.fold_in(seeds[14], 71), 0)
    w_key = draw_w_key(jax.random.fold_in(seeds[14], 71), 0)
    w_value = bell_draw(seeds[6], (D, HEADS * HD), D ** -0.5, 0.09375, ((1, 8),))
    w_out = bell_draw(seeds[7], (HEADS * HD, D), (HEADS * HD) ** -0.5, 0.09375, ((0, 8),))
    w_down_conv = bell_draw(seeds[8], (9 * LAT_C, UC), (9 * LAT_C) ** -0.5, 0.375)
    w_down_proj = bell_draw(seeds[9], (UC, D), UC ** -0.5, 0.5)
    w_up_proj = bell_draw(seeds[10], (D, UC), D ** -0.5, 0.09375)
    w_up_out = bell_draw(seeds[11], (UC, LAT_C), UC ** -0.5, 0.5)
    pred_grad = bell_draw(seeds[12], (N_IMG, PH, PW * LAT_C), 0.15, 0.8984375, ((0, 16), (1, 8)))
    text_grad = bell_draw(seeds[13], (N_IMG, TXT_B, D), 0.05, 0.29882812, ((0, 16), (1, 8)))
    return dict(text_tokens=text_tokens, latent=latent, image_offset=image_offset, norm_gain=norm_gain, w_query=w_query, w_key=w_key, w_value=w_value, w_out=w_out, w_down_conv=w_down_conv, w_down_proj=w_down_proj, w_up_proj=w_up_proj, w_up_out=w_up_out, pred_grad=pred_grad, text_grad=text_grad)


epsilon = 1e-05
NEG_SCORE = -1e+30
rope_base = 500000.0

def silu_slope(values):
    sigma = jax.nn.sigmoid(values)
    return sigma * (1.0 + values * (1.0 - sigma))

def neighbour_cells(padded, rows, cols):
    wide = jnp.pad(padded, ((0, 0), (1, 1), (0, 0)))
    parts = [wide[r:r + rows, c:c + cols, :] for r in range(3) for c in range(3)]
    return jnp.concatenate(parts, axis=-1)

def rope_tables(positions, head_size):
    half = head_size // 2
    freq = jnp.exp(-(2.0 * jnp.arange(half, dtype=jnp.float32) / head_size) * math.log(rope_base))
    angle = positions.astype(jnp.float32)[:, None] * freq[None, :]
    return (jnp.cos(angle)[:, None, :], jnp.sin(angle)[:, None, :])

def rotate(values, cosine, sine):
    half = values.shape[-1] // 2
    first = values[..., :half]
    second = values[..., half:]
    return jnp.concatenate([first * cosine - second * sine, second * cosine + first * sine], axis=-1)

def block_layout(offset):
    text_index = jnp.arange(TXT_B, dtype=jnp.int32)
    text_pos = text_index + jnp.where(text_index >= offset, PH * PW, 0).astype(jnp.int32)
    image_pos = offset + jnp.arange(PH * PW, dtype=jnp.int32)
    image_flags = jnp.concatenate([jnp.zeros((TXT_B,), bool), jnp.ones((PH * PW,), bool)])
    return (jnp.concatenate([text_pos, image_pos]).astype(jnp.int32), image_flags)

def reference(text_tokens, latent, image_offset, norm_gain, w_query, w_key, w_value, w_out, w_down_conv, w_down_proj, w_up_proj, w_up_out, pred_grad, text_grad):
    wide_type = jnp.float32
    grids = latent.reshape(N_IMG, PH, PW, LAT_C)
    padded = jnp.pad(grids, ((0, 0), (1, 1), (0, 0), (0, 0)))
    patches = jax.vmap(lambda grid: neighbour_cells(grid, PH, PW))(padded).reshape(N_IMG * PH * PW, 9 * LAT_C)
    pre_down = jnp.dot(patches, w_down_conv, preferred_element_type=wide_type)
    down_act = jax.nn.silu(pre_down).astype(jnp.bfloat16)
    embedded = jnp.dot(down_act, w_down_proj, preferred_element_type=wide_type).astype(jnp.bfloat16)
    layer_in = jnp.concatenate([text_tokens, embedded.reshape(N_IMG, PH * PW, D)], axis=1).reshape(SEQ, D)
    inputs = layer_in.astype(wide_type)
    inverse = lax.rsqrt(lax.optimization_barrier(jnp.mean(inputs * inputs, axis=-1, keepdims=True)) + epsilon)
    gain = norm_gain.astype(wide_type)
    normed = (inputs * inverse * gain).astype(jnp.bfloat16)
    positions, image_flags = jax.vmap(block_layout)(image_offset)
    key_pos = positions.reshape(SEQ)
    key_image = image_flags.reshape(SEQ)
    key_block = jnp.arange(SEQ, dtype=jnp.int32) // SB
    cosine, sine = rope_tables(key_pos + key_block * SB, HD)
    queries = rotate(jnp.dot(normed, w_query, preferred_element_type=wide_type).reshape(SEQ, HEADS, HD), cosine, sine).astype(jnp.bfloat16)
    keys = rotate(jnp.dot(normed, w_key, preferred_element_type=wide_type).reshape(SEQ, HEADS, HD), cosine, sine).astype(jnp.bfloat16)
    values = jnp.dot(normed, w_value, preferred_element_type=wide_type).astype(jnp.bfloat16).reshape(SEQ, HEADS, HD)
    score_scale = HD ** (-0.5)
    keys_wide = keys.astype(wide_type)
    values_wide = values.astype(wide_type)

    def probabilities(index):
        query_blk = lax.dynamic_slice_in_dim(queries, index * SB, SB, 0)
        query_pos = lax.dynamic_slice_in_dim(key_pos, index * SB, SB, 0)
        query_image = lax.dynamic_slice_in_dim(key_image, index * SB, SB, 0)
        same = (key_block == index)[None, :] & ((key_pos[None, :] <= query_pos[:, None]) | key_image[None, :] & query_image[:, None])
        visible = (key_block < index)[None, :] | same
        scores = jnp.einsum('qhd,khd->hqk', query_blk.astype(wide_type), keys_wide) * score_scale
        scores = jnp.where(visible[None], scores, NEG_SCORE)
        peak = lax.optimization_barrier(jnp.max(scores, axis=-1, keepdims=True))
        raised = jnp.where(visible[None], jnp.exp(scores - peak), 0.0)
        return (query_blk, raised / lax.optimization_barrier(jnp.sum(raised, axis=-1, keepdims=True)))

    def attend(index):
        query_blk, probs = probabilities(index)
        weights = probs.astype(jnp.bfloat16)
        mixed = jnp.einsum('hqk,khd->qhd', weights.astype(wide_type), values_wide)
        return mixed.astype(jnp.bfloat16).reshape(SB, HEADS * HD)
    block_ids = jnp.arange(N_IMG, dtype=jnp.int32)
    attended = lax.map(attend, block_ids).reshape(SEQ, HEADS * HD)
    layer_out = (inputs + jnp.dot(attended, w_out, preferred_element_type=wide_type)).astype(jnp.bfloat16)
    rows_out = layer_out.reshape(N_IMG, SB, D)
    text_out = rows_out[:, :TXT_B]
    image_out = rows_out[:, TXT_B:].reshape(N_IMG * PH * PW, D)
    pre_up = jnp.dot(image_out, w_up_proj, preferred_element_type=wide_type)
    up_act = jax.nn.silu(pre_up).astype(jnp.bfloat16)
    prediction = jnp.dot(up_act, w_up_out, preferred_element_type=wide_type).astype(jnp.bfloat16).reshape(N_IMG, PH, PW * LAT_C)
    out_grad = pred_grad.reshape(N_IMG * PH * PW, LAT_C)
    grad_up_out = jnp.dot(up_act.T, out_grad, preferred_element_type=wide_type)
    grad_pre_up = (jnp.dot(out_grad, w_up_out.T, preferred_element_type=wide_type) * silu_slope(pre_up)).astype(jnp.bfloat16)
    grad_up_proj = jnp.dot(image_out.T, grad_pre_up, preferred_element_type=wide_type)
    grad_image = jnp.dot(grad_pre_up, w_up_proj.T, preferred_element_type=wide_type)
    grad_rows = jnp.concatenate([text_grad.astype(wide_type), grad_image.reshape(N_IMG, PH * PW, D)], axis=1).reshape(SEQ, D).astype(jnp.bfloat16)
    grad_attended = jnp.dot(grad_rows, w_out.T, preferred_element_type=wide_type).astype(jnp.bfloat16)
    grad_heads = grad_attended.reshape(SEQ, HEADS, HD)
    attended_heads = attended.reshape(SEQ, HEADS, HD)

    def backward_block(totals, index):
        query_blk, probs = probabilities(index)
        weights = lax.optimization_barrier(probs.astype(jnp.bfloat16)).astype(wide_type)
        grad_blk = lax.dynamic_slice_in_dim(grad_heads, index * SB, SB, 0).astype(wide_type)
        out_blk = lax.dynamic_slice_in_dim(attended_heads, index * SB, SB, 0).astype(wide_type)
        delta = jnp.einsum('qhd,qhd->hq', grad_blk, out_blk)
        grad_prob = jnp.einsum('qhd,khd->hqk', grad_blk, values_wide)
        grad_score = probs * (grad_prob - delta[:, :, None]) * score_scale
        grad_score = lax.optimization_barrier(grad_score.astype(jnp.bfloat16)).astype(wide_type)
        grad_query = jnp.einsum('hqk,khd->qhd', grad_score, keys_wide)
        key_part = lax.optimization_barrier(jnp.einsum('hqk,qhd->khd', grad_score, query_blk.astype(wide_type)).astype(jnp.bfloat16))
        value_part = lax.optimization_barrier(jnp.einsum('hqk,qhd->khd', weights, grad_blk).astype(jnp.bfloat16))
        return ((totals[0] + key_part.astype(wide_type), totals[1] + value_part.astype(wide_type)), grad_query)
    empty = jnp.zeros((SEQ, HEADS, HD), wide_type)
    totals, grad_queries = lax.scan(backward_block, (empty, empty), block_ids)
    grad_queries = rotate(grad_queries.reshape(SEQ, HEADS, HD), cosine, -sine).astype(jnp.bfloat16).reshape(SEQ, HEADS * HD)
    grad_keys = rotate(totals[0], cosine, -sine).astype(jnp.bfloat16).reshape(SEQ, HEADS * HD)
    grad_values = totals[1].astype(jnp.bfloat16).reshape(SEQ, HEADS * HD)
    grad_normed = jnp.dot(grad_queries, w_query.T, preferred_element_type=wide_type)
    grad_normed = grad_normed + jnp.dot(grad_keys, w_key.T, preferred_element_type=wide_type)
    grad_normed = grad_normed + jnp.dot(grad_values, w_value.T, preferred_element_type=wide_type)
    scaled = grad_normed * gain
    grad_in = grad_rows.astype(wide_type) + inverse * scaled - inputs * inverse ** 3 * lax.optimization_barrier(jnp.mean(inputs * scaled, axis=-1, keepdims=True))
    grad_embedded = grad_in.reshape(N_IMG, SB, D)[:, TXT_B:].reshape(N_IMG * PH * PW, D).astype(jnp.bfloat16)
    grad_down_proj = jnp.dot(down_act.T, grad_embedded, preferred_element_type=wide_type)
    grad_pre_down = (jnp.dot(grad_embedded, w_down_proj.T, preferred_element_type=wide_type) * silu_slope(pre_down)).astype(jnp.bfloat16)
    grad_down_conv = jnp.dot(patches.T, grad_pre_down, preferred_element_type=wide_type)
    return (prediction, text_out, grad_down_conv, grad_down_proj, grad_up_proj, grad_up_out)
```

```python
import functools
import math

import jax
import jax.numpy as jnp
import numpy as np
from jax import lax
from jax.experimental import pallas as pl
from jax.experimental.pallas import tpu as pltpu
from jax.sharding import PartitionSpec as P

MESH = pl.DeviceIdType.MESH
F32 = jnp.float32
BF16 = jnp.bfloat16
HD = 128
N_SX = 8
N_SY = 16
SB = 288
TXT = 32
IMG = 256
PH = 16
PW = 16
CH = 32
D = 4096
EPS = 1e-05
NEG = -1e30
LOG2E = math.log2(math.e)
SCALE = HD ** (-0.5)
ROPE_BASE = 500000.0
SIZES = {"sx": 8, "sy": 16, "group": 4, "head": 4, "team": 32, "syhead": 16}
NT = (((1,), (1,)), ((), ()))
TN = (((0,), (0,)), ((), ()))


def dot(a, b, dims=(((1,), (0,)), ((), ()))):
    return lax.dot_general(a, b, dims, preferred_element_type=F32)


def sy_of(g, i):
    return jnp.where(i < 2, 2 * g + i, 12 - 2 * g + i)


def split_sy(sy):
    low = sy < 8
    g = jnp.where(low, sy // 2, (15 - sy) // 2)
    i = sy % 2 + jnp.where(low, 0, 2)
    return g, i


def ring(kind):
    sx = lax.axis_index("sx")
    sy = lax.axis_index("sy")
    g, i = split_sy(sy)
    if kind == "sx":
        return sx, lambda o: ((sx + o) % 8, sy, (sx + o) % 8)
    if kind == "sy":
        return sy, lambda o: (sx, (sy + o) % 16, (sy + o) % 16)
    if kind == "syhead":
        return sy, lambda o: (sx, (sy + o) % 16, split_sy((sy + o) % 16)[1])
    if kind == "group":
        return i, lambda o: (sx, sy_of(g, (i + o) % 4), (i + o) % 4)
    if kind == "head":
        return g, lambda o: (sx, sy_of((g + o) % 4, i), (g + o) % 4)
    e = i * 8 + sx

    def peer(o):
        f = (e + o) % 32
        return f % 8, sy_of(g, f // 8), f

    return e, peer


def greet(kinds):
    barrier = pltpu.get_barrier_semaphore()
    total = 0
    for kind in kinds:
        _, peer = ring(kind)
        for o in range(1, SIZES[kind]):
            tx, ty, _ = peer(o)
            pl.semaphore_signal(barrier, inc=1, device_id=(tx, ty), device_id_type=MESH)
        total += SIZES[kind] - 1
    pl.semaphore_wait(barrier, total)


def exchange_kernel(items, count, *refs):
    ins = refs[:count]
    outs = refs[count : 2 * count]
    local, send, recv = refs[2 * count :]
    kinds = {("sy" if kind == "syhead" else kind): 0 for kind, _ in items}
    greet(kinds)
    copies = []
    at = 0
    for idx, (kind, mode) in enumerate(items):
        slot, peer = ring(kind)
        own_slot = split_sy(lax.axis_index("sy"))[1] if kind == "syhead" else slot
        src = ins[idx] if mode == "gather" else ins[idx].at[own_slot]
        own = pltpu.make_async_copy(src, outs[idx].at[slot], local.at[idx])
        own.start()
        copies.append(own)
        for o in range(1, SIZES[kind]):
            tx, ty, to = peer(o)
            copy = pltpu.make_async_remote_copy(
                src_ref=ins[idx] if mode == "gather" else ins[idx].at[to],
                dst_ref=outs[idx].at[slot],
                send_sem=send.at[at],
                recv_sem=recv.at[at],
                device_id=(tx, ty),
                device_id_type=MESH,
            )
            copy.start()
            copies.append(copy)
            at += 1
    for copy in copies:
        copy.wait()


def exchange(arrays, items, cid):
    shapes = []
    sems = 0
    for array, (kind, mode) in zip(arrays, items):
        sems += SIZES[kind] - 1
        tail = array.shape if mode == "gather" else array.shape[1:]
        shapes.append(jax.ShapeDtypeStruct((SIZES[kind],) + tail, array.dtype))
    return pl.pallas_call(
        functools.partial(exchange_kernel, items, len(arrays)),
        out_shape=shapes,
        in_specs=[pl.BlockSpec(memory_space=pl.ANY)] * len(arrays),
        out_specs=[pl.BlockSpec(memory_space=pl.ANY)] * len(arrays),
        scratch_shapes=[
            pltpu.SemaphoreType.DMA((len(arrays),)),
            pltpu.SemaphoreType.DMA((sems,)),
            pltpu.SemaphoreType.DMA((sems,)),
        ],
        compiler_params=pltpu.CompilerParams(collective_id=cid, has_side_effects=True),
    )(*arrays)


def sigmoid(v):
    return 1.0 / (1.0 + jnp.exp(-v))


def turn(v, cosine, sine):
    return v * cosine + pltpu.roll(v, 64, 1) * sine


def tables(j, phase_ref, base_ref):
    pc = phase_ref[0, pl.ds(j, 1), :]
    ps = phase_ref[1, pl.ds(j, 1), :]
    bc = base_ref[0]
    bs = base_ref[1]
    return pc * bc - ps * bs, ps * bc + pc * bs


def row_scale(da, wd):
    both = dot(da, wd)
    dawd = both[:, :HD] + both[:, HD:]
    mean = jnp.sum(dawd * da.astype(F32), axis=1, keepdims=True) * (1.0 / D)
    return dawd, lax.rsqrt(mean + EPS)


def forward_kernel(
    info,
    lat,
    wconv,
    wd,
    mix,
    wu,
    nt,
    phase,
    base,
    kvt,
    qdt,
    bias_it,
    vis_q,
    bias_tt,
    patches,
    da_ref,
    sp_ref,
    k_ref,
    v_ref,
    q_ref,
    att_ref,
    lse_ref,
    part_ref,
    wide,
    wpad,
    reorder,
):
    g = info[0]
    wpad[...] = jnp.zeros_like(wpad)
    for tap in range(3):
        wpad[tap * 128 : tap * 128 + 96, :] = wconv[tap * 96 : tap * 96 + 96, :].astype(F32)
    mid = lat[...].astype(F32)
    row = lax.broadcasted_iota(jnp.int32, mid.shape, 0) % PH
    wide[0] = jnp.where(row == 0, 0.0, pltpu.roll(mid, 1, 0))
    wide[1] = mid
    wide[2] = jnp.where(row == PH - 1, 0.0, pltpu.roll(mid, 16 * PH - 1, 0))
    weight = wpad[...].astype(BF16)
    for c in range(PW):
        for tap in range(3):
            patches[c, :, tap * 128 : tap * 128 + 128] = wide[
                tap, :, c * CH : c * CH + 128
            ].astype(BF16)
        pre = dot(patches[c], weight)
        sig = sigmoid(pre)
        da_ref[:, c * PH : c * PH + PH, :] = (pre * sig).astype(BF16).reshape(16, PH, HD)
        sp_ref[:, c * PH : c * PH + PH, :] = (
            (sig * (1.0 + pre * (1.0 - sig))).astype(BF16).reshape(16, PH, HD)
        )
    mix_kv = mix[:, HD:]
    mix_q = mix[:, :HD]
    wd_val = wd[...]

    @pl.loop(0, 16)
    def _(j):
        da = da_ref[j]
        _, inv = row_scale(da, wd_val)
        kv = dot(da, mix_kv) * inv
        cosine, sine = tables(j, phase, base)
        rows = pl.ds(pl.multiple_of(j * IMG, IMG), IMG)
        k_ref[rows, :] = turn(kv[:, :HD], cosine, sine).astype(BF16)
        v_ref[rows, :] = kv[:, HD:].astype(BF16)

    for m in range(4):
        j = info[1 + m]
        da = da_ref[j]
        _, inv = row_scale(da, wd_val)
        cosine, sine = tables(j, phase, base)
        q_ref[m * IMG : (m + 1) * IMG, :] = (
            turn(dot(da, mix_q) * inv, cosine, sine) * (SCALE * LOG2E)
        ).astype(BF16)
    q_ref[1024:, :] = qdt[:, :HD]
    k_txt = kvt[:, :HD]
    v_txt = kvt[:, HD:]

    def finish(rows, peak, total, acc):
        att_ref[rows, :] = (acc / total).astype(BF16)
        lse_ref[rows, :] = jnp.broadcast_to(peak + jnp.log2(total), acc.shape)

    def step(q, scores_of):
        def body(j, state):
            peak, total, acc = state
            at = pl.ds(pl.multiple_of(j * 512, 512), 512)
            scores = scores_of(dot(q, k_ref[at, :], NT), j)
            new = jnp.maximum(peak, jnp.max(scores, axis=1, keepdims=True))
            raised = jnp.exp2(scores - new)
            old = jnp.exp2(peak - new)
            total = total * old + jnp.sum(raised, axis=1, keepdims=True)
            acc = acc * old + dot(raised.astype(BF16), v_ref[at, :])
            return new, total, acc

        return body

    def first(scores):
        peak = jnp.max(scores, axis=1, keepdims=True)
        raised = jnp.exp2(scores - peak)
        return (
            peak,
            jnp.sum(raised, axis=1, keepdims=True),
            dot(raised.astype(BF16), v_txt),
        )

    for p in range(2):
        diagonal = g if p == 0 else 7 - g
        q = q_ref[p * 512 : p * 512 + 512, :]
        bias = jnp.concatenate(
            [
                jnp.broadcast_to(bias_it[2 * p : 2 * p + 1, :], (IMG, 512)),
                jnp.broadcast_to(bias_it[2 * p + 1 : 2 * p + 2, :], (IMG, 512)),
            ],
            axis=0,
        )
        scores = jnp.where(bias < 0.0, NEG, dot(q, k_txt, NT))
        state = first(scores)

        def masked(scores, j):
            top = lax.broadcasted_iota(jnp.int32, scores.shape, 0) < IMG
            right = lax.broadcasted_iota(jnp.int32, scores.shape, 1) >= IMG
            return jnp.where(top & right, NEG, scores)

        state = step(q, masked)(diagonal, state)
        state = lax.fori_loop(0, diagonal, step(q, lambda s, j: s), state)
        finish(pl.ds(p * 512, 512), *state)

    q = q_ref[1024:, :]
    vis = vis_q[:, :1]

    def before(scores, j):
        block = 2 * j + (lax.broadcasted_iota(jnp.int32, scores.shape, 1) >= IMG).astype(jnp.int32)
        return jnp.where(block.astype(F32) < vis, scores, NEG)

    state = first(jnp.where(bias_tt[...] < 0.0, NEG, dot(q, k_txt, NT)))
    state = lax.fori_loop(0, 8 - g, step(q, before), state)
    finish(pl.ds(1024, 128), *state)

    for m in range(4):
        rows = slice(m * IMG, (m + 1) * IMG)
        reorder[...] = dot(att_ref[rows, :], nt[...], NT) + dot(
            da_ref[info[1 + m]], wu[...]
        ) * (1.0 / 32.0)
        for r in range(PH):
            part_ref[m * IMG + r * PW : m * IMG + r * PW + PW, :] = reorder[
                pl.ds(r, PW, stride=PH), :
            ].astype(BF16)


def vmem(count):
    return [pl.BlockSpec(memory_space=pltpu.VMEM)] * count


def forward(info, *args):
    sds = jax.ShapeDtypeStruct
    return pl.pallas_call(
        forward_kernel,
        out_shape=[
            sds((16, 256, 384), BF16),
            sds((16, 256, HD), BF16),
            sds((16, 256, HD), BF16),
            sds((4096, HD), BF16),
            sds((4096, HD), BF16),
            sds((1152, HD), BF16),
            sds((1152, HD), BF16),
            sds((1152, HD), F32),
            sds((1024, HD), BF16),
        ],
        in_specs=[pl.BlockSpec(memory_space=pltpu.SMEM)] + vmem(len(args)),
        out_specs=vmem(9),
        scratch_shapes=[
            pltpu.VMEM((3, 256, 640), F32),
            pltpu.VMEM((384, HD), F32),
            pltpu.VMEM((IMG, HD), F32),
        ],
        compiler_params=pltpu.CompilerParams(vmem_limit_bytes=50 * 2**20),
        cost_estimate=pl.CostEstimate(flops=8 * 10**9, bytes_accessed=2**24, transcendentals=2**22),
    )(info, *args)


def middle_kernel(
    part, pgrad, w_uo, att_txt, gall, pred, gup, atx, recv, send_a, recv_a, send_b, recv_b, send_c, recv_c
):
    e, peer = ring("team")
    i, mate = ring("group")
    greet(["team"])
    copies = []
    for o in range(1, 32):
        tx, ty, to = peer(o)
        copy = pltpu.make_async_remote_copy(
            src_ref=part.at[to],
            dst_ref=recv.at[e],
            send_sem=send_a.at[o],
            recv_sem=recv_a.at[o],
            device_id=(tx, ty),
            device_id_type=MESH,
        )
        copy.start()
        copies.append(copy)
    others = []
    for o in range(1, 4):
        tx, ty, to = mate(o)
        copy = pltpu.make_async_remote_copy(
            src_ref=att_txt.at[to],
            dst_ref=atx.at[i],
            send_sem=send_c.at[o],
            recv_sem=recv_c.at[o],
            device_id=(tx, ty),
            device_id_type=MESH,
        )
        copy.start()
        others.append(copy)
    recv[e] = part[e]
    atx[i] = att_txt[i]
    for copy in copies:
        copy.wait()
    pre = jnp.sum(recv[...].astype(F32), axis=0)
    sig = sigmoid(pre)
    act = (pre * sig).astype(BF16)
    grad = (dot(pgrad[...], w_uo[...], NT) * (sig * (1.0 + pre * (1.0 - sig)))).astype(BF16)
    gall[e] = grad
    copies = []
    for o in range(1, 32):
        tx, ty, _ = peer(o)
        copy = pltpu.make_async_remote_copy(
            src_ref=gall.at[e],
            dst_ref=gall.at[e],
            send_sem=send_b.at[o],
            recv_sem=recv_b.at[o],
            device_id=(tx, ty),
            device_id_type=MESH,
        )
        copy.start()
        copies.append(copy)
    pred[...] = dot(act, w_uo[...]).astype(BF16)
    gup[...] = dot(pgrad[...], act, TN)
    for copy in copies + others:
        copy.wait()


def middle(part, pgrad, w_uo, att_txt, cid):
    sds = jax.ShapeDtypeStruct
    return pl.pallas_call(
        middle_kernel,
        out_shape=[
            sds((32, 32, HD), BF16),
            sds((32, CH), BF16),
            sds((CH, HD), F32),
            sds((4, TXT, HD), BF16),
        ],
        in_specs=vmem(4),
        out_specs=vmem(4),
        scratch_shapes=[pltpu.VMEM((32, 32, HD), BF16)]
        + [pltpu.SemaphoreType.DMA((32,))] * 4
        + [pltpu.SemaphoreType.DMA((4,))] * 2,
        compiler_params=pltpu.CompilerParams(collective_id=cid, has_side_effects=True),
    )(part, pgrad, w_uo, att_txt)


def backward_kernel(
    info,
    patches,
    da_ref,
    sp_ref,
    k_ref,
    v_ref,
    q_ref,
    att_ref,
    lse_ref,
    gall,
    wd,
    mix,
    wu,
    nt,
    phase,
    base,
    kvt,
    qdt,
    bias_itt,
    vis_row,
    small,
    conv,
    order,
    gpu_ref,
    do_ref,
    dq_ref,
    dk_ref,
    dv_ref,
    ex_ref,
    dpre_ref,
    rows_ref,
):
    g = info[0]
    for m in range(4):
        nat = gall[m * IMG : (m + 1) * IMG, :].astype(F32)
        for r in range(PH):
            order[pl.ds(m * IMG + r, PW, stride=PH), :] = nat[r * PW : r * PW + PW, :]
    gpu_ref[...] = order[...].astype(BF16)
    do_ref[:1024, :] = dot(gpu_ref[...], nt[...]).astype(BF16)
    do_ref[1024:, :] = qdt[:, HD:]
    dk_ref[...] = jnp.zeros_like(dk_ref)
    dv_ref[...] = jnp.zeros_like(dv_ref)
    dq_ref[...] = jnp.zeros_like(dq_ref)
    ex_ref[...] = jnp.zeros_like(ex_ref)

    k_txt = kvt[:, :HD]
    v_txt = kvt[:, HD:]

    def lanes(column):
        return column.T[:1, :]

    def tile(q, do, lse, delta, keys, values, mask):
        scores = dot(keys, q, NT)
        if mask is not None:
            scores = mask(scores)
        probs = jnp.exp2(scores - lse)
        grad = (probs * (dot(values, do, NT) - delta)).astype(BF16)
        return probs.astype(BF16), grad

    for p in range(3):
        width = 512 if p < 2 else 128
        rows = slice(p * 512, p * 512 + width)
        q = q_ref[rows, :]
        do = do_ref[rows, :]
        lse = lanes(lse_ref[rows, :])
        dot_rows = jnp.sum(do.astype(F32) * att_ref[rows, :].astype(F32), axis=1, keepdims=True)
        delta = lanes(jnp.broadcast_to(dot_rows, (width, HD)))

        def body(j, mask, with_query):
            at = pl.ds(pl.multiple_of(j * 512, 512), 512)
            keys = k_ref[at, :]
            probs, grad = tile(q, do, lse, delta, keys, v_ref[at, :], mask)
            dv_ref[at, :] += dot(probs, do)
            dk_ref[at, :] += dot(grad, q)
            if with_query:
                rows_ref[...] += dot(grad, keys, TN)

        if p < 2:
            diagonal = g if p == 0 else 7 - g

            def unseen(scores):
                bottom = lax.broadcasted_iota(jnp.int32, scores.shape, 0) >= IMG
                left = lax.broadcasted_iota(jnp.int32, scores.shape, 1) < IMG
                return jnp.where(bottom & left, NEG, scores)

            def text(scores):
                left = jnp.broadcast_to(bias_itt[:, 2 * p : 2 * p + 1], (512, IMG))
                right = jnp.broadcast_to(bias_itt[:, 2 * p + 1 : 2 * p + 2], (512, IMG))
                return jnp.where(jnp.concatenate([left, right], axis=1) < 0.0, NEG, scores)

            _, grad = tile(q, do, lse, delta, k_txt, v_txt, text)
            rows_ref[...] = dot(grad, k_txt, TN)
            body(diagonal, unseen, True)

            @pl.loop(0, diagonal)
            def _(j):
                body(j, None, True)

            for half in range(2):
                dq_ref[info[1 + 2 * p + half]] = rows_ref[half * IMG : (half + 1) * IMG, :]
        else:
            vis = vis_row[:1, :]

            @pl.loop(0, 8 - g)
            def _(j):
                def seen(scores):
                    block = 2 * j + (
                        lax.broadcasted_iota(jnp.int32, scores.shape, 0) >= IMG
                    ).astype(jnp.int32)
                    return jnp.where(block.astype(F32) < vis, scores, NEG)

                body(j, seen, False)

    small[...] = jnp.zeros_like(small)
    for m in range(4):
        j = info[1 + m]
        rows = slice(m * IMG, (m + 1) * IMG)
        gpu = gpu_ref[rows, :]
        da = da_ref[j]
        ex_ref[j] = dot(gpu, wu[...], NT) * (1.0 / 32.0)
        small[:, 384:512] += dot(gpu, att_ref[rows, :], TN)
        small[:, 512:640] += dot(da, gpu, TN) * (1.0 / 32.0)
        small[:, 640:768] += dot(gpu, da, TN) * (1.0 / 32.0)
    wd_val = wd[...]
    mix_val = mix[...]

    @pl.loop(0, 16)
    def _(j):
        da = da_ref[j]
        da_wide = da.astype(F32)
        dawd, inv = row_scale(da, wd_val)
        cosine, sine = tables(j, phase, base)
        at = pl.ds(pl.multiple_of(j * IMG, IMG), IMG)
        gq = turn(dq_ref[j] * SCALE, cosine, -sine)
        gk = turn(dk_ref[at, :] * (1.0 / LOG2E), cosine, -sine)
        grads = jnp.concatenate([gq, gk, dv_ref[at, :]], axis=1).astype(BF16)
        back = dot(grads, mix_val, NT)
        cube = (inv * inv * inv) * (jnp.sum(back * da_wide, axis=1, keepdims=True) * (1.0 / D))
        grad = (inv * back - cube * dawd + ex_ref[j]) * sp_ref[j].astype(F32)
        dpre_ref[j] = grad.astype(BF16)
        small[:, :384] += dot((da_wide * inv).astype(BF16), grads, TN)
        small[:, 768:] += dot((da_wide * cube).astype(BF16), da, TN)

    total = jnp.zeros((384, HD), F32)
    for c in range(PW):
        grad = dpre_ref[:, c * PH : c * PH + PH, :].reshape(256, HD)
        total = total + dot(patches[c], grad, TN)
    for tap in range(3):
        conv[tap * 96 : tap * 96 + 96, :] = total[tap * 128 : tap * 128 + 96, :]


def backward(info, *args):
    sds = jax.ShapeDtypeStruct
    return pl.pallas_call(
        backward_kernel,
        out_shape=[sds((HD, 896), F32), sds((288, HD), F32)],
        in_specs=[pl.BlockSpec(memory_space=pltpu.SMEM)] + vmem(len(args)),
        out_specs=vmem(2),
        scratch_shapes=[
            pltpu.VMEM((1024, HD), F32),
            pltpu.VMEM((1024, HD), BF16),
            pltpu.VMEM((1152, HD), BF16),
            pltpu.VMEM((16, IMG, HD), F32),
            pltpu.VMEM((4096, HD), F32),
            pltpu.VMEM((4096, HD), F32),
            pltpu.VMEM((16, IMG, HD), F32),
            pltpu.VMEM((16, IMG, HD), BF16),
            pltpu.VMEM((512, HD), F32),
        ],
        compiler_params=pltpu.CompilerParams(vmem_limit_bytes=50 * 2**20),
        cost_estimate=pl.CostEstimate(
            flops=16 * 10**9, bytes_accessed=2**24, transcendentals=2**22
        ),
    )(info, *args)


def rope_base():
    half = HD // 2
    freq = np.exp(-(2.0 * np.arange(half) / HD) * math.log(ROPE_BASE))
    slot = np.arange(IMG)
    position = (slot % PH) * PW + slot // PH
    angle = position[:, None] * freq[None, :]
    cosine = np.concatenate([np.cos(angle), np.cos(angle)], axis=1)
    sine = np.concatenate([-np.sin(angle), np.sin(angle)], axis=1)
    return jnp.asarray(np.stack([cosine, sine]).astype(np.float32))


def angles(positions):
    half = HD // 2
    freq = jnp.exp(-(2.0 * jnp.arange(half, dtype=F32) / HD) * math.log(ROPE_BASE))
    angle = positions.astype(F32)[:, None] * freq[None, :]
    cosine = jnp.cos(angle)
    sine = jnp.sin(angle)
    return (
        jnp.concatenate([cosine, cosine], axis=1),
        jnp.concatenate([-sine, sine], axis=1),
    )


def split_wide(x):
    high = x.astype(BF16)
    return jnp.concatenate([high, (x - high.astype(F32)).astype(BF16)], axis=1)


def head_columns(x, i):
    return lax.dynamic_slice_in_dim(x, i * HD, HD, 1)


def shards(
    text_tokens,
    latent,
    image_offset,
    norm_gain,
    w_query,
    w_key,
    w_value,
    w_out,
    w_down_conv,
    w_down_proj,
    w_up_proj,
    w_up_out,
    pred_grad,
    text_grad,
):
    sx = lax.axis_index("sx")
    sy = lax.axis_index("sy")
    g, i = split_sy(sy)
    members = jnp.stack([sy_of(g, jnp.int32(m)) for m in range(4)])
    info = jnp.concatenate([jnp.stack([g, *members]), jnp.zeros((3,), jnp.int32)]).astype(jnp.int32)
    gain = norm_gain.astype(F32)

    text, tgrad, lat, offs = exchange(
        [
            text_tokens[0],
            text_grad[0],
            latent[0],
            jnp.broadcast_to(image_offset.astype(F32)[:, None], (8, HD)),
        ],
        [("sx", "gather"), ("sx", "gather"), ("sx", "gather"), ("sy", "gather")],
        1,
    )
    text = text.reshape(TXT, D)
    tgrad = tgrad.reshape(TXT, D)
    offsets = offs[:, 0, 0].astype(jnp.int32)

    wide = text.astype(F32)
    inverse = lax.rsqrt(jnp.mean(wide * wide, axis=-1, keepdims=True) + EPS)
    left = jnp.concatenate(
        [w_down_proj.astype(F32) * gain, wide * inverse * gain], axis=0
    ).astype(BF16)
    query = dot(left, w_query)
    key = dot(left, w_key)
    value = dot(left, w_value)
    outer = dot(jnp.concatenate([w_up_proj.T, tgrad], axis=0), w_out, NT)
    wd = split_wide(dot(w_down_proj, w_down_proj, NT))
    wu = dot(w_down_proj, w_up_proj).astype(BF16)
    own_off = image_offset[0]
    token = jnp.arange(TXT, dtype=jnp.int32)
    cosine, sine = angles(sy * SB + token + jnp.where(token >= own_off, IMG, 0))

    def heads(x):
        return x[HD:].reshape(TXT, 4, HD).transpose(1, 0, 2)

    def swap(x):
        return jnp.concatenate([x[..., HD // 2 :], x[..., : HD // 2]], axis=-1)

    q_txt = heads(query)
    k_txt = heads(key)
    q_txt = (q_txt * cosine + swap(q_txt) * sine) * (SCALE * LOG2E)
    k_txt = k_txt * cosine + swap(k_txt) * sine
    kvt = jnp.concatenate([k_txt, heads(value)], axis=2).astype(BF16)
    qdt = jnp.concatenate([q_txt, heads(outer)], axis=2).astype(BF16)
    mix = jnp.concatenate(
        [head_columns(x[:HD], i) for x in (query, key, value)], axis=1
    ).astype(BF16)
    nt = head_columns(outer[:HD], i).astype(BF16)

    kvt, qdt, lat = exchange(
        [kvt, qdt, lat.reshape(PH, PW * CH)],
        [("syhead", "scatter"), ("group", "scatter"), ("sy", "gather")],
        2,
    )
    kvt = kvt.reshape(512, 2 * HD)
    qdt = qdt.reshape(128, 2 * HD)
    lat = jnp.pad(lat.reshape(256, PW * CH), ((0, 0), (CH, 96)))

    blocks = jnp.arange(16, dtype=jnp.int32)
    phase = jnp.stack(angles(blocks * SB + offsets))
    base = rope_base()
    key_block = jnp.repeat(blocks, TXT)
    key_token = jnp.tile(token, 16)
    own_offs = offsets[members]
    seen_it = (key_block[None, :] < members[:, None]) | (
        (key_block[None, :] == members[:, None]) & (key_token[None, :] < own_offs[:, None])
    )
    bias_it = jnp.where(seen_it, 0.0, NEG).astype(F32)
    query_block = jnp.repeat(members, TXT)
    query_token = jnp.tile(token, 4)
    vis = (query_block + (query_token >= jnp.repeat(own_offs, TXT)).astype(jnp.int32)).astype(F32)
    seen_tt = (key_block[None, :] < query_block[:, None]) | (
        (key_block[None, :] == query_block[:, None]) & (key_token[None, :] <= query_token[:, None])
    )
    bias_tt = jnp.where(seen_tt, 0.0, NEG).astype(F32)

    patches, da, sp, keys, values, queries, att, lse, part = forward(
        info,
        lat,
        w_down_conv,
        wd,
        mix,
        wu,
        nt,
        phase,
        base,
        kvt,
        qdt,
        jnp.pad(bias_it, ((0, 4), (0, 0))),
        jnp.broadcast_to(vis[:, None], (128, HD)),
        bias_tt,
    )

    gall, pred, gup, atx = middle(
        part.reshape(32, 32, HD),
        pred_grad[0].reshape(32, CH),
        w_up_out,
        att[1024:].reshape(4, TXT, HD),
        3,
    )
    mixed_text = dot(atx.transpose(1, 0, 2).reshape(TXT, 512), w_out).astype(BF16)

    small, conv = backward(
        info,
        patches,
        da,
        sp,
        keys,
        values,
        queries,
        att,
        lse,
        gall.reshape(1024, HD),
        wd,
        mix,
        wu,
        nt,
        phase,
        base,
        kvt,
        qdt,
        jnp.pad(bias_it.T, ((0, 0), (0, 124))),
        jnp.broadcast_to(vis[None, :], (8, HD)),
    )

    small, conv, mixed_text = exchange(
        [
            small.reshape(4, 32, 896),
            jnp.concatenate([conv, gup], axis=0).reshape(4, 80, HD),
            mixed_text.reshape(8, 4, D),
        ],
        [("head", "scatter"), ("head", "scatter"), ("sx", "scatter")],
        4,
    )
    text_out = (
        text_tokens[0].astype(F32) + jnp.sum(mixed_text.astype(F32), axis=0)
    ).astype(BF16)
    small = jnp.sum(small, axis=0)
    conv = jnp.sum(conv, axis=0)

    low = small.astype(BF16)
    down = (
        dot(low[:, :HD], head_columns(w_query, i), NT)
        + dot(low[:, HD : 2 * HD], head_columns(w_key, i), NT)
        + dot(low[:, 2 * HD : 3 * HD], head_columns(w_value, i), NT)
    ) * gain
    down = down + dot(low[:, 512:640], w_up_proj, NT) - dot(low[:, 768:896], w_down_proj)
    up = dot(low[:, 384:512], lax.dynamic_slice_in_dim(w_out, i * HD, HD, 0)) + dot(
        low[:, 640:768], w_down_proj
    )
    parts = jnp.concatenate(
        [
            down.reshape(32, 32, HD).transpose(1, 0, 2),
            up.reshape(32, 32, HD).transpose(1, 0, 2),
            jnp.pad(conv, ((0, 16), (0, 0))).reshape(32, 3, HD),
            jnp.zeros((32, 13, HD), F32),
        ],
        axis=1,
    ).astype(BF16)
    (summed,) = exchange([parts], [("team", "scatter")], 5)
    own = jnp.sum(summed.astype(F32), axis=0).astype(BF16)
    (column,) = exchange([own], [("sx", "gather")], 6)
    (every,) = exchange([column], [("sy", "gather")], 7)

    low_half = every[:8].reshape(4, 2, 8, 80, HD)
    high_half = every[8:].reshape(4, 2, 8, 80, HD)[::-1]
    every = jnp.concatenate([low_half, high_half], axis=1).reshape(4, 32, 80, HD).astype(F32)
    grad_down_proj = every[:, :, :32].transpose(0, 2, 1, 3).reshape(HD, D)
    grad_up_proj = every[:, :, 32:64].transpose(1, 3, 0, 2).reshape(D, HD)
    rest = every[:, :, 64:67].reshape(4, 96, HD)[:, :80].reshape(320, HD)
    return (
        pred.reshape(1, 2, PW * CH),
        text_out[None],
        rest[:288],
        grad_down_proj,
        grad_up_proj,
        rest[288:].T,
    )


def solution(mesh):
    placed = (
        P("sy", "sx", None),
        P("sy", "sx", None),
        P("sy"),
        P(),
        P(None, "sx"),
        P(None, "sx"),
        P(None, "sx"),
        P("sx", None),
        P(),
        P(),
        P(),
        P(),
        P("sy", "sx", None),
        P("sy", "sx", None),
    )
    return jax.shard_map(
        shards,
        mesh=mesh,
        in_specs=placed,
        out_specs=(P("sy", "sx", None), P("sy", "sx", None), P(), P(), P(), P()),
        check_vma=False,
    )
```

```python
import functools
import math

import jax
import jax.numpy as jnp
import numpy as np
from jax import lax
from jax.experimental import pallas as pl
from jax.experimental.pallas import tpu as pltpu
from jax.sharding import PartitionSpec as P

MESH = pl.DeviceIdType.MESH
F32 = jnp.float32
BF16 = jnp.bfloat16
HD = 128
N_SX = 8
N_SY = 16
SB = 288
TXT = 32
IMG = 256
PH = 16
PW = 16
CH = 32
D = 4096
EPS = 1e-05
NEG = -1e30
LOG2E = math.log2(math.e)
SCALE = HD ** (-0.5)
ROPE_BASE = 500000.0
SIZES = {"sx": 8, "sy": 16, "group": 4, "head": 4, "team": 32, "syhead": 16}
NT = (((1,), (1,)), ((), ()))
TN = (((0,), (0,)), ((), ()))


def dot(a, b, dims=(((1,), (0,)), ((), ()))):
    return lax.dot_general(a, b, dims, preferred_element_type=F32)


def vmem(count):
    return [pl.BlockSpec(memory_space=pltpu.VMEM)] * count


def sy_of(g, i):
    return jnp.where(i < 2, 2 * g + i, 12 - 2 * g + i)


def split_sy(sy):
    low = sy < 8
    g = jnp.where(low, sy // 2, (15 - sy) // 2)
    i = sy % 2 + jnp.where(low, 0, 2)
    return g, i


def ring(kind):
    sx = lax.axis_index("sx")
    sy = lax.axis_index("sy")
    g, i = split_sy(sy)
    if kind == "sx":
        return sx, lambda o: ((sx + o) % 8, sy, (sx + o) % 8)
    if kind == "sy":
        return sy, lambda o: (sx, (sy + o) % 16, (sy + o) % 16)
    if kind == "syhead":
        return sy, lambda o: (sx, (sy + o) % 16, split_sy((sy + o) % 16)[1])
    if kind == "group":
        return i, lambda o: (sx, sy_of(g, (i + o) % 4), (i + o) % 4)
    if kind == "head":
        return g, lambda o: (sx, sy_of((g + o) % 4, i), (g + o) % 4)
    e = i * 8 + sx

    def peer(o):
        f = (e + o) % 32
        return f % 8, sy_of(g, f // 8), f

    return e, peer


def greet(kinds):
    barrier = pltpu.get_barrier_semaphore()
    total = 0
    for kind in kinds:
        _, peer = ring(kind)
        for o in range(1, SIZES[kind]):
            tx, ty, _ = peer(o)
            pl.semaphore_signal(barrier, inc=1, device_id=(tx, ty), device_id_type=MESH)
        total += SIZES[kind] - 1
    pl.semaphore_wait(barrier, total)


def remote(src, dst, send, recv, to):
    copy = pltpu.make_async_remote_copy(
        src_ref=src,
        dst_ref=dst,
        send_sem=send,
        recv_sem=recv,
        device_id=to,
        device_id_type=MESH,
    )
    copy.start()
    return copy


def swap_halves(v):
    return pltpu.roll(v, 64, 1)


def trig(shape, position):
    lane = lax.broadcasted_iota(jnp.int32, shape, 1)
    step = (lane % 64).astype(F32)
    angle = position * jnp.exp(step * (-2.0 / HD * math.log(ROPE_BASE)))
    sine = jnp.sin(angle)
    return jnp.cos(angle), jnp.where(lane < 64, -sine, sine)


def lead_kernel(
    offset,
    text,
    tgrad,
    lat,
    gain,
    w_down,
    w_up,
    w_query,
    w_key,
    w_value,
    w_out,
    mix,
    nt,
    wd,
    wu,
    kvt,
    qdt,
    lat_all,
    phase,
    bias_it,
    bias_itt,
    bias_tt,
    vis_q,
    vis_row,
    dn,
    up,
    wq,
    wk,
    wv,
    wo,
    text_in,
    tgrad_in,
    lat_in,
    offs,
    own_off,
    rows_text,
    rows_grad,
    rows_lat,
    pad_lat,
    kv_out,
    qd_out,
    local,
    send_sx,
    recv_sx,
    send_off,
    recv_off,
    send_kv,
    recv_kv,
    send_qd,
    recv_qd,
    send_lat,
    recv_lat,
):
    sx = lax.axis_index("sx")
    sy = lax.axis_index("sy")
    g, head = split_sy(sy)
    loads = []
    for at, (src, dst) in enumerate(
        [(w_down, dn), (w_up, up), (w_query, wq), (w_key, wk), (w_value, wv), (w_out, wo)]
    ):
        copy = pltpu.make_async_copy(src, dst, local.at[at])
        copy.start()
        loads.append(copy)
    greet(["sx", "sy"])
    _, beside = ring("sx")
    _, along = ring("sy")
    _, mate = ring("group")
    first = []
    for o in range(1, 8):
        tx, ty, _ = beside(o)
        for n, (src, dst) in enumerate([(lat, lat_in), (text, text_in), (tgrad, tgrad_in)]):
            first.append(
                remote(src, dst.at[sx], send_sx.at[o, n], recv_sx.at[o, n], (tx, ty))
            )
    own_off[...] = jnp.full((8, HD), offset[0].astype(F32))
    offs[sy] = own_off[...]
    second = []
    for o in range(1, 16):
        tx, ty, _ = along(o)
        second.append(remote(own_off, offs.at[sy], send_off.at[o], recv_off.at[o], (tx, ty)))
    lat_in[sx] = lat[...]
    text_in[sx] = text[...]
    tgrad_in[sx] = tgrad[...]

    gain_row = gain[...]
    loads[0].wait()
    loads[1].wait()
    down = dn[...]
    both = dot(down, down, NT)
    high = both.astype(BF16)
    wd[:, :HD] = high
    wd[:, HD:] = (both - high.astype(F32)).astype(BF16)
    wu[...] = dot(down, up[...]).astype(BF16)
    scaled = (down.astype(F32) * gain_row).astype(BF16)
    mine = pl.ds(pl.multiple_of(head * HD, HD), HD)
    for n, weight in enumerate([wq, wk, wv]):
        loads[2 + n].wait()
        mix[:, n * HD : (n + 1) * HD] = dot(scaled, weight[:, mine]).astype(BF16)
    loads[5].wait()
    nt[...] = lax.dot_general(
        up[...], wo[mine, :], (((0,), (1,)), ((), ())), preferred_element_type=F32
    ).astype(BF16)

    for o in range(7):
        first[3 * o].wait_recv()
    pad_lat[...] = jnp.zeros_like(pad_lat)
    for n in range(8):
        rows_lat[2 * n : 2 * n + 2, :] = lat_in[n].astype(F32)
    pad_lat[:, CH : CH + PW * CH] = rows_lat[...].astype(BF16)
    lat_all[sy] = pad_lat[...]
    third = []
    for o in range(1, 16):
        tx, ty, _ = along(o)
        third.append(remote(pad_lat, lat_all.at[sy], send_lat.at[o], recv_lat.at[o], (tx, ty)))

    for o in range(7):
        first[3 * o + 1].wait_recv()
        first[3 * o + 2].wait_recv()
    for n in range(8):
        rows_text[4 * n : 4 * n + 4, :] = text_in[n].astype(F32)
        rows_grad[4 * n : 4 * n + 4, :] = tgrad_in[n].astype(F32)
    wide = rows_text[...]
    inverse = lax.rsqrt(jnp.mean(wide * wide, axis=1, keepdims=True) + EPS)
    normed = (wide * inverse * gain_row).astype(BF16)
    token = lax.broadcasted_iota(jnp.int32, (TXT, HD), 0).astype(F32)
    shift = jnp.where(token >= own_off[:1, :], float(IMG), 0.0)
    cosine, sine = trig((TXT, HD), token + shift + (sy * SB).astype(F32))
    query = dot(normed, wq[...])
    key = dot(normed, wk[...])
    value = dot(normed, wv[...])
    outer = dot(rows_grad[...].astype(BF16), wo[...], NT)
    for h in range(4):
        at = slice(h * HD, (h + 1) * HD)
        kv_out[h, :, :HD] = (key[:, at] * cosine + swap_halves(key[:, at]) * sine).astype(BF16)
        kv_out[h, :, HD:] = value[:, at].astype(BF16)
        turned = query[:, at] * cosine + swap_halves(query[:, at]) * sine
        qd_out[h, :, :HD] = (turned * (SCALE * LOG2E)).astype(BF16)
        qd_out[h, :, HD:] = outer[:, at].astype(BF16)
    for o in range(1, 16):
        tx, ty, _ = along(o)
        to = split_sy(ty)[1]
        third.append(remote(kv_out.at[to], kvt.at[sy], send_kv.at[o], recv_kv.at[o], (tx, ty)))
    for o in range(1, 4):
        tx, ty, to = mate(o)
        third.append(remote(qd_out.at[to], qdt.at[head], send_qd.at[o], recv_qd.at[o], (tx, ty)))
    kvt[sy] = kv_out[head]
    qdt[head] = qd_out[head]

    for copy in second:
        copy.wait()
    block = lax.broadcasted_iota(jnp.int32, (16, HD), 0).astype(F32)
    cosine, sine = trig((16, HD), block * float(SB) + jnp.max(offs[...], axis=1))
    phase[0] = cosine
    phase[1] = sine
    members = [sy_of(g, m) for m in range(4)]
    starts = [offs[b][:1, :] for b in members]
    lane = lax.broadcasted_iota(jnp.int32, (TXT, 512), 1)
    key_block = lane // TXT
    key_token = lane % TXT
    query_token = lax.broadcasted_iota(jnp.int32, (TXT, 512), 0)
    bias_it[...] = jnp.zeros_like(bias_it)
    for m in range(4):
        b = members[m]
        start = jnp.concatenate([starts[m]] * 4, axis=1)
        seen = (key_block[:1] < b) | (
            (key_block[:1] == b) & (key_token[:1].astype(F32) < start)
        )
        bias_it[m : m + 1, :] = jnp.where(seen, 0.0, NEG)
        seen = (key_block < b) | ((key_block == b) & (key_token <= query_token))
        bias_tt[m * TXT : (m + 1) * TXT, :] = jnp.where(seen, 0.0, NEG)
        late = jnp.where(token >= starts[m], 1.0, 0.0)
        vis_q[m * TXT : (m + 1) * TXT, :] = late + b.astype(F32)
    lane = lax.broadcasted_iota(jnp.int32, (8, HD), 1)
    start = starts[0]
    owner = jnp.full((8, HD), members[0], jnp.int32)
    for m in range(1, 4):
        start = jnp.where(lane // TXT == m, starts[m], start)
        owner = jnp.where(lane // TXT == m, members[m], owner)
    late = jnp.where((lane % TXT).astype(F32) >= start, 1.0, 0.0)
    vis_row[...] = late + owner.astype(F32)
    lane = lax.broadcasted_iota(jnp.int32, (512, HD), 1)
    row = lax.broadcasted_iota(jnp.int32, (512, HD), 0)
    start = jnp.broadcast_to(starts[0], (512, HD))
    owner = jnp.full((512, HD), members[0], jnp.int32)
    for m in range(1, 4):
        start = jnp.where(lane == m, starts[m], start)
        owner = jnp.where(lane == m, members[m], owner)
    seen = (row // TXT < owner) | (
        (row // TXT == owner) & ((row % TXT).astype(F32) < start)
    )
    bias_itt[...] = jnp.where(seen, 0.0, NEG)

    for copy in first:
        copy.wait_send()
    for copy in third:
        copy.wait()


def lead(offset, text, tgrad, lat, gain, w_down, w_up, w_query, w_key, w_value, w_out, cid):
    sds = jax.ShapeDtypeStruct
    hbm = pl.BlockSpec(memory_space=pl.ANY)
    dma = pltpu.SemaphoreType.DMA
    return pl.pallas_call(
        lead_kernel,
        out_shape=[
            sds((HD, 384), BF16),
            sds((HD, HD), BF16),
            sds((HD, 256), BF16),
            sds((HD, HD), BF16),
            sds((16, TXT, 256), BF16),
            sds((4, TXT, 256), BF16),
            sds((16, PH, 640), BF16),
            sds((2, 16, HD), F32),
            sds((8, 512), F32),
            sds((512, HD), F32),
            sds((128, 512), F32),
            sds((128, HD), F32),
            sds((8, HD), F32),
        ],
        in_specs=[pl.BlockSpec(memory_space=pltpu.SMEM)] + vmem(4) + [hbm] * 6,
        out_specs=vmem(13),
        scratch_shapes=[
            pltpu.VMEM((HD, D), BF16),
            pltpu.VMEM((D, HD), BF16),
            pltpu.VMEM((D, 512), BF16),
            pltpu.VMEM((D, 512), BF16),
            pltpu.VMEM((D, 512), BF16),
            pltpu.VMEM((512, D), BF16),
            pltpu.VMEM((8, 4, D), BF16),
            pltpu.VMEM((8, 4, D), BF16),
            pltpu.VMEM((8, 2, PW * CH), BF16),
            pltpu.VMEM((16, 8, HD), F32),
            pltpu.VMEM((8, HD), F32),
            pltpu.VMEM((TXT, D), F32),
            pltpu.VMEM((TXT, D), F32),
            pltpu.VMEM((PH, PW * CH), F32),
            pltpu.VMEM((PH, 640), BF16),
            pltpu.VMEM((4, TXT, 256), BF16),
            pltpu.VMEM((4, TXT, 256), BF16),
            dma((6,)),
            dma((8, 3)),
            dma((8, 3)),
            dma((16,)),
            dma((16,)),
            dma((16,)),
            dma((16,)),
            dma((4,)),
            dma((4,)),
            dma((16,)),
            dma((16,)),
        ],
        compiler_params=pltpu.CompilerParams(
            collective_id=cid, has_side_effects=True, vmem_limit_bytes=50 * 2**20
        ),
    )(offset, text, tgrad, lat, gain, w_down, w_up, w_query, w_key, w_value, w_out)


def place(x, y, z, core):
    return 2 * x + z % 2, 4 * y + 2 * (z // 2) + core


def tail_kernel(
    small,
    conv,
    atx,
    text,
    gain,
    w_down,
    w_up,
    w_query,
    w_key,
    w_value,
    w_out,
    every,
    text_out,
    wq,
    wk,
    wv,
    wo,
    small_in,
    conv_in,
    mixed,
    mixed_in,
    parts,
    parts_in,
    own,
    local,
    send_a,
    recv_a,
    send_c,
    recv_c,
    send_t,
    recv_t,
    send_p,
    recv_p,
    send_1,
    recv_1,
    send_2,
    recv_2,
    send_3,
    recv_3,
    send_4,
    recv_4,
    send_m,
    recv_m,
):
    sx = lax.axis_index("sx")
    sy = lax.axis_index("sy")
    g, head = split_sy(sy)
    mine = pl.ds(pl.multiple_of(head * HD, HD), HD)
    loads = []
    for at, (src, dst) in enumerate(
        [
            (w_query.at[:, mine], wq),
            (w_key.at[:, mine], wk),
            (w_value.at[:, mine], wv),
            (w_out, wo),
        ]
    ):
        copy = pltpu.make_async_copy(src, dst, local.at[at])
        copy.start()
        loads.append(copy)
    core = sy % 2
    x = sx // 2
    y = sy // 4
    z = 2 * ((sy // 2) % 2) + sx % 2
    even = core == 0
    p1 = jnp.where(even, x, z)
    p2 = jnp.where(even, y, x)
    p3 = jnp.where(even, z, y)

    def chip(a, b, c):
        a = a % 4
        b = b % 4
        c = c % 4
        return place(
            jnp.where(even, a, b), jnp.where(even, b, c), jnp.where(even, c, a), core
        )

    twin = place(x, y, z, 1 - core)
    right = chip(p1, p2, p3 + 1)
    left = chip(p1, p2, p3 + 3)
    barrier = pltpu.get_barrier_semaphore()
    peers = [chip(p1 + o, p2, p3) for o in range(1, 4)]
    peers += [chip(p1, p2 + o, p3) for o in range(1, 4)]
    peers += [right, left, twin]
    for kind in ("head", "sx", "team"):
        _, peer = ring(kind)
        peers += [peer(o)[:2] for o in range(1, SIZES[kind])]
    for to in peers:
        pl.semaphore_signal(barrier, inc=1, device_id=to, device_id_type=MESH)
    pl.semaphore_wait(barrier, len(peers))

    _, peer = ring("head")
    copies = []
    for o in range(1, 4):
        tx, ty, to = peer(o)
        copies.append(
            remote(small.at[to], small_in.at[g], send_a.at[o], recv_a.at[o], (tx, ty))
        )
        copies.append(
            remote(conv.at[to], conv_in.at[g], send_c.at[o], recv_c.at[o], (tx, ty))
        )
    small_in[g] = small[g]
    conv_in[g] = conv[g]
    for load in loads:
        load.wait()
    for copy in copies:
        copy.wait()
    low = jnp.sum(small_in[...].astype(F32), axis=0).astype(BF16)
    rest = jnp.sum(conv_in[...].astype(F32), axis=0).astype(BF16)
    for e in range(32):
        parts[e, 64:, :] = (
            rest[16 * e : 16 * e + 16, :] if e < 5 else jnp.zeros((16, HD), BF16)
        )

    @pl.loop(0, 8)
    def _(c):
        at = pl.ds(pl.multiple_of(c * 512, 512), 512)
        down = dot(low[:, :HD], wq[at, :], NT)
        down = down + dot(low[:, HD : 2 * HD], wk[at, :], NT)
        down = down + dot(low[:, 2 * HD : 3 * HD], wv[at, :], NT)
        down = down * gain[:, at]
        down = down + dot(low[:, 512:640], w_up[at, :], NT)
        down = down - dot(low[:, 768:], w_down[:, at])
        grad = dot(low[:, 384:512], wo[mine, at]) + dot(low[:, 640:768], w_down[:, at])
        for k in range(4):
            parts[4 * c + k, :32, :] = down[:, k * HD : (k + 1) * HD].astype(BF16)
            parts[4 * c + k, 32:64, :] = grad[:, k * HD : (k + 1) * HD].astype(BF16)

    e, peer = ring("team")
    copies = []
    for o in range(1, 32):
        tx, ty, to = peer(o)
        copies.append(
            remote(parts.at[to], parts_in.at[e], send_p.at[o], recv_p.at[o], (tx, ty))
        )
    parts_in[e] = parts[e]

    joined = jnp.concatenate([atx[h] for h in range(4)], axis=1)

    @pl.loop(0, 8)
    def _(c):
        at = pl.ds(pl.multiple_of(c * 512, 512), 512)
        out = dot(joined, wo[:, at])
        for n in range(8):
            mixed[n, :, at] = out[4 * n : 4 * n + 4, :].astype(BF16)

    _, peer = ring("sx")
    texts = []
    for o in range(1, 8):
        tx, ty, to = peer(o)
        texts.append(
            remote(mixed.at[to], mixed_in.at[sx], send_t.at[o], recv_t.at[o], (tx, ty))
        )
    mixed_in[sx] = mixed[sx]
    for copy in copies:
        copy.wait_recv()
    own[...] = jnp.sum(parts_in[...].astype(F32), axis=0).astype(BF16)

    here = every.at[core]
    there = every.at[core]
    spot = (p3 * 4 + p2) * 4 + p1
    every[core, spot] = own[...]
    ones = [
        remote(own, here.at[spot], send_1.at[o], recv_1.at[o], chip(p1 + o, p2, p3))
        for o in (1, 2, 3)
    ]
    for copy in texts:
        copy.wait()
    total = text[...].astype(F32)
    for n in range(8):
        total = total + mixed_in[n].astype(F32)
    text_out[...] = total.astype(BF16)
    for copy in ones:
        copy.wait_recv()
    line = here.at[pl.ds((p3 * 4 + p2) * 4, 4)]
    twos = [
        remote(line, line, send_2.at[o], recv_2.at[o], chip(p1, p2 + o, p3)) for o in (1, 2, 3)
    ]
    for copy in twos:
        copy.wait_recv()

    def slab(p):
        return here.at[pl.ds((p % 4) * 16, 16)]

    def half(p, h):
        return here.at[pl.ds((p % 4) * 16 + 8 * h, 8)]

    up = remote(slab(p3), slab(p3), send_3.at[0], recv_3.at[0], right)
    dn = remote(slab(p3), slab(p3), send_3.at[1], recv_3.at[1], left)
    twins = [remote(slab(p3), slab(p3), send_m.at[0], recv_m.at[0], twin)]
    up.wait_recv()
    far_up = remote(half(p3 + 3, 0), half(p3 + 3, 0), send_4.at[0], recv_4.at[0], right)
    twins.append(remote(slab(p3 + 3), slab(p3 + 3), send_m.at[1], recv_m.at[1], twin))
    dn.wait_recv()
    far_dn = remote(half(p3 + 1, 1), half(p3 + 1, 1), send_4.at[1], recv_4.at[1], left)
    twins.append(remote(slab(p3 + 1), slab(p3 + 1), send_m.at[2], recv_m.at[2], twin))
    far_up.wait_recv()
    far_dn.wait_recv()
    twins.append(remote(slab(p3 + 2), slab(p3 + 2), send_m.at[3], recv_m.at[3], twin))
    for copy in copies + ones + twos + [up, dn, far_up, far_dn]:
        copy.wait_send()
    for copy in twins:
        copy.wait()


def tail(small, conv, atx, text, gain, w_down, w_up, w_query, w_key, w_value, w_out, cid):
    sds = jax.ShapeDtypeStruct
    hbm = pl.BlockSpec(memory_space=pl.ANY)
    dma = pltpu.SemaphoreType.DMA
    return pl.pallas_call(
        tail_kernel,
        out_shape=[sds((2, 64, 80, HD), BF16), sds((4, D), BF16)],
        in_specs=vmem(7) + [hbm] * 4,
        out_specs=vmem(2),
        scratch_shapes=[
            pltpu.VMEM((D, HD), BF16),
            pltpu.VMEM((D, HD), BF16),
            pltpu.VMEM((D, HD), BF16),
            pltpu.VMEM((512, D), BF16),
            pltpu.VMEM((4, 32, 896), BF16),
            pltpu.VMEM((4, 80, HD), BF16),
            pltpu.VMEM((8, 4, D), BF16),
            pltpu.VMEM((8, 4, D), BF16),
            pltpu.VMEM((32, 80, HD), BF16),
            pltpu.VMEM((32, 80, HD), BF16),
            pltpu.VMEM((80, HD), BF16),
            dma((4,)),
        ]
        + [dma((4,))] * 4
        + [dma((8,))] * 2
        + [dma((32,))] * 2
        + [dma((4,))] * 10,
        compiler_params=pltpu.CompilerParams(
            collective_id=cid, has_side_effects=True, vmem_limit_bytes=50 * 2**20
        ),
    )(small, conv, atx, text, gain, w_down, w_up, w_query, w_key, w_value, w_out)


def assemble_kernel(every, down, up, conv, gup):
    def block(group, e):
        sx = e % 8
        i = e // 8
        sy = 2 * group + i if i < 2 else 12 - 2 * group + i
        x = sx // 2
        y = sy // 4
        z = 2 * ((sy // 2) % 2) + sx % 2
        core = sy % 2
        return core, (z * 4 + y) * 4 + x if core == 0 else (y * 4 + x) * 4 + z

    for e in range(32):
        cols = []
        for group in range(4):
            core, spot = block(group, e)
            down[32 * group : 32 * group + 32, e * HD : (e + 1) * HD] = every[
                core, spot, :32, :
            ].astype(F32)
            cols.append(every[core, spot, 32:64, :].astype(F32))
            if e < 5:
                at = 80 * group + 16 * e
                piece = every[core, spot, 64:80, :].astype(F32)
                if at < 288:
                    conv[at : at + 16, :] = piece
                else:
                    gup[at - 288 : at - 272, :] = piece
        up[e * HD : (e + 1) * HD, :] = jnp.concatenate(cols, axis=0).T


def assemble(every):
    sds = jax.ShapeDtypeStruct
    return pl.pallas_call(
        assemble_kernel,
        out_shape=[
            sds((HD, D), F32),
            sds((D, HD), F32),
            sds((288, HD), F32),
            sds((CH, HD), F32),
        ],
        in_specs=vmem(1),
        out_specs=vmem(4),
        compiler_params=pltpu.CompilerParams(vmem_limit_bytes=50 * 2**20),
    )(every)


def sigmoid(v):
    return 1.0 / (1.0 + jnp.exp(-v))


def turn(v, cosine, sine):
    return v * cosine + pltpu.roll(v, 64, 1) * sine


def tables(j, phase_ref, base_ref):
    pc = phase_ref[0, pl.ds(j, 1), :]
    ps = phase_ref[1, pl.ds(j, 1), :]
    bc = base_ref[0]
    bs = base_ref[1]
    return pc * bc - ps * bs, ps * bc + pc * bs


def row_scale(da, wd):
    both = dot(da, wd)
    dawd = both[:, :HD] + both[:, HD:]
    mean = jnp.sum(dawd * da.astype(F32), axis=1, keepdims=True) * (1.0 / D)
    return dawd, lax.rsqrt(mean + EPS)


def forward_kernel(
    info,
    lat,
    wconv,
    wd,
    mix,
    wu,
    nt,
    phase,
    base,
    kvt,
    qdt,
    bias_it,
    vis_q,
    bias_tt,
    patches,
    da_ref,
    sp_ref,
    k_ref,
    v_ref,
    q_ref,
    att_ref,
    lse_ref,
    part_ref,
    wide,
    wpad,
    reorder,
):
    g = info[0]
    wpad[...] = jnp.zeros_like(wpad)
    for tap in range(3):
        wpad[tap * 128 : tap * 128 + 96, :] = wconv[tap * 96 : tap * 96 + 96, :].astype(F32)
    mid = lat[...].astype(F32)
    row = lax.broadcasted_iota(jnp.int32, mid.shape, 0) % PH
    wide[0] = jnp.where(row == 0, 0.0, pltpu.roll(mid, 1, 0))
    wide[1] = mid
    wide[2] = jnp.where(row == PH - 1, 0.0, pltpu.roll(mid, 16 * PH - 1, 0))
    weight = wpad[...].astype(BF16)
    for c in range(PW):
        for tap in range(3):
            patches[c, :, tap * 128 : tap * 128 + 128] = wide[
                tap, :, c * CH : c * CH + 128
            ].astype(BF16)
        pre = dot(patches[c], weight)
        sig = sigmoid(pre)
        da_ref[:, c * PH : c * PH + PH, :] = (pre * sig).astype(BF16).reshape(16, PH, HD)
        sp_ref[:, c * PH : c * PH + PH, :] = (
            (sig * (1.0 + pre * (1.0 - sig))).astype(BF16).reshape(16, PH, HD)
        )
    mix_kv = mix[:, HD:]
    mix_q = mix[:, :HD]
    wd_val = wd[...]

    @pl.loop(0, 16)
    def _(j):
        da = da_ref[j]
        _, inv = row_scale(da, wd_val)
        kv = dot(da, mix_kv) * inv
        cosine, sine = tables(j, phase, base)
        rows = pl.ds(pl.multiple_of(j * IMG, IMG), IMG)
        k_ref[rows, :] = turn(kv[:, :HD], cosine, sine).astype(BF16)
        v_ref[rows, :] = kv[:, HD:].astype(BF16)

    for m in range(4):
        j = info[1 + m]
        da = da_ref[j]
        _, inv = row_scale(da, wd_val)
        cosine, sine = tables(j, phase, base)
        q_ref[m * IMG : (m + 1) * IMG, :] = (
            turn(dot(da, mix_q) * inv, cosine, sine) * (SCALE * LOG2E)
        ).astype(BF16)
    q_ref[1024:, :] = qdt[:, :HD]
    k_txt = kvt[:, :HD]
    v_txt = kvt[:, HD:]

    def finish(rows, peak, total, acc):
        att_ref[rows, :] = (acc / total).astype(BF16)
        lse_ref[rows, :] = jnp.broadcast_to(peak + jnp.log2(total), acc.shape)

    def step(q, scores_of):
        def body(j, state):
            peak, total, acc = state
            at = pl.ds(pl.multiple_of(j * 512, 512), 512)
            scores = scores_of(dot(q, k_ref[at, :], NT), j)
            new = jnp.maximum(peak, jnp.max(scores, axis=1, keepdims=True))
            raised = jnp.exp2(scores - new)
            old = jnp.exp2(peak - new)
            total = total * old + jnp.sum(raised, axis=1, keepdims=True)
            acc = acc * old + dot(raised.astype(BF16), v_ref[at, :])
            return new, total, acc

        return body

    def first(scores):
        peak = jnp.max(scores, axis=1, keepdims=True)
        raised = jnp.exp2(scores - peak)
        return (
            peak,
            jnp.sum(raised, axis=1, keepdims=True),
            dot(raised.astype(BF16), v_txt),
        )

    for p in range(2):
        diagonal = g if p == 0 else 7 - g
        q = q_ref[p * 512 : p * 512 + 512, :]
        bias = jnp.concatenate(
            [
                jnp.broadcast_to(bias_it[2 * p : 2 * p + 1, :], (IMG, 512)),
                jnp.broadcast_to(bias_it[2 * p + 1 : 2 * p + 2, :], (IMG, 512)),
            ],
            axis=0,
        )
        scores = jnp.where(bias < 0.0, NEG, dot(q, k_txt, NT))
        state = first(scores)

        def masked(scores, j):
            top = lax.broadcasted_iota(jnp.int32, scores.shape, 0) < IMG
            right = lax.broadcasted_iota(jnp.int32, scores.shape, 1) >= IMG
            return jnp.where(top & right, NEG, scores)

        state = step(q, masked)(diagonal, state)
        state = lax.fori_loop(0, diagonal, step(q, lambda s, j: s), state)
        finish(pl.ds(p * 512, 512), *state)

    q = q_ref[1024:, :]
    vis = vis_q[:, :1]

    def before(scores, j):
        block = 2 * j + (lax.broadcasted_iota(jnp.int32, scores.shape, 1) >= IMG).astype(jnp.int32)
        return jnp.where(block.astype(F32) < vis, scores, NEG)

    state = first(jnp.where(bias_tt[...] < 0.0, NEG, dot(q, k_txt, NT)))
    state = lax.fori_loop(0, 8 - g, step(q, before), state)
    finish(pl.ds(1024, 128), *state)

    for m in range(4):
        rows = slice(m * IMG, (m + 1) * IMG)
        reorder[...] = dot(att_ref[rows, :], nt[...], NT) + dot(
            da_ref[info[1 + m]], wu[...]
        ) * (1.0 / 32.0)
        for r in range(PH):
            part_ref[m * IMG + r * PW : m * IMG + r * PW + PW, :] = reorder[
                pl.ds(r, PW, stride=PH), :
            ].astype(BF16)


def forward(info, *args):
    sds = jax.ShapeDtypeStruct
    return pl.pallas_call(
        forward_kernel,
        out_shape=[
            sds((16, 256, 384), BF16),
            sds((16, 256, HD), BF16),
            sds((16, 256, HD), BF16),
            sds((4096, HD), BF16),
            sds((4096, HD), BF16),
            sds((1152, HD), BF16),
            sds((1152, HD), BF16),
            sds((1152, HD), F32),
            sds((1024, HD), BF16),
        ],
        in_specs=[pl.BlockSpec(memory_space=pltpu.SMEM)] + vmem(len(args)),
        out_specs=vmem(9),
        scratch_shapes=[
            pltpu.VMEM((3, 256, 640), F32),
            pltpu.VMEM((384, HD), F32),
            pltpu.VMEM((IMG, HD), F32),
        ],
        compiler_params=pltpu.CompilerParams(vmem_limit_bytes=50 * 2**20),
        cost_estimate=pl.CostEstimate(flops=8 * 10**9, bytes_accessed=2**24, transcendentals=2**22),
    )(info, *args)


def middle_kernel(
    part, pgrad, w_uo, att_txt, gall, pred, gup, atx, recv, send_a, recv_a, send_b, recv_b, send_c, recv_c
):
    e, peer = ring("team")
    i, mate = ring("group")
    greet(["team"])
    copies = []
    for o in range(1, 32):
        tx, ty, to = peer(o)
        copy = pltpu.make_async_remote_copy(
            src_ref=part.at[to],
            dst_ref=recv.at[e],
            send_sem=send_a.at[o],
            recv_sem=recv_a.at[o],
            device_id=(tx, ty),
            device_id_type=MESH,
        )
        copy.start()
        copies.append(copy)
    others = []
    for o in range(1, 4):
        tx, ty, to = mate(o)
        copy = pltpu.make_async_remote_copy(
            src_ref=att_txt.at[to],
            dst_ref=atx.at[i],
            send_sem=send_c.at[o],
            recv_sem=recv_c.at[o],
            device_id=(tx, ty),
            device_id_type=MESH,
        )
        copy.start()
        others.append(copy)
    recv[e] = part[e]
    atx[i] = att_txt[i]
    for copy in copies:
        copy.wait()
    pre = jnp.sum(recv[...].astype(F32), axis=0)
    sig = sigmoid(pre)
    act = (pre * sig).astype(BF16)
    grad = (dot(pgrad[...], w_uo[...], NT) * (sig * (1.0 + pre * (1.0 - sig)))).astype(BF16)
    gall[e] = grad
    copies = []
    for o in range(1, 32):
        tx, ty, _ = peer(o)
        copy = pltpu.make_async_remote_copy(
            src_ref=gall.at[e],
            dst_ref=gall.at[e],
            send_sem=send_b.at[o],
            recv_sem=recv_b.at[o],
            device_id=(tx, ty),
            device_id_type=MESH,
        )
        copy.start()
        copies.append(copy)
    pred[...] = dot(act, w_uo[...]).astype(BF16)
    gup[...] = dot(pgrad[...], act, TN)
    for copy in copies + others:
        copy.wait()


def middle(part, pgrad, w_uo, att_txt, cid):
    sds = jax.ShapeDtypeStruct
    return pl.pallas_call(
        middle_kernel,
        out_shape=[
            sds((32, 32, HD), BF16),
            sds((32, CH), BF16),
            sds((CH, HD), F32),
            sds((4, TXT, HD), BF16),
        ],
        in_specs=vmem(4),
        out_specs=vmem(4),
        scratch_shapes=[pltpu.VMEM((32, 32, HD), BF16)]
        + [pltpu.SemaphoreType.DMA((32,))] * 4
        + [pltpu.SemaphoreType.DMA((4,))] * 2,
        compiler_params=pltpu.CompilerParams(collective_id=cid, has_side_effects=True),
    )(part, pgrad, w_uo, att_txt)


def backward_kernel(
    info,
    patches,
    da_ref,
    sp_ref,
    k_ref,
    v_ref,
    q_ref,
    att_ref,
    lse_ref,
    gall,
    wd,
    mix,
    wu,
    nt,
    phase,
    base,
    kvt,
    qdt,
    bias_itt,
    vis_row,
    gup,
    small_out,
    conv,
    small,
    order,
    gpu_ref,
    do_ref,
    dq_ref,
    dk_ref,
    dv_ref,
    ex_ref,
    dpre_ref,
    rows_ref,
):
    g = info[0]
    for m in range(4):
        nat = gall[m * IMG : (m + 1) * IMG, :].astype(F32)
        for r in range(PH):
            order[pl.ds(m * IMG + r, PW, stride=PH), :] = nat[r * PW : r * PW + PW, :]
    gpu_ref[...] = order[...].astype(BF16)
    do_ref[:1024, :] = dot(gpu_ref[...], nt[...]).astype(BF16)
    do_ref[1024:, :] = qdt[:, HD:]
    dk_ref[...] = jnp.zeros_like(dk_ref)
    dv_ref[...] = jnp.zeros_like(dv_ref)
    dq_ref[...] = jnp.zeros_like(dq_ref)
    ex_ref[...] = jnp.zeros_like(ex_ref)

    k_txt = kvt[:, :HD]
    v_txt = kvt[:, HD:]

    def lanes(column):
        return column.T[:1, :]

    def tile(q, do, lse, delta, keys, values, mask):
        scores = dot(keys, q, NT)
        if mask is not None:
            scores = mask(scores)
        probs = jnp.exp2(scores - lse)
        grad = (probs * (dot(values, do, NT) - delta)).astype(BF16)
        return probs.astype(BF16), grad

    for p in range(3):
        width = 512 if p < 2 else 128
        rows = slice(p * 512, p * 512 + width)
        q = q_ref[rows, :]
        do = do_ref[rows, :]
        lse = lanes(lse_ref[rows, :])
        dot_rows = jnp.sum(do.astype(F32) * att_ref[rows, :].astype(F32), axis=1, keepdims=True)
        delta = lanes(jnp.broadcast_to(dot_rows, (width, HD)))

        def body(j, mask, with_query):
            at = pl.ds(pl.multiple_of(j * 512, 512), 512)
            keys = k_ref[at, :]
            probs, grad = tile(q, do, lse, delta, keys, v_ref[at, :], mask)
            dv_ref[at, :] += dot(probs, do)
            dk_ref[at, :] += dot(grad, q)
            if with_query:
                rows_ref[...] += dot(grad, keys, TN)

        if p < 2:
            diagonal = g if p == 0 else 7 - g

            def unseen(scores):
                bottom = lax.broadcasted_iota(jnp.int32, scores.shape, 0) >= IMG
                left = lax.broadcasted_iota(jnp.int32, scores.shape, 1) < IMG
                return jnp.where(bottom & left, NEG, scores)

            def text(scores):
                left = jnp.broadcast_to(bias_itt[:, 2 * p : 2 * p + 1], (512, IMG))
                right = jnp.broadcast_to(bias_itt[:, 2 * p + 1 : 2 * p + 2], (512, IMG))
                return jnp.where(jnp.concatenate([left, right], axis=1) < 0.0, NEG, scores)

            _, grad = tile(q, do, lse, delta, k_txt, v_txt, text)
            rows_ref[...] = dot(grad, k_txt, TN)
            body(diagonal, unseen, True)

            @pl.loop(0, diagonal)
            def _(j):
                body(j, None, True)

            for half in range(2):
                dq_ref[info[1 + 2 * p + half]] = rows_ref[half * IMG : (half + 1) * IMG, :]
        else:
            vis = vis_row[:1, :]

            @pl.loop(0, 8 - g)
            def _(j):
                def seen(scores):
                    block = 2 * j + (
                        lax.broadcasted_iota(jnp.int32, scores.shape, 0) >= IMG
                    ).astype(jnp.int32)
                    return jnp.where(block.astype(F32) < vis, scores, NEG)

                body(j, seen, False)

    small[...] = jnp.zeros_like(small)
    for m in range(4):
        j = info[1 + m]
        rows = slice(m * IMG, (m + 1) * IMG)
        gpu = gpu_ref[rows, :]
        da = da_ref[j]
        ex_ref[j] = dot(gpu, wu[...], NT) * (1.0 / 32.0)
        small[:, 384:512] += dot(gpu, att_ref[rows, :], TN)
        small[:, 512:640] += dot(da, gpu, TN) * (1.0 / 32.0)
        small[:, 640:768] += dot(gpu, da, TN) * (1.0 / 32.0)
    wd_val = wd[...]
    mix_val = mix[...]

    @pl.loop(0, 16)
    def _(j):
        da = da_ref[j]
        da_wide = da.astype(F32)
        dawd, inv = row_scale(da, wd_val)
        cosine, sine = tables(j, phase, base)
        at = pl.ds(pl.multiple_of(j * IMG, IMG), IMG)
        gq = turn(dq_ref[j] * SCALE, cosine, -sine)
        gk = turn(dk_ref[at, :] * (1.0 / LOG2E), cosine, -sine)
        grads = jnp.concatenate([gq, gk, dv_ref[at, :]], axis=1).astype(BF16)
        back = dot(grads, mix_val, NT)
        cube = (inv * inv * inv) * (jnp.sum(back * da_wide, axis=1, keepdims=True) * (1.0 / D))
        grad = (inv * back - cube * dawd + ex_ref[j]) * sp_ref[j].astype(F32)
        dpre_ref[j] = grad.astype(BF16)
        small[:, :384] += dot((da_wide * inv).astype(BF16), grads, TN)
        small[:, 768:] += dot((da_wide * cube).astype(BF16), da, TN)

    total = jnp.zeros((384, HD), F32)
    for c in range(PW):
        grad = dpre_ref[:, c * PH : c * PH + PH, :].reshape(256, HD)
        total = total + dot(patches[c], grad, TN)
    for tap in range(3):
        conv[tap * 96 : tap * 96 + 96, :] = total[tap * 128 : tap * 128 + 96, :].astype(BF16)
    conv[288:, :] = gup[...].astype(BF16)
    small_out[...] = small[...].astype(BF16)


def backward(info, *args):
    sds = jax.ShapeDtypeStruct
    return pl.pallas_call(
        backward_kernel,
        out_shape=[sds((HD, 896), BF16), sds((320, HD), BF16)],
        in_specs=[pl.BlockSpec(memory_space=pltpu.SMEM)] + vmem(len(args)),
        out_specs=vmem(2),
        scratch_shapes=[
            pltpu.VMEM((HD, 896), F32),
            pltpu.VMEM((1024, HD), F32),
            pltpu.VMEM((1024, HD), BF16),
            pltpu.VMEM((1152, HD), BF16),
            pltpu.VMEM((16, IMG, HD), F32),
            pltpu.VMEM((4096, HD), F32),
            pltpu.VMEM((4096, HD), F32),
            pltpu.VMEM((16, IMG, HD), F32),
            pltpu.VMEM((16, IMG, HD), BF16),
            pltpu.VMEM((512, HD), F32),
        ],
        compiler_params=pltpu.CompilerParams(vmem_limit_bytes=50 * 2**20),
        cost_estimate=pl.CostEstimate(
            flops=16 * 10**9, bytes_accessed=2**24, transcendentals=2**22
        ),
    )(info, *args)


def rope_base():
    half = HD // 2
    freq = np.exp(-(2.0 * np.arange(half) / HD) * math.log(ROPE_BASE))
    slot = np.arange(IMG)
    position = (slot % PH) * PW + slot // PH
    angle = position[:, None] * freq[None, :]
    cosine = np.concatenate([np.cos(angle), np.cos(angle)], axis=1)
    sine = np.concatenate([-np.sin(angle), np.sin(angle)], axis=1)
    return jnp.asarray(np.stack([cosine, sine]).astype(np.float32))


def shards(
    text_tokens,
    latent,
    image_offset,
    norm_gain,
    w_query,
    w_key,
    w_value,
    w_out,
    w_down_conv,
    w_down_proj,
    w_up_proj,
    w_up_out,
    pred_grad,
    text_grad,
):
    sx = lax.axis_index("sx")
    sy = lax.axis_index("sy")
    g, i = split_sy(sy)
    members = jnp.stack([sy_of(g, jnp.int32(m)) for m in range(4)])
    info = jnp.concatenate([jnp.stack([g, *members]), jnp.zeros((3,), jnp.int32)]).astype(jnp.int32)
    gain = norm_gain.astype(F32)[None]

    mix, nt, wd, wu, kvt, qdt, lat, phase, bias_it, bias_itt, bias_tt, vis_q, vis_row = lead(
        image_offset,
        text_tokens[0],
        text_grad[0],
        latent[0],
        gain,
        w_down_proj,
        w_up_proj,
        w_query,
        w_key,
        w_value,
        w_out,
        1,
    )
    kvt = kvt.reshape(512, 2 * HD)
    qdt = qdt.reshape(128, 2 * HD)
    base = rope_base()

    patches, da, sp, keys, values, queries, att, lse, part = forward(
        info,
        lat.reshape(256, 640),
        w_down_conv,
        wd,
        mix,
        wu,
        nt,
        phase,
        base,
        kvt,
        qdt,
        bias_it,
        vis_q,
        bias_tt,
    )

    gall, pred, gup, atx = middle(
        part.reshape(32, 32, HD),
        pred_grad[0].reshape(32, CH),
        w_up_out,
        att[1024:].reshape(4, TXT, HD),
        2,
    )

    small, conv = backward(
        info,
        patches,
        da,
        sp,
        keys,
        values,
        queries,
        att,
        lse,
        gall.reshape(1024, HD),
        wd,
        mix,
        wu,
        nt,
        phase,
        base,
        kvt,
        qdt,
        bias_itt,
        vis_row,
        gup,
    )

    every, text_out = tail(
        small.reshape(4, 32, 896),
        conv.reshape(4, 80, HD),
        atx,
        text_tokens[0],
        gain,
        w_down_proj,
        w_up_proj,
        w_query,
        w_key,
        w_value,
        w_out,
        3,
    )
    grad_down_proj, grad_up_proj, grad_conv, grad_up_out = assemble(every)
    return (
        pred.reshape(1, 2, PW * CH),
        text_out[None],
        grad_conv,
        grad_down_proj,
        grad_up_proj,
        grad_up_out.T,
    )


def solution(mesh):
    placed = (
        P("sy", "sx", None),
        P("sy", "sx", None),
        P("sy"),
        P(),
        P(None, "sx"),
        P(None, "sx"),
        P(None, "sx"),
        P("sx", None),
        P(),
        P(),
        P(),
        P(),
        P("sy", "sx", None),
        P("sy", "sx", None),
    )
    return jax.shard_map(
        shards,
        mesh=mesh,
        in_specs=placed,
        out_specs=(P("sy", "sx", None), P("sy", "sx", None), P(), P(), P(), P()),
        check_vma=False,
    )
```

```python
import functools
import math
import types

import jax
import jax.numpy as jnp
import numpy as np
from jax import lax
from jax.experimental import pallas as pl
from jax.experimental.pallas import tpu as pltpu
from jax.sharding import PartitionSpec as P

MESH = pl.DeviceIdType.MESH
F32 = jnp.float32
BF16 = jnp.bfloat16
HD = 128
SB = 288
TXT = 32
IMG = 256
PH = 16
PW = 16
CH = 32
D = 4096
EPS = 1e-05
NEG = -1e30
LOG2E = math.log2(math.e)
SCALE = HD ** (-0.5)
ROPE_BASE = 500000.0
SIZES = {"sx": 8, "sy": 16, "group": 4, "head": 4, "team": 32}
NT = (((1,), (1,)), ((), ()))
TN = (((0,), (0,)), ((), ()))


def dot(a, b, dims=(((1,), (0,)), ((), ()))):
    return lax.dot_general(a, b, dims, preferred_element_type=F32)


def vmem(count):
    return [pl.BlockSpec(memory_space=pltpu.VMEM)] * count


def mod(a, n):
    return a % n if isinstance(a, int) else lax.rem(a, n)


def div(a, n):
    return a // n if isinstance(a, int) else lax.div(a, n)


def sy_of(g, i):
    if isinstance(i, int):
        return 2 * g + i if i < 2 else 12 - 2 * g + i
    return jnp.where(i < 2, 2 * g + i, 12 - 2 * g + i)


def split_sy(sy):
    low = sy < 8
    g = jnp.where(low, div(sy, 2), div(15 - sy, 2))
    i = mod(sy, 2) + jnp.where(low, 0, 2)
    return g, i


def ring(kind):
    sx = lax.axis_index("sx")
    sy = lax.axis_index("sy")
    g, i = split_sy(sy)
    if kind == "sx":
        return sx, lambda o: (mod(sx + o, 8), sy, mod(sx + o, 8))
    if kind == "sy":
        return sy, lambda o: (sx, mod(sy + o, 16), mod(sy + o, 16))
    if kind == "group":
        return i, lambda o: (sx, sy_of(g, mod(i + o, 4)), mod(i + o, 4))
    if kind == "head":
        return g, lambda o: (sx, sy_of(mod(g + o, 4), i), mod(g + o, 4))
    e = i * 8 + sx

    def peer(o):
        f = mod(e + o, 32)
        return mod(f, 8), sy_of(g, div(f, 8)), f

    return e, peer


def remote(src, dst, send, recv, to):
    copy = pltpu.make_async_remote_copy(
        src_ref=src,
        dst_ref=dst,
        send_sem=send,
        recv_sem=recv,
        device_id=to,
        device_id_type=MESH,
    )
    copy.start()
    return copy


class Fan:
    def __init__(self, kind, source, land, sems, slot_of=None):
        own, peer = ring(kind)
        self.land = land.at[pl.ds(0, SIZES[kind] - 1)]
        self.sems = sems

        @pl.loop(1, SIZES[kind])
        def _(o):
            tx, ty, to = peer(o)
            src = source if slot_of is None else source.at[slot_of(ty, to)]
            remote(src, land.at[own], sems.at[0], sems.at[1], (tx, ty))

    def arrived(self):
        pltpu.make_async_copy(self.land, self.land, self.sems.at[1]).wait()

    def sent(self):
        pltpu.make_async_copy(self.land, self.land, self.sems.at[0]).wait()


def sigmoid(v):
    return 1.0 / (1.0 + jnp.exp(-v))


def turn(v, cosine, sine):
    return v * cosine + pltpu.roll(v, 64, 1) * sine


def trig(shape, position):
    lane = lax.broadcasted_iota(jnp.int32, shape, 1)
    step = (lane % 64).astype(F32)
    angle = position * jnp.exp(step * (-2.0 / HD * math.log(ROPE_BASE)))
    sine = jnp.sin(angle)
    return jnp.cos(angle), jnp.where(lane < 64, -sine, sine)


def tables(j, phase_ref, base_ref):
    pc = phase_ref[0, pl.ds(j, 1), :]
    ps = phase_ref[1, pl.ds(j, 1), :]
    bc = base_ref[0]
    bs = base_ref[1]
    return pc * bc - ps * bs, ps * bc + pc * bs


def row_scale(da, wd):
    both = dot(da, wd)
    dawd = both[:, :HD] + both[:, HD:]
    mean = jnp.sum(dawd * da.astype(F32), axis=1, keepdims=True) * (1.0 / D)
    return dawd, lax.rsqrt(mean + EPS)


def lanes(column):
    return column.T[:1, :]


def place(x, y, z, core):
    return 2 * x + mod(z, 2), 4 * y + 2 * div(z, 2) + core


class Spread:
    def __init__(self, every, sems):
        self.every = every
        self.sems = sems
        sx = lax.axis_index("sx")
        sy = lax.axis_index("sy")
        self.core = mod(sy, 2)
        x = div(sx, 2)
        y = div(sy, 4)
        z = 2 * mod(div(sy, 2), 2) + mod(sx, 2)
        self.even = self.core == 0
        self.p1 = jnp.where(self.even, x, z)
        self.p2 = jnp.where(self.even, y, x)
        self.p3 = jnp.where(self.even, z, y)
        self.twin = place(x, y, z, 1 - self.core)
        self.here = every.at[self.core]
        self.spot = (self.p3 * 4 + self.p2) * 4 + self.p1
        self.live = []

    def chip(self, a, b, c):
        a = mod(a, 4)
        b = mod(b, 4)
        c = mod(c, 4)
        even = self.even
        return place(
            jnp.where(even, a, b), jnp.where(even, b, c), jnp.where(even, c, a), self.core
        )

    def send(self, ref, n, to):
        copy = remote(ref, ref, self.sems.at[0, n], self.sems.at[1, n], to)
        self.live.append(copy)
        return copy

    def slab(self, p):
        return self.here.at[pl.ds(mod(p, 4) * 16, 16)]

    def plane(self, block):
        self.every[self.core, self.spot] = block
        mine = self.here.at[self.spot]

        @pl.loop(1, 16)
        def _(o):
            to = self.chip(self.p1 + mod(o, 4), self.p2 + div(o, 4), self.p3)
            remote(mine, mine, self.sems.at[0, 0], self.sems.at[1, 0], to)

    def slabs(self):
        plane = self.here.at[pl.ds(0, 15)]
        pltpu.make_async_copy(plane, plane, self.sems.at[1, 0]).wait()
        own = self.slab(self.p3)
        self.wave = [self.send(own, o, self.chip(self.p1, self.p2, self.p3 + o)) for o in (1, 3, 2)]
        self.twins = [self.send(own, 4, self.twin)]

    def pass_on(self):
        for o, copy in zip((1, 3, 2), self.wave):
            copy.wait_recv()
            self.twins.append(self.send(self.slab(self.p3 + 4 - o), 4 + o, self.twin))

    def arrived(self):
        for copy in self.twins:
            copy.wait_recv()

    def sent(self):
        plane = self.here.at[pl.ds(0, 15)]
        pltpu.make_async_copy(plane, plane, self.sems.at[0, 0]).wait()
        for copy in self.live:
            copy.wait_send()


def greet(wide):
    barrier = pltpu.get_barrier_semaphore()
    for kind in ("team", "sy"):
        _, peer = ring(kind)

        @pl.loop(1, SIZES[kind])
        def _(o):
            tx, ty, _ = peer(o)
            pl.semaphore_signal(barrier, inc=1, device_id=(tx, ty), device_id_type=MESH)

    @pl.loop(1, 16)
    def _(o):
        to = wide.chip(wide.p1 + mod(o, 4), wide.p2 + div(o, 4), wide.p3)
        pl.semaphore_signal(barrier, inc=1, device_id=to, device_id_type=MESH)

    @pl.loop(1, 4)
    def _(o):
        to = wide.chip(wide.p1, wide.p2, wide.p3 + o)
        pl.semaphore_signal(barrier, inc=1, device_id=to, device_id_type=MESH)

    pl.semaphore_wait(barrier, 31 + 15 + 15 + 3)


def masks(r, g, members):
    block = lax.broadcasted_iota(jnp.int32, (16, HD), 0).astype(F32)
    cosine, sine = trig((16, HD), block * float(SB) + jnp.max(r.offs[...], axis=1))
    r.phase[0] = cosine
    r.phase[1] = sine
    starts = [r.offs[b][:1, :] for b in members]
    row = lax.broadcasted_iota(jnp.int32, (512, TXT), 0)
    query = lax.broadcasted_iota(jnp.int32, (512, TXT), 1)
    for m in range(4):
        b = members[m]
        seen = (row // TXT < b) | ((row // TXT == b) & (row % TXT <= query))
        r.bias_tt[:, m * TXT : (m + 1) * TXT] = jnp.where(seen, 0.0, NEG)
    lane = lax.broadcasted_iota(jnp.int32, (8, HD), 1)
    start = starts[0]
    owner = jnp.full((8, HD), members[0], jnp.int32)
    for m in range(1, 4):
        start = jnp.where(lane // TXT == m, starts[m], start)
        owner = jnp.where(lane // TXT == m, members[m], owner)
    late = jnp.where((lane % TXT).astype(F32) >= start, 1.0, 0.0)
    r.vis[...] = late + owner.astype(F32)
    lane = lax.broadcasted_iota(jnp.int32, (512, HD), 1)
    row = lax.broadcasted_iota(jnp.int32, (512, HD), 0)
    start = jnp.broadcast_to(starts[0], (512, HD))
    owner = jnp.full((512, HD), members[0], jnp.int32)
    for m in range(1, 4):
        start = jnp.where(lane == m, starts[m], start)
        owner = jnp.where(lane == m, members[m], owner)
    seen = (row // TXT < owner) | ((row // TXT == owner) & ((row % TXT).astype(F32) < start))
    r.bias_ti[...] = jnp.where(seen, 0.0, NEG)


def down_block(r):
    r.wpad[...] = jnp.zeros_like(r.wpad)
    for tap in range(3):
        r.wpad[tap * 128 : tap * 128 + 96, :] = r.wconv[tap * 96 : tap * 96 + 96, :].astype(F32)
    mid = r.lat_all[...].reshape(256, 640).astype(F32)
    row = lax.broadcasted_iota(jnp.int32, mid.shape, 0) % PH
    r.wide[0] = jnp.where(row == 0, 0.0, pltpu.roll(mid, 1, 0))
    r.wide[1] = mid
    r.wide[2] = jnp.where(row == PH - 1, 0.0, pltpu.roll(mid, 16 * PH - 1, 0))
    weight = r.wpad[...].astype(BF16)
    for c in range(PW):
        for tap in range(3):
            r.patches[c, :, tap * 128 : tap * 128 + 128] = r.wide[
                tap, :, c * CH : c * CH + 128
            ].astype(BF16)
        pre = dot(r.patches[c], weight)
        sig = sigmoid(pre)
        r.da[:, c * PH : c * PH + PH, :] = (pre * sig).astype(BF16).reshape(16, PH, HD)
        r.sp[:, c * PH : c * PH + PH, :] = (
            (sig * (1.0 + pre * (1.0 - sig))).astype(BF16).reshape(16, PH, HD)
        )


def project(r, members):
    mix_kv = r.mix[:, HD:]
    mix_q = r.mix[:, :HD]
    wd = r.wd[...]

    @pl.loop(0, 16, unroll=4)
    def _(j):
        da = r.da[j]
        _, inv = row_scale(da, wd)
        kv = dot(da, mix_kv) * inv
        cosine, sine = tables(j, r.phase, r.base)
        rows = pl.ds(pl.multiple_of(j * IMG, IMG), IMG)
        r.k[rows, :] = turn(kv[:, :HD], cosine, sine).astype(BF16)
        r.v[rows, :] = kv[:, HD:].astype(BF16)
        r.vt[:, rows] = kv[:, HD:].T.astype(BF16)

    for m in range(4):
        da = r.da[members[m]]
        r.da_own[m * IMG : (m + 1) * IMG, :] = da
        _, inv = row_scale(da, wd)
        cosine, sine = tables(members[m], r.phase, r.base)
        r.q[m * IMG : (m + 1) * IMG, :] = (
            turn(dot(da, mix_q) * inv, cosine, sine) * (SCALE * LOG2E)
        ).astype(BF16)


def tile_rows(j):
    return pl.ds(pl.multiple_of(j * 512, 512), 512)


def absorb(state, scores, vt, e_ref, m_ref):
    top = jnp.max(scores, axis=0, keepdims=True)
    new = top if state is None else jnp.maximum(state[0], top)
    raised = jnp.exp2(scores - new)
    low = raised.astype(BF16)
    e_ref[...] = low
    m_ref[...] = jnp.broadcast_to(new, m_ref.shape)
    total = jnp.sum(raised, axis=0, keepdims=True)
    mixed = dot(vt, low)
    if state is None:
        return new, total, mixed
    old = jnp.exp2(state[0] - new)
    return new, state[1] * old + total, state[2] * old + mixed


def conclude(r, p, width, state):
    peak, total, acc = state
    r.att[p * 512 : p * 512 + width, :] = (acc / total).T.astype(BF16)
    r.lse[p, :, :width] = jnp.broadcast_to(peak + jnp.log2(total), (8, width))


def diagonal_mask(scores):
    bottom = lax.broadcasted_iota(jnp.int32, scores.shape, 0) >= IMG
    left = lax.broadcasted_iota(jnp.int32, scores.shape, 1) < IMG
    return jnp.where(bottom & left, NEG, scores)


def attend_images(r, p, diagonal, text_ready):
    q = r.q[p * 512 : p * 512 + 512, :]
    base = 4 * p

    def tile(j):
        return dot(r.k[tile_rows(j), :], q, NT)

    state = absorb(
        None,
        diagonal_mask(tile(diagonal)),
        r.vt[:, tile_rows(diagonal)],
        r.e_img.at[base + diagonal],
        r.m_img.at[base + diagonal],
    )

    def body(j, state):
        return absorb(
            state, tile(j), r.vt[:, tile_rows(j)], r.e_img.at[base + j], r.m_img.at[base + j]
        )

    state = lax.fori_loop(0, diagonal, body, state)
    text_ready()
    scores = dot(r.kt[...], q, NT)
    bias = jnp.concatenate(
        [
            jnp.broadcast_to(r.bias_ti[:, 2 * p + half : 2 * p + half + 1], (512, IMG))
            for half in range(2)
        ],
        axis=1,
    )
    scores = jnp.where(bias < 0.0, NEG, scores)
    state = absorb(state, scores, r.vtt[...], r.e_txt.at[p], r.m_txt.at[p])
    conclude(r, p, 512, state)


def attend_text(r, count, kept):
    q = r.q[1024:, :]
    vis = r.vis[:1, :]
    scores = jnp.where(r.bias_tt[...] < 0.0, NEG, dot(r.kt[...], q, NT))
    state = absorb(None, scores, r.vtt[...], r.e_q.at[8], r.m_q.at[8])

    def body(j, state):
        scores = dot(r.k[tile_rows(j), :], q, NT)
        block = 2 * j + (lax.broadcasted_iota(jnp.int32, scores.shape, 0) >= IMG).astype(jnp.int32)
        scores = jnp.where(block.astype(F32) < vis, scores, NEG)
        return absorb(state, scores, r.vt[:, tile_rows(j)], r.e_q.at[j], r.m_q.at[j])

    conclude(r, 2, 128, lax.fori_loop(0, count, body, state))


def normalise(e_ref, m_ref, lse):
    factor = jnp.exp2(m_ref[:1, :] - lse)
    e_ref[...] = (e_ref[...].astype(F32) * factor).astype(BF16)


def backward_rows(r, p, width):
    rows = slice(p * 512, p * 512 + width)
    q = r.q[rows, :]
    do = r.do[rows, :]
    sums = jnp.sum(do.astype(F32) * r.att[rows, :].astype(F32), axis=1, keepdims=True)
    return q, do, lanes(jnp.broadcast_to(sums, (width, HD)))


def backward_images(r, p, diagonal, members):
    q, do, delta = backward_rows(r, p, 512)
    base = 4 * p

    probs = r.e_txt[p].astype(F32)
    grad = (probs * (dot(r.vtx[...], do, NT) - delta)).astype(BF16)
    r.dqs[...] = dot(grad, r.kt[...], TN)

    @pl.loop(0, diagonal + 1)
    def _(j):
        at = tile_rows(j)
        keys = r.k[at, :]
        probs = r.e_img[base + j]
        grad = (probs.astype(F32) * (dot(r.v[at, :], do, NT) - delta)).astype(BF16)
        r.dv[at, :] += dot(probs, do)
        r.dk[at, :] += dot(grad, q)
        r.dqs[...] += dot(grad, keys, TN)

    for half in range(2):
        r.dq[2 * p + half] = r.dqs[half * IMG : (half + 1) * IMG, :]


def backward_text(r, count):
    q, do, delta = backward_rows(r, 2, 128)

    @pl.loop(0, count)
    def _(j):
        at = tile_rows(j)
        probs = r.e_q[j]
        grad = (probs.astype(F32) * (dot(r.v[at, :], do, NT) - delta)).astype(BF16)
        r.dv[at, :] += dot(probs, do)
        r.dk[at, :] += dot(grad, q)


def image_grads(r, g):
    wd = r.wd[...]
    mix = r.mix[...]
    r.small[...] = jnp.zeros_like(r.small)

    @pl.loop(0, 16, unroll=2)
    def _(j):
        group, m = split_sy(j)
        ours = (group == g).astype(F32)
        da = r.da[j]
        da_wide = da.astype(F32)
        dawd, inv = row_scale(da, wd)
        cosine, sine = tables(j, r.phase, r.base)
        at = pl.ds(pl.multiple_of(j * IMG, IMG), IMG)
        gq = turn(r.dq[m] * (ours * SCALE), cosine, -sine)
        gk = turn(r.dk[at, :] * (1.0 / LOG2E), cosine, -sine)
        grads = jnp.concatenate([gq, gk, r.dv[at, :]], axis=1).astype(BF16)
        back = dot(grads, mix, NT)
        cube = (inv * inv * inv) * (jnp.sum(back * da_wide, axis=1, keepdims=True) * (1.0 / D))
        grad = (inv * back - cube * dawd + r.ex[m] * ours) * r.sp[j].astype(F32)
        r.dpre[j] = grad.astype(BF16)
        r.small[:, :384] += dot((da_wide * inv).astype(BF16), grads, TN)
        r.small[:, 384:] += dot((da_wide * cube).astype(BF16), da, TN)


def conv_grad(r):
    total = jnp.zeros((384, HD), F32)
    for c in range(PW):
        grad = r.dpre[:, c * PH : c * PH + PH, :].reshape(256, HD)
        total = total + dot(r.patches[c], grad, TN)
    rows = [total[tap * 128 : tap * 128 + 96, :] for tap in range(3)] + [r.gup[...]]
    whole = jnp.concatenate(rows, axis=0).astype(BF16)
    for n in range(4):
        r.conv[n] = whole[80 * n : 80 * n + 80, :]


def block_of(group, e):
    i = div(e, 8)
    sx = mod(e, 8)
    sy = sy_of(group, i)
    x = div(sx, 2)
    y = div(sy, 4)
    z = 2 * mod(div(sy, 2), 2) + mod(sx, 2)
    core = mod(i, 2)
    return core, jnp.where(core == 0, (z * 4 + y) * 4 + x, (y * 4 + x) * 4 + z)


def lay_up(r):
    @pl.loop(0, 32, unroll=2)
    def _(e):
        cols = [r.every_u[block_of(group, e)].astype(F32) for group in range(4)]
        at = pl.ds(pl.multiple_of(e * HD, HD), HD)
        r.grad_up[at, :] = jnp.concatenate(cols, axis=0).T.astype(BF16)


def lay_down(r):
    @pl.loop(0, 32, unroll=2)
    def _(e):
        at = pl.ds(pl.multiple_of(e * HD, HD), HD)
        for group in range(4):
            r.grad_down[32 * group : 32 * group + 32, at] = r.every_d[block_of(group, e)]


def whole_kernel(names, *refs):
    r = types.SimpleNamespace(**dict(zip(names, refs)))
    sx = lax.axis_index("sx")
    sy = lax.axis_index("sy")
    g, head = split_sy(sy)
    members = [sy_of(g, m) for m in range(4)]
    mine = pl.ds(pl.multiple_of(head * HD, HD), HD)
    loads = []
    for at, (src, dst) in enumerate(
        [
            (r.w_down, r.dn),
            (r.w_up, r.up),
            (r.w_query, r.wq),
            (r.w_key, r.wk),
            (r.w_value, r.wv),
            (r.w_out, r.wo),
        ]
    ):
        copy = pltpu.make_async_copy(src, dst, r.local.at[at])
        copy.start()
        loads.append(copy)
    wide_u = Spread(r.every_u, r.s_wide_u)
    wide_d = Spread(r.every_d, r.s_wide_d)
    greet(wide_u)

    lat = Fan("sx", r.lat, r.lat_in, r.s_lat)
    r.own_off[...] = jnp.full((8, HD), r.offset[0].astype(F32))
    for k in range(2):
        row = r.pgrad[...].astype(F32)[k : k + 1, :]
        for c in range(PW):
            r.pg[k * PW + c : k * PW + c + 1, :] = row[:, c * CH : c * CH + CH]
    offs = Fan("sy", r.own_off, r.offs, r.s_off)
    text = Fan("sx", r.text, r.text_in, r.s_text)
    tgrad = Fan("sx", r.tgrad, r.tgrad_in, r.s_tgrad)
    r.lat_in[sx] = r.lat[...]
    r.offs[sy] = r.own_off[...]
    r.text_in[sx] = r.text[...]
    r.tgrad_in[sx] = r.tgrad[...]

    r.pad_lat[...] = jnp.zeros_like(r.pad_lat)
    lat.arrived()
    for n in range(8):
        r.rows_lat[2 * n : 2 * n + 2, :] = r.lat_in[n].astype(F32)
    r.pad_lat[:, CH : CH + PW * CH] = r.rows_lat[...].astype(BF16)
    lats = Fan("sy", r.pad_lat, r.lat_all, r.s_lats)
    r.lat_all[sy] = r.pad_lat[...]

    gain = r.gain[...].astype(F32)
    loads[0].wait()
    loads[1].wait()
    down = r.dn[...]
    both = dot(down, down, NT)
    high = both.astype(BF16)
    r.wd[:, :HD] = high
    r.wd[:, HD:] = (both - high.astype(F32)).astype(BF16)
    r.wu[...] = dot(down, r.up[...]).astype(BF16)
    scaled = (down.astype(F32) * gain).astype(BF16)
    for n, weight in enumerate([r.wq, r.wk, r.wv]):
        loads[2 + n].wait()
        r.mix[:, n * HD : (n + 1) * HD] = dot(scaled, weight[:, mine]).astype(BF16)
    loads[5].wait()
    r.nt[...] = dot(r.up[...], r.wo[mine, :], (((0,), (1,)), ((), ()))).astype(BF16)

    text.arrived()
    tgrad.arrived()
    for n in range(8):
        r.rows_text[4 * n : 4 * n + 4, :] = r.text_in[n].astype(F32)
        r.rows_grad[4 * n : 4 * n + 4, :] = r.tgrad_in[n].astype(F32)
    wide = r.rows_text[...]
    inverse = lax.rsqrt(jnp.mean(wide * wide, axis=1, keepdims=True) + EPS)
    normed = (wide * inverse * gain).astype(BF16)
    token = lax.broadcasted_iota(jnp.int32, (TXT, HD), 0).astype(F32)
    shift = jnp.where(token >= r.own_off[:1, :], float(IMG), 0.0)
    cosine, sine = trig((TXT, HD), token + shift + (sy * SB).astype(F32))
    query = dot(normed, r.wq[...])
    key = dot(normed, r.wk[...])
    value = dot(normed, r.wv[...])
    outer = dot(r.rows_grad[...].astype(BF16), r.wo[...], NT)
    for h in range(4):
        at = slice(h * HD, (h + 1) * HD)
        r.kv_out[h, :, :HD] = turn(key[:, at], cosine, sine).astype(BF16)
        r.kv_out[h, :, HD:] = value[:, at].astype(BF16)
        turned = turn(query[:, at], cosine, sine)
        r.qd_out[h, :, :HD] = (turned * (SCALE * LOG2E)).astype(BF16)
        r.qd_out[h, :, HD:] = outer[:, at].astype(BF16)
    kvs = Fan("sy", r.kv_out, r.kv_in, r.s_kv, lambda ty, to: split_sy(ty)[1])
    qds = Fan("group", r.qd_out, r.qd_in, r.s_qd, lambda ty, to: to)
    r.kv_in[sy] = r.kv_out[head]
    r.qd_in[head] = r.qd_out[head]

    offs.arrived()
    masks(r, g, members)

    lats.arrived()
    down_block(r)
    project(r, members)

    def text_ready():
        kvs.arrived()
        qds.arrived()
        kv = r.kv_in[...].reshape(512, 256)
        qd = r.qd_in[...].reshape(128, 256)
        r.kt[...] = kv[:, :HD]
        r.vtx[...] = kv[:, HD:]
        r.vtt[...] = kv[:, HD:].astype(F32).T.astype(BF16)
        r.q[1024:, :] = qd[:, :HD]
        r.do[1024:, :] = qd[:, HD:]

    def add_part(m):
        r.reorder[...] = dot(r.att[m * IMG : (m + 1) * IMG, :], r.nt[...], NT) + dot(
            r.da_own[m * IMG : (m + 1) * IMG, :], r.wu[...]
        ) * (1.0 / 32.0)
        for n in range(8):
            for k in range(2):
                r.part[8 * m + n, k * PW : (k + 1) * PW, :] = r.reorder[
                    pl.ds(2 * n + k, PW, stride=PH), :
                ].astype(BF16)

    attend_images(r, 1, 7 - g, text_ready)
    add_part(2)
    add_part(3)
    attend_images(r, 0, g, lambda: None)
    add_part(0)
    add_part(1)

    e, _ = ring("team")
    parts = Fan("team", r.part, r.part_in, r.s_part, lambda ty, to: to)
    r.part_in[e] = r.part[e]
    attend_text(r, 8 - g, None)
    for m in range(4):
        r.att_txt[m] = r.att[1024 + m * TXT : 1024 + (m + 1) * TXT, :]
    atx = Fan("group", r.att_txt, r.atx, r.s_atx, lambda ty, to: to)
    r.atx[head] = r.att_txt[head]
    r.dk[...] = jnp.zeros_like(r.dk)
    r.dv[...] = jnp.zeros_like(r.dv)
    parts.arrived()
    pre = jnp.sum(r.part_in[...].astype(F32), axis=0)
    sig = sigmoid(pre)
    act = (pre * sig).astype(BF16)
    slope = sig * (1.0 + pre * (1.0 - sig))
    pgrad = r.pg[...].astype(BF16)
    r.gown[...] = (dot(pgrad, r.w_uo[...]) * slope).astype(BF16)
    ups = Fan("team", r.gown, r.gall, r.s_up)
    r.gall[e] = r.gown[...]
    pred = dot(act, r.w_uo[...], NT)
    for k in range(2):
        for c in range(PW):
            r.pred_rows[k : k + 1, c * CH : c * CH + CH] = pred[k * PW + c : k * PW + c + 1, :]
    r.pred[...] = r.pred_rows[...].astype(BF16)
    r.gup[...] = dot(pgrad, act, TN)
    for p, diagonal in ((0, g), (1, 7 - g)):
        lse = r.lse[p, :1, :]

        @pl.loop(0, diagonal + 1)
        def _(j):
            normalise(r.e_img.at[4 * p + j], r.m_img.at[4 * p + j], lse)

        normalise(r.e_txt.at[p], r.m_txt.at[p], lse)

    @pl.loop(0, 8 - g)
    def _(j):
        normalise(r.e_q.at[j], r.m_q.at[j], r.lse[2, :1, :HD])

    ups.arrived()
    for m in range(4):
        for n in range(8):
            nat = r.gall[8 * m + n].astype(F32)
            for k in range(2):
                r.order[pl.ds(m * IMG + 2 * n + k, PW, stride=PH), :] = nat[
                    k * PW : (k + 1) * PW, :
                ]
    r.gpu[...] = r.order[...].astype(BF16)
    r.do[:1024, :] = dot(r.gpu[...], r.nt[...]).astype(BF16)

    gpu = r.gpu[...]
    grad = dot(gpu, r.wu[...], NT) * (1.0 / 32.0)
    for m in range(4):
        r.ex[m] = grad[m * IMG : (m + 1) * IMG, :]
    own = r.da_own[...]
    r.small_u[:, :HD] = dot(gpu, r.att[:1024, :], TN)
    r.small_u[:, HD : 2 * HD] = dot(gpu, own, TN) * (1.0 / 32.0)
    r.small_u[:, 2 * HD :] = dot(own, gpu, TN) * (1.0 / 32.0)
    for n in range(4):
        r.low_u[n] = r.small_u[32 * n : 32 * n + 32, :].astype(BF16)
    heads_u = Fan("head", r.low_u, r.low_u_in, r.s_hu, lambda ty, to: to)
    r.low_u_in[g] = r.low_u[g]

    backward_images(r, 1, 7 - g, members)

    heads_u.arrived()
    low_u = jnp.sum(r.low_u_in[...].astype(F32), axis=0).astype(BF16)

    @pl.loop(0, 8)
    def _(c):
        at = pl.ds(pl.multiple_of(c * 512, 512), 512)
        grad = dot(low_u[:, :HD], r.wo[mine, at]) + dot(low_u[:, HD : 2 * HD], r.dn[:, at])
        for k in range(4):
            r.wide_u[4 * c + k] = grad[:, k * HD : (k + 1) * HD].astype(BF16)

    sums_u = Fan("team", r.wide_u, r.wide_u_in, r.s_su, lambda ty, to: to)
    r.wide_u_in[e] = r.wide_u[e]

    backward_images(r, 0, g, members)

    atx.arrived()
    joined = jnp.concatenate([r.atx[h] for h in range(4)], axis=1)

    @pl.loop(0, 8)
    def _(c):
        at = pl.ds(pl.multiple_of(c * 512, 512), 512)
        out = dot(joined, r.wo[:, at])
        for n in range(8):
            r.mixed[n, :, at] = out[4 * n : 4 * n + 4, :].astype(BF16)

    mixes = Fan("sx", r.mixed, r.mixed_in, r.s_mix, lambda ty, to: to)
    r.mixed_in[sx] = r.mixed[sx]

    backward_text(r, 8 - g)

    sums_u.arrived()
    wide_u.plane(jnp.sum(r.wide_u_in[...].astype(F32), axis=0).astype(BF16))
    image_grads(r, g)

    for n in range(4):
        r.low_d[n] = r.small[32 * n : 32 * n + 32, :].astype(BF16)
    heads_d = Fan("head", r.low_d, r.low_d_in, r.s_hd, lambda ty, to: to)
    r.low_d_in[g] = r.low_d[g]
    wide_u.slabs()
    conv_grad(r)
    convs = Fan("head", r.conv, r.conv_in, r.s_c1, lambda ty, to: to)
    r.conv_in[g] = r.conv[g]
    heads_d.arrived()
    low = jnp.sum(r.low_d_in[...].astype(F32), axis=0).astype(BF16)

    @pl.loop(0, 8)
    def _(c):
        at = pl.ds(pl.multiple_of(c * 512, 512), 512)
        grad = dot(low[:, :HD], r.wq[at, mine], NT)
        grad = grad + dot(low[:, HD : 2 * HD], r.wk[at, mine], NT)
        grad = grad + dot(low[:, 2 * HD : 3 * HD], r.wv[at, mine], NT)
        grad = grad * r.gain[:, at].astype(F32)
        grad = grad + dot(low_u[:, 2 * HD :], r.up[at, :], NT)
        grad = grad - dot(low[:, 3 * HD :], r.dn[:, at])
        for k in range(4):
            r.wide_d[4 * c + k] = grad[:, k * HD : (k + 1) * HD].astype(BF16)

    sums_d = Fan("team", r.wide_d, r.wide_d_in, r.s_sd, lambda ty, to: to)
    r.wide_d_in[e] = r.wide_d[e]
    convs.arrived()
    r.conv_a[...] = jnp.sum(r.conv_in[...].astype(F32), axis=0).astype(BF16)
    beside = Fan("sx", r.conv_a, r.conv_sx, r.s_c2)
    r.conv_sx[sx] = r.conv_a[...]
    wide_u.pass_on()
    mixes.arrived()
    total = r.text[...].astype(F32)
    for n in range(8):
        total = total + r.mixed_in[n].astype(F32)
    r.text_out[...] = total.astype(BF16)
    beside.arrived()
    r.conv_b[...] = jnp.sum(r.conv_sx[...].astype(F32), axis=0).astype(BF16)
    along = Fan("group", r.conv_b, r.conv_gr, r.s_c3)
    r.conv_gr[head] = r.conv_b[...]
    sums_d.arrived()
    wide_d.plane(jnp.sum(r.wide_d_in[...].astype(F32), axis=0).astype(BF16))
    along.arrived()
    r.conv_c[...] = jnp.sum(r.conv_gr[...].astype(F32), axis=0).astype(BF16)
    across = Fan("head", r.conv_c, r.conv_all, r.s_c4)
    r.conv_all[g] = r.conv_c[...]
    wide_d.slabs()
    wide_u.arrived()
    lay_up(r)
    wide_d.pass_on()
    across.arrived()
    wide_d.arrived()
    lay_down(r)
    for fan in (
        lat,
        offs,
        text,
        tgrad,
        lats,
        kvs,
        qds,
        parts,
        atx,
        ups,
        heads_u,
        sums_u,
        mixes,
        heads_d,
        convs,
        sums_d,
        beside,
        along,
        across,
    ):
        fan.sent()
    wide_u.sent()
    wide_d.sent()


def whole(inputs, cid):
    sds = jax.ShapeDtypeStruct
    dma = pltpu.SemaphoreType.DMA
    space = pltpu.VMEM
    outs = {
        "pred": ((2, PW * CH), BF16),
        "text_out": ((4, D), BF16),
        "grad_down": ((HD, D), BF16),
        "grad_up": ((D, HD), BF16),
        "conv_all": ((4, 80, HD), BF16),
    }
    scratch = {
        "pg": ((32, CH), F32),
        "pred_rows": ((2, PW * CH), F32),
        "every_u": ((2, 64, 32, HD), BF16),
        "every_d": ((2, 64, 32, HD), BF16),
        "dn": ((HD, D), BF16),
        "up": ((D, HD), BF16),
        "wq": ((D, 512), BF16),
        "wk": ((D, 512), BF16),
        "wv": ((D, 512), BF16),
        "wo": ((512, D), BF16),
        "lat_in": ((8, 2, PW * CH), BF16),
        "text_in": ((8, 4, D), BF16),
        "tgrad_in": ((8, 4, D), BF16),
        "own_off": ((8, HD), F32),
        "offs": ((16, 8, HD), F32),
        "pad_lat": ((PH, 640), BF16),
        "rows_lat": ((PH, PW * CH), F32),
        "lat_all": ((16, PH, 640), BF16),
        "rows_text": ((TXT, D), F32),
        "rows_grad": ((TXT, D), F32),
        "wd": ((HD, 256), BF16),
        "wu": ((HD, HD), BF16),
        "mix": ((HD, 384), BF16),
        "nt": ((HD, HD), BF16),
        "kv_out": ((4, TXT, 256), BF16),
        "qd_out": ((4, TXT, 256), BF16),
        "kv_in": ((16, TXT, 256), BF16),
        "qd_in": ((4, TXT, 256), BF16),
        "phase": ((2, 16, HD), F32),
        "bias_tt": ((512, 128), F32),
        "bias_ti": ((512, HD), F32),
        "vis": ((8, HD), F32),
        "wpad": ((384, HD), F32),
        "wide": ((3, 256, 640), F32),
        "patches": ((16, 256, 384), BF16),
        "da": ((16, 256, HD), BF16),
        "sp": ((16, 256, HD), BF16),
        "da_own": ((1024, HD), BF16),
        "k": ((4096, HD), BF16),
        "v": ((4096, HD), BF16),
        "vt": ((HD, 4096), BF16),
        "q": ((1152, HD), BF16),
        "kt": ((512, HD), BF16),
        "vtx": ((512, HD), BF16),
        "vtt": ((HD, 512), BF16),
        "e_img": ((12, 512, 512), BF16),
        "m_img": ((12, 8, 512), F32),
        "e_txt": ((2, 512, 512), BF16),
        "m_txt": ((2, 8, 512), F32),
        "e_q": ((9, 512, 128), BF16),
        "m_q": ((9, 8, 128), F32),
        "lse": ((3, 8, 512), F32),
        "att": ((1152, HD), BF16),
        "reorder": ((IMG, HD), F32),
        "part": ((32, 32, HD), BF16),
        "part_in": ((32, 32, HD), BF16),
        "att_txt": ((4, TXT, HD), BF16),
        "atx": ((4, TXT, HD), BF16),
        "gown": ((32, HD), BF16),
        "gall": ((32, 32, HD), BF16),
        "gup": ((CH, HD), F32),
        "order": ((1024, HD), F32),
        "gpu": ((1024, HD), BF16),
        "do": ((1152, HD), BF16),
        "dk": ((4096, HD), F32),
        "dv": ((4096, HD), F32),
        "dq": ((4, IMG, HD), F32),
        "dqs": ((512, HD), F32),
        "ex": ((4, IMG, HD), F32),
        "dpre": ((16, IMG, HD), BF16),
        "small_u": ((HD, 384), F32),
        "low_u": ((4, 32, 384), BF16),
        "low_u_in": ((4, 32, 384), BF16),
        "small": ((HD, 512), F32),
        "low_d": ((4, 32, 512), BF16),
        "low_d_in": ((4, 32, 512), BF16),
        "wide_u": ((32, 32, HD), BF16),
        "wide_u_in": ((32, 32, HD), BF16),
        "wide_d": ((32, 32, HD), BF16),
        "wide_d_in": ((32, 32, HD), BF16),
        "mixed": ((8, 4, D), BF16),
        "mixed_in": ((8, 4, D), BF16),
        "conv": ((4, 80, HD), BF16),
        "conv_in": ((4, 80, HD), BF16),
        "conv_a": ((80, HD), BF16),
        "conv_sx": ((8, 80, HD), BF16),
        "conv_b": ((80, HD), BF16),
        "conv_gr": ((4, 80, HD), BF16),
        "conv_c": ((80, HD), BF16),
    }
    sems = {"local": (6,), "s_wide_u": (2, 8), "s_wide_d": (2, 8)}
    for name in (
        ("lat", "off", "text", "tgrad", "lats", "kv", "qd", "part", "atx", "up", "hu", "su")
        + ("mix", "hd", "sd", "c1", "c2", "c3", "c4")
    ):
        sems["s_" + name] = (2,)
    names = list(inputs) + list(outs) + list(scratch) + list(sems)
    hbm = {"w_down", "w_up", "w_query", "w_key", "w_value", "w_out"}
    specs = []
    for name in inputs:
        kind = pl.ANY if name in hbm else pltpu.SMEM if name == "offset" else pltpu.VMEM
        specs.append(pl.BlockSpec(memory_space=kind))
    return pl.pallas_call(
        functools.partial(whole_kernel, names),
        out_shape=[sds(*v) for v in outs.values()],
        in_specs=specs,
        out_specs=vmem(len(outs)),
        scratch_shapes=[space(*v) for v in scratch.values()] + [dma(v) for v in sems.values()],
        compiler_params=pltpu.CompilerParams(
            collective_id=cid, has_side_effects=True, vmem_limit_bytes=60 * 2**20
        ),
    )(*inputs.values())


def rope_base():
    half = HD // 2
    freq = np.exp(-(2.0 * np.arange(half) / HD) * math.log(ROPE_BASE))
    slot = np.arange(IMG)
    position = (slot % PH) * PW + slot // PH
    angle = position[:, None] * freq[None, :]
    cosine = np.concatenate([np.cos(angle), np.cos(angle)], axis=1)
    sine = np.concatenate([-np.sin(angle), np.sin(angle)], axis=1)
    return jnp.asarray(np.stack([cosine, sine]).astype(np.float32))


def shards(
    text_tokens,
    latent,
    image_offset,
    norm_gain,
    w_query,
    w_key,
    w_value,
    w_out,
    w_down_conv,
    w_down_proj,
    w_up_proj,
    w_up_out,
    pred_grad,
    text_grad,
):
    pred, text_out, grad_down_proj, grad_up_proj, conv = whole(
        {
            "offset": image_offset,
            "text": text_tokens[0],
            "tgrad": text_grad[0],
            "lat": latent[0],
            "gain": norm_gain[None],
            "pgrad": pred_grad[0],
            "wconv": w_down_conv,
            "w_uo": w_up_out.T,
            "base": rope_base(),
            "w_down": w_down_proj,
            "w_up": w_up_proj,
            "w_query": w_query,
            "w_key": w_key,
            "w_value": w_value,
            "w_out": w_out,
        },
        1,
    )
    conv = conv.reshape(320, HD).astype(F32)
    return (
        pred[None],
        text_out[None],
        conv[:288],
        grad_down_proj.astype(F32),
        grad_up_proj.astype(F32),
        conv[288:].T,
    )


def solution(mesh):
    placed = (
        P("sy", "sx", None),
        P("sy", "sx", None),
        P("sy"),
        P(),
        P(None, "sx"),
        P(None, "sx"),
        P(None, "sx"),
        P("sx", None),
        P(),
        P(),
        P(),
        P(),
        P("sy", "sx", None),
        P("sy", "sx", None),
    )
    return jax.shard_map(
        shards,
        mesh=mesh,
        in_specs=placed,
        out_specs=(P("sy", "sx", None), P("sy", "sx", None), P(), P(), P(), P()),
        check_vma=False,
    )
```

```python
import functools
import math
import types

import jax
import jax.numpy as jnp
import numpy as np
from jax import lax
from jax.experimental import pallas as pl
from jax.experimental.pallas import tpu as pltpu
from jax.sharding import PartitionSpec as P

MESH = pl.DeviceIdType.MESH
F32 = jnp.float32
BF16 = jnp.bfloat16
HD = 128
SB = 288
TXT = 32
IMG = 256
PH = 16
PW = 16
CH = 32
D = 4096
EPS = 1e-05
NEG = -1e30
LOG2E = math.log2(math.e)
SCALE = HD ** (-0.5)
ROPE_BASE = 500000.0
SIZES = {"sx": 8, "sy": 16, "group": 4, "head": 4, "team": 32}
NT = (((1,), (1,)), ((), ()))
TN = (((0,), (0,)), ((), ()))


def dot(a, b, dims=(((1,), (0,)), ((), ()))):
    return lax.dot_general(a, b, dims, preferred_element_type=F32)


def vmem(count):
    return [pl.BlockSpec(memory_space=pltpu.VMEM)] * count


def mod(a, n):
    return a % n if isinstance(a, int) else lax.rem(a, n)


def div(a, n):
    return a // n if isinstance(a, int) else lax.div(a, n)


def sy_of(g, i):
    if isinstance(i, int):
        return 2 * g + i if i < 2 else 12 - 2 * g + i
    return jnp.where(i < 2, 2 * g + i, 12 - 2 * g + i)


def split_sy(sy):
    low = sy < 8
    g = jnp.where(low, div(sy, 2), div(15 - sy, 2))
    i = mod(sy, 2) + jnp.where(low, 0, 2)
    return g, i


def ring(kind):
    sx = lax.axis_index("sx")
    sy = lax.axis_index("sy")
    g, i = split_sy(sy)
    if kind == "sx":
        return sx, lambda o: (mod(sx + o, 8), sy, mod(sx + o, 8))
    if kind == "sy":
        return sy, lambda o: (sx, mod(sy + o, 16), mod(sy + o, 16))
    if kind == "group":
        return i, lambda o: (sx, sy_of(g, mod(i + o, 4)), mod(i + o, 4))
    if kind == "head":
        return g, lambda o: (sx, sy_of(mod(g + o, 4), i), mod(g + o, 4))
    e = i * 8 + sx

    def peer(o):
        f = mod(e + o, 32)
        return mod(f, 8), sy_of(g, div(f, 8)), f

    return e, peer


def remote(src, dst, send, recv, to):
    copy = pltpu.make_async_remote_copy(
        src_ref=src,
        dst_ref=dst,
        send_sem=send,
        recv_sem=recv,
        device_id=to,
        device_id_type=MESH,
    )
    copy.start()
    return copy


class Fan:
    def __init__(self, kind, source, land, sems, slot_of=None):
        own, peer = ring(kind)
        self.land = land.at[pl.ds(0, SIZES[kind] - 1)]
        self.sems = sems

        @pl.loop(1, SIZES[kind])
        def _(o):
            tx, ty, to = peer(o)
            src = source if slot_of is None else source.at[slot_of(ty, to)]
            remote(src, land.at[own], sems.at[0], sems.at[1], (tx, ty))

    def arrived(self):
        pltpu.make_async_copy(self.land, self.land, self.sems.at[1]).wait()

    def sent(self):
        pltpu.make_async_copy(self.land, self.land, self.sems.at[0]).wait()


def sigmoid(v):
    return 1.0 / (1.0 + jnp.exp(-v))


def turn(v, cosine, sine):
    return v * cosine + pltpu.roll(v, 64, 1) * sine


def trig(shape, position):
    lane = lax.broadcasted_iota(jnp.int32, shape, 1)
    step = (lane % 64).astype(F32)
    angle = position * jnp.exp(step * (-2.0 / HD * math.log(ROPE_BASE)))
    sine = jnp.sin(angle)
    return jnp.cos(angle), jnp.where(lane < 64, -sine, sine)


def tables(j, phase_ref, base_ref):
    pc = phase_ref[0, pl.ds(j, 1), :]
    ps = phase_ref[1, pl.ds(j, 1), :]
    bc = base_ref[0]
    bs = base_ref[1]
    return pc * bc - ps * bs, ps * bc + pc * bs


def row_sum(v):
    return dot(v.astype(BF16), jnp.ones((HD, HD), BF16))


def row_scale(da, wd):
    both = dot(da, wd)
    dawd = both[:, :HD] + both[:, HD:]
    return dawd, lax.rsqrt(row_sum(dawd * da.astype(F32)) * (1.0 / D) + EPS)


def lanes(column):
    return column.T[:1, :]


def place(x, y, z, core):
    return 2 * x + mod(z, 2), 4 * y + 2 * div(z, 2) + core


class Spread:
    def __init__(self, every, sems):
        self.every = every
        self.sems = sems
        sx = lax.axis_index("sx")
        sy = lax.axis_index("sy")
        self.core = mod(sy, 2)
        x = div(sx, 2)
        y = div(sy, 4)
        z = 2 * mod(div(sy, 2), 2) + mod(sx, 2)
        self.even = self.core == 0
        self.p1 = jnp.where(self.even, x, z)
        self.p2 = jnp.where(self.even, y, x)
        self.p3 = jnp.where(self.even, z, y)
        self.twin = place(x, y, z, 1 - self.core)
        self.here = every.at[self.core]
        self.spot = (self.p3 * 4 + self.p2) * 4 + self.p1
        self.live = []

    def chip(self, a, b, c):
        a = mod(a, 4)
        b = mod(b, 4)
        c = mod(c, 4)
        even = self.even
        return place(
            jnp.where(even, a, b), jnp.where(even, b, c), jnp.where(even, c, a), self.core
        )

    def send(self, ref, n, to):
        copy = remote(ref, ref, self.sems.at[0, n], self.sems.at[1, n], to)
        self.live.append(copy)
        return copy

    def slab(self, p):
        return self.here.at[pl.ds(mod(p, 4) * 16, 16)]

    def plane(self, block):
        self.every[self.core, self.spot] = block
        mine = self.here.at[self.spot]

        @pl.loop(1, 16)
        def _(o):
            to = self.chip(self.p1 + mod(o, 4), self.p2 + div(o, 4), self.p3)
            remote(mine, mine, self.sems.at[0, 0], self.sems.at[1, 0], to)

    def slabs(self):
        plane = self.here.at[pl.ds(0, 15)]
        pltpu.make_async_copy(plane, plane, self.sems.at[1, 0]).wait()
        own = self.slab(self.p3)
        self.wave = [self.send(own, o, self.chip(self.p1, self.p2, self.p3 + o)) for o in (1, 3, 2)]
        self.twins = [self.send(own, 4, self.twin)]

    def pass_on(self):
        for o, copy in zip((1, 3, 2), self.wave):
            copy.wait_recv()
            self.twins.append(self.send(self.slab(self.p3 + 4 - o), 4 + o, self.twin))

    def arrived(self):
        for copy in self.twins:
            copy.wait_recv()

    def sent(self):
        plane = self.here.at[pl.ds(0, 15)]
        pltpu.make_async_copy(plane, plane, self.sems.at[0, 0]).wait()
        for copy in self.live:
            copy.wait_send()


def greet(wide):
    barrier = pltpu.get_barrier_semaphore()
    for kind in ("team", "sy"):
        _, peer = ring(kind)

        @pl.loop(1, SIZES[kind])
        def _(o):
            tx, ty, _ = peer(o)
            pl.semaphore_signal(barrier, inc=1, device_id=(tx, ty), device_id_type=MESH)

    @pl.loop(1, 16)
    def _(o):
        to = wide.chip(wide.p1 + mod(o, 4), wide.p2 + div(o, 4), wide.p3)
        pl.semaphore_signal(barrier, inc=1, device_id=to, device_id_type=MESH)

    @pl.loop(1, 4)
    def _(o):
        to = wide.chip(wide.p1, wide.p2, wide.p3 + o)
        pl.semaphore_signal(barrier, inc=1, device_id=to, device_id_type=MESH)

    return lambda: pl.semaphore_wait(barrier, 31 + 15 + 15 + 3)


def masks(r, g, members):
    block = lax.broadcasted_iota(jnp.int32, (16, HD), 0).astype(F32)
    cosine, sine = trig((16, HD), block * float(SB) + jnp.max(r.offs[...], axis=1))
    r.phase[0] = cosine
    r.phase[1] = sine
    starts = [r.offs[b][:1, :] for b in members]
    row = lax.broadcasted_iota(jnp.int32, (512, TXT), 0)
    query = lax.broadcasted_iota(jnp.int32, (512, TXT), 1)
    for m in range(4):
        b = members[m]
        seen = (row // TXT < b) | ((row // TXT == b) & (row % TXT <= query))
        r.bias_tt[:, m * TXT : (m + 1) * TXT] = jnp.where(seen, 0.0, NEG)
    lane = lax.broadcasted_iota(jnp.int32, (8, HD), 1)
    start = starts[0]
    owner = jnp.full((8, HD), members[0], jnp.int32)
    for m in range(1, 4):
        start = jnp.where(lane // TXT == m, starts[m], start)
        owner = jnp.where(lane // TXT == m, members[m], owner)
    late = jnp.where((lane % TXT).astype(F32) >= start, 1.0, 0.0)
    r.vis[...] = late + owner.astype(F32)
    lane = lax.broadcasted_iota(jnp.int32, (512, HD), 1)
    row = lax.broadcasted_iota(jnp.int32, (512, HD), 0)
    start = jnp.broadcast_to(starts[0], (512, HD))
    owner = jnp.full((512, HD), members[0], jnp.int32)
    for m in range(1, 4):
        start = jnp.where(lane == m, starts[m], start)
        owner = jnp.where(lane == m, members[m], owner)
    seen = (row // TXT < owner) | ((row // TXT == owner) & ((row % TXT).astype(F32) < start))
    r.bias_ti[...] = jnp.where(seen, 0.0, NEG)


def down_block(r):
    r.wpad[...] = jnp.zeros_like(r.wpad)
    for tap in range(3):
        r.wpad[tap * 128 : tap * 128 + 96, :] = r.wconv[tap * 96 : tap * 96 + 96, :].astype(F32)
    mid = r.lat_all[...].reshape(256, 640).astype(F32)
    row = lax.broadcasted_iota(jnp.int32, mid.shape, 0) % PH
    r.wide[0] = jnp.where(row == 0, 0.0, pltpu.roll(mid, 1, 0))
    r.wide[1] = mid
    r.wide[2] = jnp.where(row == PH - 1, 0.0, pltpu.roll(mid, 16 * PH - 1, 0))
    weight = r.wpad[...].astype(BF16)
    for c in range(PW):
        for tap in range(3):
            r.patches[c, :, tap * 128 : tap * 128 + 128] = r.wide[
                tap, :, c * CH : c * CH + 128
            ].astype(BF16)
        pre = dot(r.patches[c], weight)
        sig = sigmoid(pre)
        r.da[:, c * PH : c * PH + PH, :] = (pre * sig).astype(BF16).reshape(16, PH, HD)
        r.sp[:, c * PH : c * PH + PH, :] = (
            (sig * (1.0 + pre * (1.0 - sig))).astype(BF16).reshape(16, PH, HD)
        )


def project(r, members):
    mix_kv = r.mix[:, HD:]
    mix_q = r.mix[:, :HD]
    wd = r.wd[...]

    @pl.loop(0, 4)
    def _(n):
        da = r.da[pl.ds(4 * n, 4)].reshape(4 * IMG, HD)
        _, inv = row_scale(da, wd)
        scaled = (da.astype(F32) * inv).astype(BF16)
        kv = dot(scaled, mix_kv)
        whole = pl.ds(pl.multiple_of(n * 1024, 1024), 1024)
        r.vt[:, whole] = dot(mix_kv[:, HD:], scaled, (((0,), (1,)), ((), ()))).astype(BF16)
        for m in range(4):
            j = 4 * n + m
            cosine, sine = tables(j, r.phase, r.base)
            rows = pl.ds(pl.multiple_of(j * IMG, IMG), IMG)
            part = kv[m * IMG : (m + 1) * IMG, :]
            r.k[rows, :] = turn(part[:, :HD], cosine, sine).astype(BF16)
            r.v[rows, :] = part[:, HD:].astype(BF16)

    for m in range(4):
        r.da_own[m * IMG : (m + 1) * IMG, :] = r.da[members[m]]
    da = r.da_own[...]
    _, inv = row_scale(da, wd)
    queries = dot((da.astype(F32) * inv).astype(BF16), mix_q) * (SCALE * LOG2E)
    for m in range(4):
        rows = slice(m * IMG, (m + 1) * IMG)
        cosine, sine = tables(members[m], r.phase, r.base)
        r.q[rows, :] = turn(queries[rows, :], cosine, sine).astype(BF16)


def tile_rows(j):
    return pl.ds(pl.multiple_of(j * 512, 512), 512)


def absorb(state, scores, vt, e_ref, m_ref):
    top = jnp.max(scores, axis=0, keepdims=True)
    new = top if state is None else jnp.maximum(state[0], top)
    raised = jnp.exp2(scores - new)
    low = raised.astype(BF16)
    e_ref[...] = low
    m_ref[...] = jnp.broadcast_to(new, m_ref.shape)
    total = jnp.sum(raised, axis=0, keepdims=True)
    mixed = dot(vt, low)
    if state is None:
        return new, total, mixed
    old = jnp.exp2(state[0] - new)
    return new, state[1] * old + total, state[2] * old + mixed


def conclude(r, p, width, state):
    peak, total, acc = state
    r.att[p * 512 : p * 512 + width, :] = (acc / total).T.astype(BF16)
    r.lse[p, :, :width] = jnp.broadcast_to(peak + jnp.log2(total), (8, width))


def diagonal_mask(scores):
    bottom = lax.broadcasted_iota(jnp.int32, scores.shape, 0) >= IMG
    left = lax.broadcasted_iota(jnp.int32, scores.shape, 1) < IMG
    return jnp.where(bottom & left, NEG, scores)


def attend_images(r, p, diagonal, text_ready):
    q = r.q[p * 512 : p * 512 + 512, :]
    base = 4 * p

    def tile(j):
        return dot(r.k[tile_rows(j), :], q, NT)

    state = absorb(
        None,
        diagonal_mask(tile(diagonal)),
        r.vt[:, tile_rows(diagonal)],
        r.e_img.at[base + diagonal],
        r.m_img.at[base + diagonal],
    )

    def body(j, state):
        return absorb(
            state, tile(j), r.vt[:, tile_rows(j)], r.e_img.at[base + j], r.m_img.at[base + j]
        )

    state = lax.fori_loop(0, diagonal, body, state)
    text_ready()
    scores = dot(r.kt[...], q, NT)
    bias = jnp.concatenate(
        [
            jnp.broadcast_to(r.bias_ti[:, 2 * p + half : 2 * p + half + 1], (512, IMG))
            for half in range(2)
        ],
        axis=1,
    )
    scores = jnp.where(bias < 0.0, NEG, scores)
    state = absorb(state, scores, r.vtt[...], r.e_txt.at[p], r.m_txt.at[p])
    conclude(r, p, 512, state)


def attend_text(r, count, kept):
    q = r.q[1024:, :]
    vis = r.vis[:1, :]
    scores = jnp.where(r.bias_tt[...] < 0.0, NEG, dot(r.kt[...], q, NT))
    state = absorb(None, scores, r.vtt[...], r.e_q.at[8], r.m_q.at[8])

    def body(j, state):
        scores = dot(r.k[tile_rows(j), :], q, NT)
        block = 2 * j + (lax.broadcasted_iota(jnp.int32, scores.shape, 0) >= IMG).astype(jnp.int32)
        scores = jnp.where(block.astype(F32) < vis, scores, NEG)
        return absorb(state, scores, r.vt[:, tile_rows(j)], r.e_q.at[j], r.m_q.at[j])

    conclude(r, 2, 128, lax.fori_loop(0, count, body, state))


def normalise(e_ref, m_ref, lse):
    factor = jnp.exp2(m_ref[:1, :] - lse)
    e_ref[...] = (e_ref[...].astype(F32) * factor).astype(BF16)


def backward_rows(r, p, width):
    rows = slice(p * 512, p * 512 + width)
    q = r.q[rows, :]
    do = r.do[rows, :]
    sums = jnp.sum(do.astype(F32) * r.att[rows, :].astype(F32), axis=1, keepdims=True)
    return q, do, lanes(jnp.broadcast_to(sums, (width, HD)))


def backward_images(r, p, diagonal, members):
    q, do, delta = backward_rows(r, p, 512)
    base = 4 * p

    probs = r.e_txt[p].astype(F32)
    grad = (probs * (dot(r.vtx[...], do, NT) - delta)).astype(BF16)
    r.dqs[...] = dot(grad, r.kt[...], TN)

    @pl.loop(0, diagonal + 1)
    def _(j):
        at = tile_rows(j)
        keys = r.k[at, :]
        probs = r.e_img[base + j]
        grad = (probs.astype(F32) * (dot(r.v[at, :], do, NT) - delta)).astype(BF16)
        r.dv[at, :] += dot(probs, do)
        r.dk[at, :] += dot(grad, q)
        r.dqs[...] += dot(grad, keys, TN)

    for half in range(2):
        r.dq[2 * p + half] = r.dqs[half * IMG : (half + 1) * IMG, :]


def backward_text(r, count):
    q, do, delta = backward_rows(r, 2, 128)

    @pl.loop(0, count)
    def _(j):
        at = tile_rows(j)
        probs = r.e_q[j]
        grad = (probs.astype(F32) * (dot(r.v[at, :], do, NT) - delta)).astype(BF16)
        r.dv[at, :] += dot(probs, do)
        r.dk[at, :] += dot(grad, q)


def image_grads(r, g):
    wd = r.wd[...]
    mix = r.mix[...]
    r.small[...] = jnp.zeros_like(r.small)

    @pl.loop(0, 4)
    def _(n):
        da = r.da[pl.ds(4 * n, 4)].reshape(4 * IMG, HD)
        da_wide = da.astype(F32)
        dawd, inv = row_scale(da, wd)
        extra = []
        for k in range(4):
            j = 4 * n + k
            group, m = split_sy(j)
            ours = (group == g).astype(F32)
            cosine, sine = tables(j, r.phase, r.base)
            at = pl.ds(pl.multiple_of(j * IMG, IMG), IMG)
            rows = slice(k * IMG, (k + 1) * IMG)
            gq = turn(r.dq[m] * (ours * SCALE), cosine, -sine)
            gk = turn(r.dk[at, :] * (1.0 / LOG2E), cosine, -sine)
            r.grads[rows, :HD] = gq.astype(BF16)
            r.grads[rows, HD : 2 * HD] = gk.astype(BF16)
            r.grads[rows, 2 * HD :] = r.dv[at, :].astype(BF16)
            extra.append(r.ex[m] * ours)
        grads = r.grads[...]
        back = dot(grads, mix, NT)
        cube = (inv * inv * inv) * (row_sum(back * da_wide) * (1.0 / D))
        slope = r.sp[pl.ds(4 * n, 4)].reshape(4 * IMG, HD).astype(F32)
        grad = (inv * back - cube * dawd + jnp.concatenate(extra, axis=0)) * slope
        r.dpre[pl.ds(4 * n, 4)] = grad.astype(BF16).reshape(4, IMG, HD)
        r.small[:, :384] += dot((da_wide * inv).astype(BF16), grads, TN)
        r.small[:, 384:] += dot((da_wide * cube).astype(BF16), da, TN)


def conv_grad(r):
    total = jnp.zeros((384, HD), F32)
    for c in range(PW):
        grad = r.dpre[:, c * PH : c * PH + PH, :].reshape(256, HD)
        total = total + dot(r.patches[c], grad, TN)
    rows = [total[tap * 128 : tap * 128 + 96, :] for tap in range(3)] + [r.gup[...]]
    whole = jnp.concatenate(rows, axis=0).astype(BF16)
    for n in range(4):
        r.conv[n] = whole[80 * n : 80 * n + 80, :]


def block_of(group, e):
    sx = e % 8
    sy = sy_of(group, e // 8)
    x = sx // 2
    y = sy // 4
    z = 2 * ((sy // 2) % 2) + sx % 2
    core = sy % 2
    return core, (z * 4 + y) * 4 + x if core == 0 else (y * 4 + x) * 4 + z


def lay_up(r):
    for e in range(32):
        cols = [r.every_u[block_of(group, e)].astype(F32) for group in range(4)]
        r.grad_up[e * HD : (e + 1) * HD, :] = jnp.concatenate(cols, axis=0).T.astype(BF16)


def lay_down(r):
    for e in range(32):
        for group in range(4):
            r.grad_down[32 * group : 32 * group + 32, e * HD : (e + 1) * HD] = r.every_d[
                block_of(group, e)
            ]


def whole_kernel(names, *refs):
    r = types.SimpleNamespace(**dict(zip(names, refs)))
    sx = lax.axis_index("sx")
    sy = lax.axis_index("sy")
    g, head = split_sy(sy)
    members = [sy_of(g, m) for m in range(4)]
    mine = pl.ds(pl.multiple_of(head * HD, HD), HD)
    loads = []
    for at, (src, dst) in enumerate(
        [
            (r.w_down, r.dn),
            (r.w_up, r.up),
            (r.w_query, r.wq),
            (r.w_key, r.wk),
            (r.w_value, r.wv),
            (r.w_out, r.wo),
        ]
    ):
        copy = pltpu.make_async_copy(src, dst, r.local.at[at])
        copy.start()
        loads.append(copy)
    wide_u = Spread(r.every_u, r.s_wide_u)
    wide_d = Spread(r.every_d, r.s_wide_d)
    all_here = greet(wide_u)
    r.own_off[...] = jnp.full((8, HD), r.offset[0].astype(F32))
    r.pad_lat[...] = jnp.zeros_like(r.pad_lat)
    for k in range(2):
        row = r.pgrad[...].astype(F32)[k : k + 1, :]
        for c in range(PW):
            r.pg[k * PW + c : k * PW + c + 1, :] = row[:, c * CH : c * CH + CH]
    gain = r.gain[...].astype(F32).reshape(1, D)
    r.gain_row[...] = gain
    loads[0].wait()
    loads[1].wait()
    down = r.dn[...]
    both = dot(down, down, NT)
    high = both.astype(BF16)
    r.wd[:, :HD] = high
    r.wd[:, HD:] = (both - high.astype(F32)).astype(BF16)
    r.wu[...] = dot(down, r.up[...]).astype(BF16)
    scaled = (down.astype(F32) * gain).astype(BF16)
    all_here()

    lat = Fan("sx", r.lat, r.lat_in, r.s_lat)
    r.lat_in[sx] = r.lat[...]

    lat.arrived()
    for n in range(8):
        r.rows_lat[2 * n : 2 * n + 2, :] = r.lat_in[n].astype(F32)
    r.pad_lat[:, CH : CH + PW * CH] = r.rows_lat[...].astype(BF16)
    lats = Fan("sy", r.pad_lat, r.lat_all, r.s_lats)
    r.lat_all[sy] = r.pad_lat[...]
    offs = Fan("sy", r.own_off, r.offs, r.s_off)
    r.offs[sy] = r.own_off[...]
    text = Fan("sx", r.text, r.text_in, r.s_text)
    tgrad = Fan("sx", r.tgrad, r.tgrad_in, r.s_tgrad)
    r.text_in[sx] = r.text[...]
    r.tgrad_in[sx] = r.tgrad[...]

    for n, weight in enumerate([r.wq, r.wk, r.wv]):
        loads[2 + n].wait()
        r.mix[:, n * HD : (n + 1) * HD] = dot(scaled, weight[:, mine]).astype(BF16)
    loads[5].wait()
    r.nt[...] = dot(r.up[...], r.wo[mine, :], (((0,), (1,)), ((), ()))).astype(BF16)

    lats.arrived()
    down_block(r)

    text.arrived()
    tgrad.arrived()
    for n in range(8):
        r.rows_text[4 * n : 4 * n + 4, :] = r.text_in[n].astype(F32)
        r.rows_grad[4 * n : 4 * n + 4, :] = r.tgrad_in[n].astype(F32)
    wide = r.rows_text[...]
    inverse = lax.rsqrt(jnp.mean(wide * wide, axis=1, keepdims=True) + EPS)
    normed = (wide * inverse * gain).astype(BF16)
    token = lax.broadcasted_iota(jnp.int32, (TXT, HD), 0).astype(F32)
    shift = jnp.where(token >= r.own_off[:1, :], float(IMG), 0.0)
    cosine, sine = trig((TXT, HD), token + shift + (sy * SB).astype(F32))
    query = dot(normed, r.wq[...])
    key = dot(normed, r.wk[...])
    value = dot(normed, r.wv[...])
    outer = dot(r.rows_grad[...].astype(BF16), r.wo[...], NT)
    for h in range(4):
        at = slice(h * HD, (h + 1) * HD)
        r.kv_out[h, :, :HD] = turn(key[:, at], cosine, sine).astype(BF16)
        r.kv_out[h, :, HD:] = value[:, at].astype(BF16)
        turned = turn(query[:, at], cosine, sine)
        r.qd_out[h, :, :HD] = (turned * (SCALE * LOG2E)).astype(BF16)
        r.qd_out[h, :, HD:] = outer[:, at].astype(BF16)
    kvs = Fan("sy", r.kv_out, r.kv_in, r.s_kv, lambda ty, to: split_sy(ty)[1])
    qds = Fan("group", r.qd_out, r.qd_in, r.s_qd, lambda ty, to: to)
    r.kv_in[sy] = r.kv_out[head]
    r.qd_in[head] = r.qd_out[head]

    offs.arrived()
    masks(r, g, members)

    project(r, members)

    def text_ready():
        kvs.arrived()
        qds.arrived()
        kv = r.kv_in[...].reshape(512, 256)
        qd = r.qd_in[...].reshape(128, 256)
        r.kt[...] = kv[:, :HD]
        r.vtx[...] = kv[:, HD:]
        r.vtt[...] = kv[:, HD:].astype(F32).T.astype(BF16)
        r.q[1024:, :] = qd[:, :HD]
        r.do[1024:, :] = qd[:, HD:]

    def add_part(m):
        r.reorder[...] = dot(r.att[m * IMG : (m + 1) * IMG, :], r.nt[...], NT) + dot(
            r.da_own[m * IMG : (m + 1) * IMG, :], r.wu[...]
        ) * (1.0 / 32.0)
        for n in range(8):
            for k in range(2):
                r.part[8 * m + n, k * PW : (k + 1) * PW, :] = r.reorder[
                    pl.ds(2 * n + k, PW, stride=PH), :
                ].astype(BF16)

    attend_images(r, 1, 7 - g, text_ready)
    add_part(2)
    add_part(3)
    attend_images(r, 0, g, lambda: None)
    add_part(0)
    add_part(1)

    e, _ = ring("team")
    parts = Fan("team", r.part, r.part_in, r.s_part, lambda ty, to: to)
    r.part_in[e] = r.part[e]
    attend_text(r, 8 - g, None)
    for m in range(4):
        r.att_txt[m] = r.att[1024 + m * TXT : 1024 + (m + 1) * TXT, :]
    atx = Fan("group", r.att_txt, r.atx, r.s_atx, lambda ty, to: to)
    r.atx[head] = r.att_txt[head]
    r.dk[...] = jnp.zeros_like(r.dk)
    r.dv[...] = jnp.zeros_like(r.dv)
    parts.arrived()
    pre = jnp.sum(r.part_in[...].astype(F32), axis=0)
    sig = sigmoid(pre)
    act = (pre * sig).astype(BF16)
    slope = sig * (1.0 + pre * (1.0 - sig))
    pgrad = r.pg[...].astype(BF16)
    r.gown[...] = (dot(pgrad, r.w_uo[...]) * slope).astype(BF16)
    ups = Fan("team", r.gown, r.gall, r.s_up)
    r.gall[e] = r.gown[...]
    pred = dot(act, r.w_uo[...], NT)
    for k in range(2):
        for c in range(PW):
            r.pred_rows[k : k + 1, c * CH : c * CH + CH] = pred[k * PW + c : k * PW + c + 1, :]
    r.pred[...] = r.pred_rows[...].astype(BF16)
    r.gup[...] = dot(pgrad, act, TN)
    for p, diagonal in ((0, g), (1, 7 - g)):
        lse = r.lse[p, :1, :]

        @pl.loop(0, diagonal + 1)
        def _(j):
            normalise(r.e_img.at[4 * p + j], r.m_img.at[4 * p + j], lse)

        normalise(r.e_txt.at[p], r.m_txt.at[p], lse)

    @pl.loop(0, 8 - g)
    def _(j):
        normalise(r.e_q.at[j], r.m_q.at[j], r.lse[2, :1, :HD])

    backward_text(r, 8 - g)

    atx.arrived()
    joined = jnp.concatenate([r.atx[h] for h in range(4)], axis=1)

    @pl.loop(0, 8)
    def _(c):
        at = pl.ds(pl.multiple_of(c * 512, 512), 512)
        out = dot(joined, r.wo[:, at])
        for n in range(8):
            r.mixed[n, :, at] = out[4 * n : 4 * n + 4, :].astype(BF16)

    mixes = Fan("sx", r.mixed, r.mixed_in, r.s_mix, lambda ty, to: to)
    r.mixed_in[sx] = r.mixed[sx]

    ups.arrived()
    for m in range(4):
        for n in range(8):
            nat = r.gall[8 * m + n].astype(F32)
            for k in range(2):
                r.order[pl.ds(m * IMG + 2 * n + k, PW, stride=PH), :] = nat[
                    k * PW : (k + 1) * PW, :
                ]
    r.gpu[...] = r.order[...].astype(BF16)
    r.do[:1024, :] = dot(r.gpu[...], r.nt[...]).astype(BF16)

    gpu = r.gpu[...]
    grad = dot(gpu, r.wu[...], NT) * (1.0 / 32.0)
    for m in range(4):
        r.ex[m] = grad[m * IMG : (m + 1) * IMG, :]
    own = r.da_own[...]
    r.small_u[:, :HD] = dot(gpu, r.att[:1024, :], TN)
    r.small_u[:, HD : 2 * HD] = dot(gpu, own, TN) * (1.0 / 32.0)
    r.small_u[:, 2 * HD :] = dot(own, gpu, TN) * (1.0 / 32.0)
    for n in range(4):
        r.low_u[n] = r.small_u[32 * n : 32 * n + 32, :].astype(BF16)
    heads_u = Fan("head", r.low_u, r.low_u_in, r.s_hu, lambda ty, to: to)
    r.low_u_in[g] = r.low_u[g]

    backward_images(r, 0, g, members)

    heads_u.arrived()
    low_u = jnp.sum(r.low_u_in[...].astype(F32), axis=0).astype(BF16)

    @pl.loop(0, 8)
    def _(c):
        at = pl.ds(pl.multiple_of(c * 512, 512), 512)
        grad = dot(low_u[:, :HD], r.wo[mine, at]) + dot(low_u[:, HD : 2 * HD], r.dn[:, at])
        for k in range(4):
            r.wide_u[4 * c + k] = grad[:, k * HD : (k + 1) * HD].astype(BF16)

    sums_u = Fan("team", r.wide_u, r.wide_u_in, r.s_su, lambda ty, to: to)
    r.wide_u_in[e] = r.wide_u[e]

    backward_images(r, 1, 7 - g, members)

    sums_u.arrived()
    wide_u.plane(jnp.sum(r.wide_u_in[...].astype(F32), axis=0).astype(BF16))
    image_grads(r, g)

    for n in range(4):
        r.low_d[n] = r.small[32 * n : 32 * n + 32, :].astype(BF16)
    heads_d = Fan("head", r.low_d, r.low_d_in, r.s_hd, lambda ty, to: to)
    r.low_d_in[g] = r.low_d[g]
    conv_grad(r)
    convs = Fan("head", r.conv, r.conv_in, r.s_c1, lambda ty, to: to)
    r.conv_in[g] = r.conv[g]
    heads_d.arrived()
    low = jnp.sum(r.low_d_in[...].astype(F32), axis=0).astype(BF16)

    @pl.loop(0, 8)
    def _(c):
        at = pl.ds(pl.multiple_of(c * 512, 512), 512)
        grad = dot(low[:, :HD], r.wq[at, mine], NT)
        grad = grad + dot(low[:, HD : 2 * HD], r.wk[at, mine], NT)
        grad = grad + dot(low[:, 2 * HD : 3 * HD], r.wv[at, mine], NT)
        grad = grad * r.gain_row[:, at]
        grad = grad + dot(low_u[:, 2 * HD :], r.up[at, :], NT)
        grad = grad - dot(low[:, 3 * HD :], r.dn[:, at])
        for k in range(4):
            r.wide_d[4 * c + k] = grad[:, k * HD : (k + 1) * HD].astype(BF16)

    sums_d = Fan("team", r.wide_d, r.wide_d_in, r.s_sd, lambda ty, to: to)
    r.wide_d_in[e] = r.wide_d[e]
    wide_u.slabs()
    convs.arrived()
    r.conv_a[...] = jnp.sum(r.conv_in[...].astype(F32), axis=0).astype(BF16)
    beside = Fan("sx", r.conv_a, r.conv_sx, r.s_c2)
    r.conv_sx[sx] = r.conv_a[...]
    mixes.arrived()
    total = r.text[...].astype(F32)
    for n in range(8):
        total = total + r.mixed_in[n].astype(F32)
    r.text_out[...] = total.astype(BF16)
    sums_d.arrived()
    wide_d.plane(jnp.sum(r.wide_d_in[...].astype(F32), axis=0).astype(BF16))
    beside.arrived()
    r.conv_b[...] = jnp.sum(r.conv_sx[...].astype(F32), axis=0).astype(BF16)
    along = Fan("group", r.conv_b, r.conv_gr, r.s_c3)
    r.conv_gr[head] = r.conv_b[...]
    wide_u.pass_on()
    wide_d.slabs()
    along.arrived()
    r.conv_c[...] = jnp.sum(r.conv_gr[...].astype(F32), axis=0).astype(BF16)
    across = Fan("head", r.conv_c, r.conv_all, r.s_c4)
    r.conv_all[g] = r.conv_c[...]
    wide_u.arrived()
    lay_up(r)
    wide_d.pass_on()
    across.arrived()
    for n in range(3):
        r.grad_conv[80 * n : 80 * n + 80, :] = r.conv_all[n].astype(F32)
    rest = r.conv_all[3].astype(F32)
    r.grad_conv[240:, :] = rest[:48, :]
    r.grad_out[...] = rest[48:, :]
    wide_d.arrived()
    lay_down(r)
    for fan in (
        lat,
        offs,
        text,
        tgrad,
        lats,
        kvs,
        qds,
        parts,
        atx,
        ups,
        heads_u,
        sums_u,
        mixes,
        heads_d,
        convs,
        sums_d,
        beside,
        along,
        across,
    ):
        fan.sent()
    wide_u.sent()
    wide_d.sent()


def whole(inputs, cid):
    sds = jax.ShapeDtypeStruct
    dma = pltpu.SemaphoreType.DMA
    space = pltpu.VMEM
    outs = {
        "pred": ((2, PW * CH), BF16),
        "text_out": ((4, D), BF16),
        "grad_down": ((HD, D), BF16),
        "grad_up": ((D, HD), BF16),
        "grad_conv": ((288, HD), F32),
        "grad_out": ((CH, HD), F32),
    }
    scratch = {
        "conv_all": ((4, 80, HD), BF16),
        "gain_row": ((1, D), F32),
        "pg": ((32, CH), F32),
        "pred_rows": ((2, PW * CH), F32),
        "every_u": ((2, 64, 32, HD), BF16),
        "every_d": ((2, 64, 32, HD), BF16),
        "dn": ((HD, D), BF16),
        "up": ((D, HD), BF16),
        "wq": ((D, 512), BF16),
        "wk": ((D, 512), BF16),
        "wv": ((D, 512), BF16),
        "wo": ((512, D), BF16),
        "lat_in": ((8, 2, PW * CH), BF16),
        "text_in": ((8, 4, D), BF16),
        "tgrad_in": ((8, 4, D), BF16),
        "own_off": ((8, HD), F32),
        "offs": ((16, 8, HD), F32),
        "pad_lat": ((PH, 640), BF16),
        "rows_lat": ((PH, PW * CH), F32),
        "lat_all": ((16, PH, 640), BF16),
        "rows_text": ((TXT, D), F32),
        "rows_grad": ((TXT, D), F32),
        "wd": ((HD, 256), BF16),
        "wu": ((HD, HD), BF16),
        "mix": ((HD, 384), BF16),
        "nt": ((HD, HD), BF16),
        "kv_out": ((4, TXT, 256), BF16),
        "qd_out": ((4, TXT, 256), BF16),
        "kv_in": ((16, TXT, 256), BF16),
        "qd_in": ((4, TXT, 256), BF16),
        "phase": ((2, 16, HD), F32),
        "bias_tt": ((512, 128), F32),
        "bias_ti": ((512, HD), F32),
        "vis": ((8, HD), F32),
        "wpad": ((384, HD), F32),
        "wide": ((3, 256, 640), F32),
        "patches": ((16, 256, 384), BF16),
        "da": ((16, 256, HD), BF16),
        "sp": ((16, 256, HD), BF16),
        "da_own": ((1024, HD), BF16),
        "k": ((4096, HD), BF16),
        "v": ((4096, HD), BF16),
        "vt": ((HD, 4096), BF16),
        "q": ((1152, HD), BF16),
        "kt": ((512, HD), BF16),
        "vtx": ((512, HD), BF16),
        "vtt": ((HD, 512), BF16),
        "e_img": ((12, 512, 512), BF16),
        "m_img": ((12, 8, 512), F32),
        "e_txt": ((2, 512, 512), BF16),
        "m_txt": ((2, 8, 512), F32),
        "e_q": ((9, 512, 128), BF16),
        "m_q": ((9, 8, 128), F32),
        "lse": ((3, 8, 512), F32),
        "att": ((1152, HD), BF16),
        "reorder": ((IMG, HD), F32),
        "part": ((32, 32, HD), BF16),
        "part_in": ((32, 32, HD), BF16),
        "att_txt": ((4, TXT, HD), BF16),
        "atx": ((4, TXT, HD), BF16),
        "gown": ((32, HD), BF16),
        "gall": ((32, 32, HD), BF16),
        "gup": ((CH, HD), F32),
        "order": ((1024, HD), F32),
        "gpu": ((1024, HD), BF16),
        "do": ((1152, HD), BF16),
        "dk": ((4096, HD), F32),
        "dv": ((4096, HD), F32),
        "dq": ((4, IMG, HD), F32),
        "dqs": ((512, HD), F32),
        "ex": ((4, IMG, HD), F32),
        "dpre": ((16, IMG, HD), BF16),
        "grads": ((1024, 384), BF16),
        "small_u": ((HD, 384), F32),
        "low_u": ((4, 32, 384), BF16),
        "low_u_in": ((4, 32, 384), BF16),
        "small": ((HD, 512), F32),
        "low_d": ((4, 32, 512), BF16),
        "low_d_in": ((4, 32, 512), BF16),
        "wide_u": ((32, 32, HD), BF16),
        "wide_u_in": ((32, 32, HD), BF16),
        "wide_d": ((32, 32, HD), BF16),
        "wide_d_in": ((32, 32, HD), BF16),
        "mixed": ((8, 4, D), BF16),
        "mixed_in": ((8, 4, D), BF16),
        "conv": ((4, 80, HD), BF16),
        "conv_in": ((4, 80, HD), BF16),
        "conv_a": ((80, HD), BF16),
        "conv_sx": ((8, 80, HD), BF16),
        "conv_b": ((80, HD), BF16),
        "conv_gr": ((4, 80, HD), BF16),
        "conv_c": ((80, HD), BF16),
    }
    sems = {"local": (6,), "s_wide_u": (2, 8), "s_wide_d": (2, 8)}
    for name in (
        ("lat", "off", "text", "tgrad", "lats", "kv", "qd", "part", "atx", "up", "hu", "su")
        + ("mix", "hd", "sd", "c1", "c2", "c3", "c4")
    ):
        sems["s_" + name] = (2,)
    names = list(inputs) + list(outs) + list(scratch) + list(sems)
    hbm = {"w_down", "w_up", "w_query", "w_key", "w_value", "w_out"}
    specs = []
    for name in inputs:
        kind = pl.ANY if name in hbm else pltpu.SMEM if name == "offset" else pltpu.VMEM
        specs.append(pl.BlockSpec(memory_space=kind))
    return pl.pallas_call(
        functools.partial(whole_kernel, names),
        out_shape=[sds(*v) for v in outs.values()],
        in_specs=specs,
        out_specs=vmem(len(outs)),
        scratch_shapes=[space(*v) for v in scratch.values()] + [dma(v) for v in sems.values()],
        compiler_params=pltpu.CompilerParams(
            collective_id=cid, has_side_effects=True, vmem_limit_bytes=61 * 2**20
        ),
    )(*inputs.values())


def results_kernel(pred, text, down, up, conv, out, *results):
    for src, dst in zip((pred, text), results[:2]):
        dst[0] = src[...]
    for src, dst in zip((down, up, conv), results[2:5]):
        dst[...] = src[...].astype(F32)
    results[5][...] = out[...]


def results(*arrays):
    sds = jax.ShapeDtypeStruct
    shapes = [
        sds((1, 2, PW * CH), BF16),
        sds((1, 4, D), BF16),
        sds((HD, D), F32),
        sds((D, HD), F32),
        sds((288, HD), F32),
        sds((CH, HD), F32),
    ]
    return pl.pallas_call(
        results_kernel,
        out_shape=shapes,
        in_specs=vmem(6),
        out_specs=vmem(6),
        compiler_params=pltpu.CompilerParams(vmem_limit_bytes=32 * 2**20),
    )(*arrays)


def rope_base():
    half = HD // 2
    freq = np.exp(-(2.0 * np.arange(half) / HD) * math.log(ROPE_BASE))
    slot = np.arange(IMG)
    position = (slot % PH) * PW + slot // PH
    angle = position[:, None] * freq[None, :]
    cosine = np.concatenate([np.cos(angle), np.cos(angle)], axis=1)
    sine = np.concatenate([-np.sin(angle), np.sin(angle)], axis=1)
    return jnp.asarray(np.stack([cosine, sine]).astype(np.float32))


def shards(
    text_tokens,
    latent,
    image_offset,
    norm_gain,
    w_query,
    w_key,
    w_value,
    w_out,
    w_down_conv,
    w_down_proj,
    w_up_proj,
    w_up_out,
    pred_grad,
    text_grad,
):
    pred, text_out, grad_down_proj, grad_up_proj, grad_conv, grad_out = whole(
        {
            "offset": image_offset,
            "text": text_tokens[0],
            "tgrad": text_grad[0],
            "lat": latent[0],
            "gain": norm_gain,
            "pgrad": pred_grad[0],
            "wconv": w_down_conv,
            "w_uo": w_up_out.T,
            "base": rope_base(),
            "w_down": w_down_proj,
            "w_up": w_up_proj,
            "w_query": w_query,
            "w_key": w_key,
            "w_value": w_value,
            "w_out": w_out,
        },
        1,
    )
    pred, text_out, grad_down_proj, grad_up_proj, grad_conv, grad_out = results(
        pred, text_out, grad_down_proj, grad_up_proj, grad_conv, grad_out
    )
    return pred, text_out, grad_conv, grad_down_proj, grad_up_proj, grad_out.T


def solution(mesh):
    placed = (
        P("sy", "sx", None),
        P("sy", "sx", None),
        P("sy"),
        P(),
        P(None, "sx"),
        P(None, "sx"),
        P(None, "sx"),
        P("sx", None),
        P(),
        P(),
        P(),
        P(),
        P("sy", "sx", None),
        P("sy", "sx", None),
    )
    return jax.shard_map(
        shards,
        mesh=mesh,
        in_specs=placed,
        out_specs=(P("sy", "sx", None), P("sy", "sx", None), P(), P(), P(), P()),
        check_vma=False,
    )
```

```python
import functools
import math
import types

import jax
import jax.numpy as jnp
import numpy as np
from jax import lax
from jax.experimental import pallas as pl
from jax.experimental.pallas import tpu as pltpu
from jax.sharding import PartitionSpec as P

MESH = pl.DeviceIdType.MESH
F32 = jnp.float32
BF16 = jnp.bfloat16
HD = 128
SB = 288
TXT = 32
IMG = 256
PH = 16
PW = 16
CH = 32
D = 4096
EPS = 1e-05
NEG = -1e30
LOG2E = math.log2(math.e)
SCALE = HD ** (-0.5)
ROPE_BASE = 500000.0
SIZES = {"sx": 8, "sy": 16, "group": 4, "head": 4, "team": 32}
NT = (((1,), (1,)), ((), ()))
TN = (((0,), (0,)), ((), ()))


def dot(a, b, dims=(((1,), (0,)), ((), ()))):
    return lax.dot_general(a, b, dims, preferred_element_type=F32)


def vmem(count):
    return [pl.BlockSpec(memory_space=pltpu.VMEM)] * count


def mod(a, n):
    return a % n if isinstance(a, int) else lax.rem(a, n)


def div(a, n):
    return a // n if isinstance(a, int) else lax.div(a, n)


def sy_of(g, i):
    if isinstance(i, int):
        return 2 * g + i if i < 2 else 12 - 2 * g + i
    return jnp.where(i < 2, 2 * g + i, 12 - 2 * g + i)


def split_sy(sy):
    low = sy < 8
    g = jnp.where(low, div(sy, 2), div(15 - sy, 2))
    i = mod(sy, 2) + jnp.where(low, 0, 2)
    return g, i


def ring(kind):
    sx = lax.axis_index("sx")
    sy = lax.axis_index("sy")
    g, i = split_sy(sy)
    if kind == "sx":
        return sx, lambda o: (mod(sx + o, 8), sy, mod(sx + o, 8))
    if kind == "sy":
        return sy, lambda o: (sx, mod(sy + o, 16), mod(sy + o, 16))
    if kind == "group":
        return i, lambda o: (sx, sy_of(g, mod(i + o, 4)), mod(i + o, 4))
    if kind == "head":
        return g, lambda o: (sx, sy_of(mod(g + o, 4), i), mod(g + o, 4))
    e = i * 8 + sx

    def peer(o):
        f = mod(e + o, 32)
        return mod(f, 8), sy_of(g, div(f, 8)), f

    return e, peer


def remote(src, dst, send, recv, to):
    copy = pltpu.make_async_remote_copy(
        src_ref=src,
        dst_ref=dst,
        send_sem=send,
        recv_sem=recv,
        device_id=to,
        device_id_type=MESH,
    )
    copy.start()
    return copy


class Fan:
    def __init__(self, kind, source, land, sems, slot_of=None):
        own, peer = ring(kind)
        self.land = land.at[pl.ds(0, SIZES[kind] - 1)]
        self.sems = sems

        @pl.loop(1, SIZES[kind])
        def _(o):
            tx, ty, to = peer(o)
            src = source if slot_of is None else source.at[slot_of(ty, to)]
            remote(src, land.at[own], sems.at[0], sems.at[1], (tx, ty))

    def arrived(self):
        pltpu.make_async_copy(self.land, self.land, self.sems.at[1]).wait()

    def sent(self):
        pltpu.make_async_copy(self.land, self.land, self.sems.at[0]).wait()


class Team:
    def __init__(self, source, land, sems):
        sy = lax.axis_index("sy")
        self.g, i = split_sy(sy)
        self.own = i * 8 + lax.axis_index("sx")
        self.source = source
        self.slots = land
        self.land = land.at[pl.ds(0, 31)]
        self.sems = sems

    def push(self, f):
        @pl.when(f != self.own)
        def _():
            to = (mod(f, 8), sy_of(self.g, div(f, 8)))
            remote(
                self.source.at[f], self.slots.at[self.own], self.sems.at[0], self.sems.at[1], to
            )

    def keep(self):
        self.slots[self.own] = self.source[self.own]

    arrived = Fan.arrived
    sent = Fan.sent


def sigmoid(v):
    return 1.0 / (1.0 + jnp.exp(-v))


def turn(v, cosine, sine):
    return v * cosine + pltpu.roll(v, 64, 1) * sine


def trig(shape, position):
    lane = lax.broadcasted_iota(jnp.int32, shape, 1)
    step = (lane % 64).astype(F32)
    angle = position * jnp.exp(step * (-2.0 / HD * math.log(ROPE_BASE)))
    sine = jnp.sin(angle)
    return jnp.cos(angle), jnp.where(lane < 64, -sine, sine)


def tables(j, phase_ref, base_ref):
    pc = phase_ref[0, pl.ds(j, 1), :]
    ps = phase_ref[1, pl.ds(j, 1), :]
    bc = base_ref[0]
    bs = base_ref[1]
    return pc * bc - ps * bs, ps * bc + pc * bs


def row_sum(v):
    return dot(v.astype(BF16), jnp.ones((HD, HD), BF16))


def row_scale(da, wd):
    both = dot(da, wd)
    dawd = both[:, :HD] + both[:, HD:]
    return dawd, lax.rsqrt(row_sum(dawd * da.astype(F32)) * (1.0 / D) + EPS)


def lanes(column):
    return column.T[:1, :]


def place(x, y, z, core):
    return 2 * x + mod(z, 2), 4 * y + 2 * div(z, 2) + core


class Spread:
    def __init__(self, every, sems):
        self.every = every
        self.sems = sems
        sx = lax.axis_index("sx")
        sy = lax.axis_index("sy")
        self.core = mod(sy, 2)
        x = div(sx, 2)
        y = div(sy, 4)
        z = 2 * mod(div(sy, 2), 2) + mod(sx, 2)
        self.even = self.core == 0
        self.p1 = jnp.where(self.even, x, z)
        self.p2 = jnp.where(self.even, y, x)
        self.p3 = jnp.where(self.even, z, y)
        self.twin = place(x, y, z, 1 - self.core)
        self.here = every.at[self.core]
        self.spot = (self.p3 * 4 + self.p2) * 4 + self.p1
        self.live = []

    def chip(self, a, b, c):
        a = mod(a, 4)
        b = mod(b, 4)
        c = mod(c, 4)
        even = self.even
        return place(
            jnp.where(even, a, b), jnp.where(even, b, c), jnp.where(even, c, a), self.core
        )

    def send(self, ref, n, to):
        copy = remote(ref, ref, self.sems.at[0, n], self.sems.at[1, n], to)
        self.live.append(copy)
        return copy

    def slab(self, p):
        return self.here.at[pl.ds(mod(p, 4) * 16, 16)]

    def plane(self, block):
        self.every[self.core, self.spot] = block
        mine = self.here.at[self.spot]

        @pl.loop(1, 16)
        def _(o):
            to = self.chip(self.p1 + mod(o, 4), self.p2 + div(o, 4), self.p3)
            remote(mine, mine, self.sems.at[0, 0], self.sems.at[1, 0], to)

    def slabs(self):
        plane = self.here.at[pl.ds(0, 15)]
        pltpu.make_async_copy(plane, plane, self.sems.at[1, 0]).wait()
        own = self.slab(self.p3)
        self.wave = [self.send(own, o, self.chip(self.p1, self.p2, self.p3 + o)) for o in (1, 3, 2)]
        self.twins = [self.send(own, 4, self.twin)]

    def pass_on(self):
        for o, copy in zip((1, 3, 2), self.wave):
            copy.wait_recv()
            self.twins.append(self.send(self.slab(self.p3 + 4 - o), 4 + o, self.twin))

    def arrived(self):
        for copy in self.twins:
            copy.wait_recv()

    def sent(self):
        plane = self.here.at[pl.ds(0, 15)]
        pltpu.make_async_copy(plane, plane, self.sems.at[0, 0]).wait()
        for copy in self.live:
            copy.wait_send()


def greet(wide):
    barrier = pltpu.get_barrier_semaphore()
    for kind in ("team", "sy"):
        _, peer = ring(kind)

        @pl.loop(1, SIZES[kind])
        def _(o):
            tx, ty, _ = peer(o)
            pl.semaphore_signal(barrier, inc=1, device_id=(tx, ty), device_id_type=MESH)

    @pl.loop(1, 16)
    def _(o):
        to = wide.chip(wide.p1 + mod(o, 4), wide.p2 + div(o, 4), wide.p3)
        pl.semaphore_signal(barrier, inc=1, device_id=to, device_id_type=MESH)

    @pl.loop(1, 4)
    def _(o):
        to = wide.chip(wide.p1, wide.p2, wide.p3 + o)
        pl.semaphore_signal(barrier, inc=1, device_id=to, device_id_type=MESH)

    return lambda: pl.semaphore_wait(barrier, 31 + 15 + 15 + 3)


def masks(r, g, members):
    block = lax.broadcasted_iota(jnp.int32, (16, HD), 0).astype(F32)
    cosine, sine = trig((16, HD), block * float(SB) + jnp.max(r.offs[...], axis=1))
    r.phase[0] = cosine
    r.phase[1] = sine
    starts = [r.offs[b][:1, :] for b in members]
    row = lax.broadcasted_iota(jnp.int32, (512, TXT), 0)
    query = lax.broadcasted_iota(jnp.int32, (512, TXT), 1)
    for m in range(4):
        b = members[m]
        seen = (row // TXT < b) | ((row // TXT == b) & (row % TXT <= query))
        r.bias_tt[:, m * TXT : (m + 1) * TXT] = jnp.where(seen, 0.0, NEG)
    lane = lax.broadcasted_iota(jnp.int32, (8, HD), 1)
    start = starts[0]
    owner = jnp.full((8, HD), members[0], jnp.int32)
    for m in range(1, 4):
        start = jnp.where(lane // TXT == m, starts[m], start)
        owner = jnp.where(lane // TXT == m, members[m], owner)
    late = jnp.where((lane % TXT).astype(F32) >= start, 1.0, 0.0)
    r.vis[...] = late + owner.astype(F32)
    lane = lax.broadcasted_iota(jnp.int32, (512, HD), 1)
    row = lax.broadcasted_iota(jnp.int32, (512, HD), 0)
    start = jnp.broadcast_to(starts[0], (512, HD))
    owner = jnp.full((512, HD), members[0], jnp.int32)
    for m in range(1, 4):
        start = jnp.where(lane == m, starts[m], start)
        owner = jnp.where(lane == m, members[m], owner)
    seen = (row // TXT < owner) | ((row // TXT == owner) & ((row % TXT).astype(F32) < start))
    r.bias_ti[...] = jnp.where(seen, 0.0, NEG)


def down_block(r):
    r.wpad[...] = jnp.zeros_like(r.wpad)
    for tap in range(3):
        r.wpad[tap * 128 : tap * 128 + 96, :] = r.wconv[tap * 96 : tap * 96 + 96, :].astype(F32)
    mid = r.lat_all[...].reshape(256, PW * CH).astype(F32)
    mid = pltpu.roll(jnp.concatenate([mid, jnp.zeros((256, HD), F32)], axis=1), CH, 1)
    row = lax.broadcasted_iota(jnp.int32, mid.shape, 0) % PH
    r.wide[0] = jnp.where(row == 0, 0.0, pltpu.roll(mid, 1, 0))
    r.wide[1] = mid
    r.wide[2] = jnp.where(row == PH - 1, 0.0, pltpu.roll(mid, 16 * PH - 1, 0))
    weight = r.wpad[...].astype(BF16)
    for c in range(PW):
        for tap in range(3):
            r.patches[c, :, tap * 128 : tap * 128 + 128] = r.wide[
                tap, :, c * CH : c * CH + 128
            ].astype(BF16)
        pre = dot(r.patches[c], weight)
        sig = sigmoid(pre)
        r.da[:, c * PH : c * PH + PH, :] = (pre * sig).astype(BF16).reshape(16, PH, HD)
        r.sp[:, c * PH : c * PH + PH, :] = (
            (sig * (1.0 + pre * (1.0 - sig))).astype(BF16).reshape(16, PH, HD)
        )


def project(r, members):
    mix_kv = r.mix[:, HD:]
    mix_q = r.mix[:, :HD]
    wd = r.wd[...]

    @pl.loop(0, 4)
    def _(n):
        da = r.da[pl.ds(4 * n, 4)].reshape(4 * IMG, HD)
        _, inv = row_scale(da, wd)
        scaled = (da.astype(F32) * inv).astype(BF16)
        kv = dot(scaled, mix_kv)
        whole = pl.ds(pl.multiple_of(n * 1024, 1024), 1024)
        r.vt[:, whole] = dot(mix_kv[:, HD:], scaled, (((0,), (1,)), ((), ()))).astype(BF16)
        for m in range(4):
            j = 4 * n + m
            cosine, sine = tables(j, r.phase, r.base)
            rows = pl.ds(pl.multiple_of(j * IMG, IMG), IMG)
            part = kv[m * IMG : (m + 1) * IMG, :]
            r.k[rows, :] = turn(part[:, :HD], cosine, sine).astype(BF16)
            r.v[rows, :] = part[:, HD:].astype(BF16)

    for m in range(4):
        r.da_own[m * IMG : (m + 1) * IMG, :] = r.da[members[m]]
    da = r.da_own[...]
    _, inv = row_scale(da, wd)
    queries = dot((da.astype(F32) * inv).astype(BF16), mix_q) * (SCALE * LOG2E)
    for m in range(4):
        rows = slice(m * IMG, (m + 1) * IMG)
        cosine, sine = tables(members[m], r.phase, r.base)
        r.q[rows, :] = turn(queries[rows, :], cosine, sine).astype(BF16)


def tile_rows(j):
    return pl.ds(pl.multiple_of(j * 512, 512), 512)


def absorb(state, scores, vt, e_ref, m_ref):
    top = jnp.max(scores, axis=0, keepdims=True)
    new = top if state is None else jnp.maximum(state[0], top)
    raised = jnp.exp2(scores - new)
    low = raised.astype(BF16)
    e_ref[...] = low
    m_ref[...] = jnp.broadcast_to(new, m_ref.shape)
    total = jnp.sum(raised, axis=0, keepdims=True)
    mixed = dot(vt, low)
    if state is None:
        return new, total, mixed
    old = jnp.exp2(state[0] - new)
    return new, state[1] * old + total, state[2] * old + mixed


def conclude(r, p, width, state):
    peak, total, acc = state
    r.att[p * 512 : p * 512 + width, :] = (acc / total).T.astype(BF16)
    r.lse[p, :, :width] = jnp.broadcast_to(peak + jnp.log2(total), (8, width))


def diagonal_mask(scores):
    bottom = lax.broadcasted_iota(jnp.int32, scores.shape, 0) >= IMG
    left = lax.broadcasted_iota(jnp.int32, scores.shape, 1) < IMG
    return jnp.where(bottom & left, NEG, scores)


def attend_images(r, p, diagonal, text_ready):
    q = r.q[p * 512 : p * 512 + 512, :]
    base = 4 * p

    def tile(j):
        return dot(r.k[tile_rows(j), :], q, NT)

    state = absorb(
        None,
        diagonal_mask(tile(diagonal)),
        r.vt[:, tile_rows(diagonal)],
        r.e_img.at[base + diagonal],
        r.m_img.at[base + diagonal],
    )

    def body(j, state):
        return absorb(
            state, tile(j), r.vt[:, tile_rows(j)], r.e_img.at[base + j], r.m_img.at[base + j]
        )

    state = lax.fori_loop(0, diagonal, body, state)
    text_ready()
    scores = dot(r.kt[...], q, NT)
    bias = jnp.concatenate(
        [
            jnp.broadcast_to(r.bias_ti[:, 2 * p + half : 2 * p + half + 1], (512, IMG))
            for half in range(2)
        ],
        axis=1,
    )
    scores = jnp.where(bias < 0.0, NEG, scores)
    state = absorb(state, scores, r.vtt[...], r.e_txt.at[p], r.m_txt.at[p])
    conclude(r, p, 512, state)


def attend_text(r, count, kept):
    q = r.q[1024:, :]
    vis = r.vis[:1, :]
    scores = jnp.where(r.bias_tt[...] < 0.0, NEG, dot(r.kt[...], q, NT))
    state = absorb(None, scores, r.vtt[...], r.e_q.at[8], r.m_q.at[8])

    def body(j, state):
        scores = dot(r.k[tile_rows(j), :], q, NT)
        block = 2 * j + (lax.broadcasted_iota(jnp.int32, scores.shape, 0) >= IMG).astype(jnp.int32)
        scores = jnp.where(block.astype(F32) < vis, scores, NEG)
        return absorb(state, scores, r.vt[:, tile_rows(j)], r.e_q.at[j], r.m_q.at[j])

    conclude(r, 2, 128, lax.fori_loop(0, count, body, state))


def normalise(e_ref, m_ref, lse):
    factor = jnp.exp2(m_ref[:1, :] - lse)
    e_ref[...] = (e_ref[...].astype(F32) * factor).astype(BF16)


def backward_rows(r, p, width):
    rows = slice(p * 512, p * 512 + width)
    q = r.q[rows, :]
    do = r.do[rows, :]
    sums = jnp.sum(do.astype(F32) * r.att[rows, :].astype(F32), axis=1, keepdims=True)
    return q, do, lanes(jnp.broadcast_to(sums, (width, HD)))


def backward_images(r, p, diagonal, members):
    q, do, delta = backward_rows(r, p, 512)
    base = 4 * p

    probs = r.e_txt[p].astype(F32)
    grad = (probs * (dot(r.vtx[...], do, NT) - delta)).astype(BF16)
    r.dqs[...] = dot(grad, r.kt[...], TN)

    @pl.loop(0, diagonal + 1)
    def _(j):
        at = tile_rows(j)
        keys = r.k[at, :]
        probs = r.e_img[base + j]
        grad = (probs.astype(F32) * (dot(r.v[at, :], do, NT) - delta)).astype(BF16)
        r.dv[at, :] += dot(probs, do)
        r.dk[at, :] += dot(grad, q)
        r.dqs[...] += dot(grad, keys, TN)

    for half in range(2):
        r.dq[2 * p + half] = r.dqs[half * IMG : (half + 1) * IMG, :]


def backward_text(r, count):
    q, do, delta = backward_rows(r, 2, 128)

    @pl.loop(0, count)
    def _(j):
        at = tile_rows(j)
        probs = r.e_q[j]
        grad = (probs.astype(F32) * (dot(r.v[at, :], do, NT) - delta)).astype(BF16)
        r.dv[at, :] += dot(probs, do)
        r.dk[at, :] += dot(grad, q)


def image_grads(r, g):
    wd = r.wd[...]
    mix = r.mix[...]
    r.small[...] = jnp.zeros_like(r.small)

    @pl.loop(0, 4)
    def _(n):
        da = r.da[pl.ds(4 * n, 4)].reshape(4 * IMG, HD)
        da_wide = da.astype(F32)
        dawd, inv = row_scale(da, wd)
        extra = []
        for k in range(4):
            j = 4 * n + k
            group, m = split_sy(j)
            ours = (group == g).astype(F32)
            cosine, sine = tables(j, r.phase, r.base)
            at = pl.ds(pl.multiple_of(j * IMG, IMG), IMG)
            rows = slice(k * IMG, (k + 1) * IMG)
            gq = turn(r.dq[m] * (ours * SCALE), cosine, -sine)
            gk = turn(r.dk[at, :] * (1.0 / LOG2E), cosine, -sine)
            r.grads[rows, :HD] = gq.astype(BF16)
            r.grads[rows, HD : 2 * HD] = gk.astype(BF16)
            r.grads[rows, 2 * HD :] = r.dv[at, :].astype(BF16)
            extra.append(r.ex[m] * ours)
        grads = r.grads[...]
        back = dot(grads, mix, NT)
        cube = (inv * inv * inv) * (row_sum(back * da_wide) * (1.0 / D))
        slope = r.sp[pl.ds(4 * n, 4)].reshape(4 * IMG, HD).astype(F32)
        grad = (inv * back - cube * dawd + jnp.concatenate(extra, axis=0)) * slope
        r.dpre[pl.ds(4 * n, 4)] = grad.astype(BF16).reshape(4, IMG, HD)
        r.small[:, :384] += dot((da_wide * inv).astype(BF16), grads, TN)
        r.small[:, 384:] += dot((da_wide * cube).astype(BF16), da, TN)


def conv_grad(r):
    total = jnp.zeros((384, HD), F32)
    for c in range(PW):
        grad = r.dpre[:, c * PH : c * PH + PH, :].reshape(256, HD)
        total = total + dot(r.patches[c], grad, TN)
    rows = [total[tap * 128 : tap * 128 + 96, :] for tap in range(3)] + [r.gup[...]]
    whole = jnp.concatenate(rows, axis=0).astype(BF16)
    for n in range(4):
        r.conv[n] = whole[80 * n : 80 * n + 80, :]


def block_of(group, e):
    sx = e % 8
    sy = sy_of(group, e // 8)
    x = sx // 2
    y = sy // 4
    z = 2 * ((sy // 2) % 2) + sx % 2
    core = sy % 2
    return core, (z * 4 + y) * 4 + x if core == 0 else (y * 4 + x) * 4 + z


def lay_up(r):
    for e in range(32):
        cols = [r.every_u[block_of(group, e)].astype(F32) for group in range(4)]
        r.grad_up[e * HD : (e + 1) * HD, :] = jnp.concatenate(cols, axis=0).T.astype(BF16)


def lay_down(r):
    for e in range(32):
        for group in range(4):
            r.grad_down[32 * group : 32 * group + 32, e * HD : (e + 1) * HD] = r.every_d[
                block_of(group, e)
            ]


def whole_kernel(names, *refs):
    r = types.SimpleNamespace(**dict(zip(names, refs)))
    sx = lax.axis_index("sx")
    sy = lax.axis_index("sy")
    g, head = split_sy(sy)
    members = [sy_of(g, m) for m in range(4)]
    mine = pl.ds(pl.multiple_of(head * HD, HD), HD)
    loads = []
    for at, (src, dst) in enumerate(
        [
            (r.w_down, r.dn),
            (r.w_up, r.up),
            (r.w_query, r.wq),
            (r.w_key, r.wk),
            (r.w_value, r.wv),
            (r.w_out, r.wo),
        ]
    ):
        copy = pltpu.make_async_copy(src, dst, r.local.at[at])
        copy.start()
        loads.append(copy)
    wide_u = Spread(r.every_u, r.s_wide_u)
    wide_d = Spread(r.every_d, r.s_wide_d)
    all_here = greet(wide_u)
    r.own_off[...] = jnp.full((8, HD), r.offset[0].astype(F32))
    for k in range(2):
        row = r.pgrad[...].astype(F32)[k : k + 1, :]
        for c in range(PW):
            r.pg[k * PW + c : k * PW + c + 1, :] = row[:, c * CH : c * CH + CH]
    gain = r.gain[...].astype(F32).reshape(1, D)
    r.gain_row[...] = gain
    loads[0].wait()
    loads[1].wait()
    down = r.dn[...]
    both = dot(down, down, NT)
    high = both.astype(BF16)
    r.wd[:, :HD] = high
    r.wd[:, HD:] = (both - high.astype(F32)).astype(BF16)
    r.wu[...] = dot(down, r.up[...]).astype(BF16)
    scaled = (down.astype(F32) * gain).astype(BF16)
    all_here()

    lat = Fan("sx", r.lat, r.lat_in, r.s_lat)
    text = Fan("sx", r.text, r.text_in, r.s_text)
    r.lat_in[sx] = r.lat[...]
    r.text_in[sx] = r.text[...]

    lat.arrived()
    for n in range(8):
        r.rows_lat[2 * n : 2 * n + 2, :] = r.lat_in[n].astype(F32)
    r.row_lat[...] = r.rows_lat[...].astype(BF16)
    lats = Fan("sy", r.row_lat, r.lat_all, r.s_lats)
    r.lat_all[sy] = r.row_lat[...]
    offs = Fan("sy", r.own_off, r.offs, r.s_off)
    r.offs[sy] = r.own_off[...]

    for n, weight in enumerate([r.wq, r.wk, r.wv]):
        loads[2 + n].wait()
        r.mix[:, n * HD : (n + 1) * HD] = dot(scaled, weight[:, mine]).astype(BF16)
    loads[5].wait()
    r.nt[...] = dot(r.up[...], r.wo[mine, :], (((0,), (1,)), ((), ()))).astype(BF16)

    text.arrived()
    for n in range(8):
        r.rows_text[4 * n : 4 * n + 4, :] = r.text_in[n].astype(F32)
    wide = r.rows_text[...]
    inverse = lax.rsqrt(jnp.mean(wide * wide, axis=1, keepdims=True) + EPS)
    normed = (wide * inverse * gain).astype(BF16)
    token = lax.broadcasted_iota(jnp.int32, (TXT, HD), 0).astype(F32)
    shift = jnp.where(token >= r.own_off[:1, :], float(IMG), 0.0)
    cosine, sine = trig((TXT, HD), token + shift + (sy * SB).astype(F32))
    query = dot(normed, r.wq[...])
    key = dot(normed, r.wk[...])
    value = dot(normed, r.wv[...])
    for h in range(4):
        at = slice(h * HD, (h + 1) * HD)
        r.kv_out[h, :, :HD] = turn(key[:, at], cosine, sine).astype(BF16)
        r.kv_out[h, :, HD:] = value[:, at].astype(BF16)
        turned = turn(query[:, at], cosine, sine)
        r.qd_out[h] = (turned * (SCALE * LOG2E)).astype(BF16)
    kvs = Fan("sy", r.kv_out, r.kv_in, r.s_kv, lambda ty, to: split_sy(ty)[1])
    qds = Fan("group", r.qd_out, r.qd_in, r.s_qd, lambda ty, to: to)
    r.kv_in[sy] = r.kv_out[head]
    r.qd_in[head] = r.qd_out[head]

    offs.arrived()
    masks(r, g, members)

    lats.arrived()
    tgrad = Fan("sx", r.tgrad, r.tgrad_in, r.s_tgrad)
    r.tgrad_in[sx] = r.tgrad[...]
    down_block(r)

    project(r, members)

    def text_ready():
        kvs.arrived()
        qds.arrived()
        kv = r.kv_in[...].reshape(512, 256)
        r.kt[...] = kv[:, :HD]
        r.vtx[...] = kv[:, HD:]
        r.vtt[...] = kv[:, HD:].astype(F32).T.astype(BF16)
        r.q[1024:, :] = r.qd_in[...].reshape(128, HD)

    def add_part(m):
        r.reorder[...] = dot(r.att[m * IMG : (m + 1) * IMG, :], r.nt[...], NT) + dot(
            r.da_own[m * IMG : (m + 1) * IMG, :], r.wu[...]
        ) * (1.0 / 32.0)
        for n in range(8):
            for k in range(2):
                r.part[8 * m + n, k * PW : (k + 1) * PW, :] = r.reorder[
                    pl.ds(2 * n + k, PW, stride=PH), :
                ].astype(BF16)

    parts = Team(r.part, r.part_in, r.s_part)
    e = parts.own
    attend_images(r, 1, 7 - g, text_ready)
    add_part(2)
    add_part(3)

    @pl.loop(0, 16)
    def _(o):
        parts.push(16 + mod(e + o, 16))

    attend_images(r, 0, g, lambda: None)
    add_part(0)
    add_part(1)

    @pl.loop(0, 16)
    def _(o):
        parts.push(mod(e + o, 16))

    parts.keep()

    tgrad.arrived()
    for n in range(8):
        r.rows_grad[4 * n : 4 * n + 4, :] = r.tgrad_in[n].astype(F32)
    outer = dot(r.rows_grad[...].astype(BF16), r.wo[...], NT)
    for h in range(4):
        r.d_out[h] = outer[:, h * HD : (h + 1) * HD].astype(BF16)
    outers = Fan("group", r.d_out, r.d_in, r.s_do, lambda ty, to: to)
    r.d_in[head] = r.d_out[head]
    attend_text(r, 8 - g, None)
    for m in range(4):
        r.att_txt[m] = r.att[1024 + m * TXT : 1024 + (m + 1) * TXT, :]
    atx = Fan("group", r.att_txt, r.atx, r.s_atx, lambda ty, to: to)
    r.atx[head] = r.att_txt[head]
    r.dk[...] = jnp.zeros_like(r.dk)
    r.dv[...] = jnp.zeros_like(r.dv)
    parts.arrived()
    pre = jnp.sum(r.part_in[...].astype(F32), axis=0)
    sig = sigmoid(pre)
    act = (pre * sig).astype(BF16)
    slope = sig * (1.0 + pre * (1.0 - sig))
    pgrad = r.pg[...].astype(BF16)
    r.gown[...] = (dot(pgrad, r.w_uo[...]) * slope).astype(BF16)
    ups = Fan("team", r.gown, r.gall, r.s_up)
    r.gall[e] = r.gown[...]
    pred = dot(act, r.w_uo[...], NT)
    for k in range(2):
        for c in range(PW):
            r.pred_rows[k : k + 1, c * CH : c * CH + CH] = pred[k * PW + c : k * PW + c + 1, :]
    r.pred[...] = r.pred_rows[...].astype(BF16)
    r.gup[...] = dot(pgrad, act, TN)
    for p, diagonal in ((0, g), (1, 7 - g)):
        lse = r.lse[p, :1, :]

        @pl.loop(0, diagonal + 1)
        def _(j):
            normalise(r.e_img.at[4 * p + j], r.m_img.at[4 * p + j], lse)

        normalise(r.e_txt.at[p], r.m_txt.at[p], lse)

    @pl.loop(0, 8 - g)
    def _(j):
        normalise(r.e_q.at[j], r.m_q.at[j], r.lse[2, :1, :HD])

    outers.arrived()
    r.do[1024:, :] = r.d_in[...].reshape(128, HD)
    backward_text(r, 8 - g)

    atx.arrived()
    joined = jnp.concatenate([r.atx[h] for h in range(4)], axis=1)

    @pl.loop(0, 8)
    def _(c):
        at = pl.ds(pl.multiple_of(c * 512, 512), 512)
        out = dot(joined, r.wo[:, at])
        for n in range(8):
            r.mixed[n, :, at] = out[4 * n : 4 * n + 4, :].astype(BF16)

    mixes = Fan("sx", r.mixed, r.mixed_in, r.s_mix, lambda ty, to: to)
    r.mixed_in[sx] = r.mixed[sx]

    ups.arrived()
    for m in range(4):
        for n in range(8):
            nat = r.gall[8 * m + n].astype(F32)
            for k in range(2):
                r.order[pl.ds(m * IMG + 2 * n + k, PW, stride=PH), :] = nat[
                    k * PW : (k + 1) * PW, :
                ]
    r.gpu[...] = r.order[...].astype(BF16)
    r.do[:1024, :] = dot(r.gpu[...], r.nt[...]).astype(BF16)

    gpu = r.gpu[...]
    grad = dot(gpu, r.wu[...], NT) * (1.0 / 32.0)
    for m in range(4):
        r.ex[m] = grad[m * IMG : (m + 1) * IMG, :]
    own = r.da_own[...]
    r.small_u[:, :HD] = dot(gpu, r.att[:1024, :], TN)
    r.small_u[:, HD : 2 * HD] = dot(gpu, own, TN) * (1.0 / 32.0)
    r.small_u[:, 2 * HD :] = dot(own, gpu, TN) * (1.0 / 32.0)
    for n in range(4):
        r.low_u[n] = r.small_u[32 * n : 32 * n + 32, :].astype(BF16)
    heads_u = Fan("head", r.low_u, r.low_u_in, r.s_hu, lambda ty, to: to)
    r.low_u_in[g] = r.low_u[g]

    backward_images(r, 0, g, members)

    heads_u.arrived()
    low_u = jnp.sum(r.low_u_in[...].astype(F32), axis=0).astype(BF16)

    sums_u = Team(r.wide_u, r.wide_u_in, r.s_su)

    @pl.loop(0, 8)
    def _(n):
        c = mod(n + div(e, 4), 8)
        at = pl.ds(pl.multiple_of(c * 512, 512), 512)
        grad = dot(low_u[:, :HD], r.wo[mine, at]) + dot(low_u[:, HD : 2 * HD], r.dn[:, at])
        for k in range(4):
            r.wide_u[4 * c + k] = grad[:, k * HD : (k + 1) * HD].astype(BF16)
            sums_u.push(4 * c + k)

    sums_u.keep()

    backward_images(r, 1, 7 - g, members)

    sums_u.arrived()
    wide_u.plane(jnp.sum(r.wide_u_in[...].astype(F32), axis=0).astype(BF16))
    image_grads(r, g)

    for n in range(4):
        r.low_d[n] = r.small[32 * n : 32 * n + 32, :].astype(BF16)
    heads_d = Fan("head", r.low_d, r.low_d_in, r.s_hd, lambda ty, to: to)
    r.low_d_in[g] = r.low_d[g]
    conv_grad(r)
    convs = Fan("head", r.conv, r.conv_in, r.s_c1, lambda ty, to: to)
    r.conv_in[g] = r.conv[g]

    @pl.loop(0, 8)
    def _(c):
        at = pl.ds(pl.multiple_of(c * 512, 512), 512)
        r.base_d[:, at] = dot(low_u[:, 2 * HD :], r.up[at, :], NT)

    heads_d.arrived()
    low = jnp.sum(r.low_d_in[...].astype(F32), axis=0).astype(BF16)

    sums_d = Team(r.wide_d, r.wide_d_in, r.s_sd)

    @pl.loop(0, 8)
    def _(n):
        c = mod(n + div(e, 4), 8)
        at = pl.ds(pl.multiple_of(c * 512, 512), 512)
        grad = dot(low[:, :HD], r.wq[at, mine], NT)
        grad = grad + dot(low[:, HD : 2 * HD], r.wk[at, mine], NT)
        grad = grad + dot(low[:, 2 * HD : 3 * HD], r.wv[at, mine], NT)
        grad = grad * r.gain_row[:, at]
        grad = grad + r.base_d[:, at]
        grad = grad - dot(low[:, 3 * HD :], r.dn[:, at])
        for k in range(4):
            r.wide_d[4 * c + k] = grad[:, k * HD : (k + 1) * HD].astype(BF16)
            sums_d.push(4 * c + k)

    sums_d.keep()
    wide_u.slabs()
    convs.arrived()
    r.conv_a[...] = jnp.sum(r.conv_in[...].astype(F32), axis=0).astype(BF16)
    beside = Fan("sx", r.conv_a, r.conv_sx, r.s_c2)
    r.conv_sx[sx] = r.conv_a[...]
    mixes.arrived()
    total = r.text[...].astype(F32)
    for n in range(8):
        total = total + r.mixed_in[n].astype(F32)
    r.text_out[...] = total.astype(BF16)
    sums_d.arrived()
    wide_d.plane(jnp.sum(r.wide_d_in[...].astype(F32), axis=0).astype(BF16))
    beside.arrived()
    r.conv_b[...] = jnp.sum(r.conv_sx[...].astype(F32), axis=0).astype(BF16)
    along = Fan("group", r.conv_b, r.conv_gr, r.s_c3)
    r.conv_gr[head] = r.conv_b[...]
    wide_u.pass_on()
    wide_d.slabs()
    along.arrived()
    r.conv_c[...] = jnp.sum(r.conv_gr[...].astype(F32), axis=0).astype(BF16)
    across = Fan("head", r.conv_c, r.conv_all, r.s_c4)
    r.conv_all[g] = r.conv_c[...]
    wide_u.arrived()
    lay_up(r)
    wide_d.pass_on()
    across.arrived()
    for n in range(3):
        r.grad_conv[80 * n : 80 * n + 80, :] = r.conv_all[n].astype(F32)
    rest = r.conv_all[3].astype(F32)
    r.grad_conv[240:, :] = rest[:48, :]
    r.grad_out[...] = rest[48:, :]
    wide_d.arrived()
    lay_down(r)
    for fan in (
        lat,
        offs,
        text,
        tgrad,
        lats,
        kvs,
        qds,
        outers,
        parts,
        atx,
        ups,
        heads_u,
        sums_u,
        mixes,
        heads_d,
        convs,
        sums_d,
        beside,
        along,
        across,
    ):
        fan.sent()
    wide_u.sent()
    wide_d.sent()


def whole(inputs, cid):
    sds = jax.ShapeDtypeStruct
    dma = pltpu.SemaphoreType.DMA
    space = pltpu.VMEM
    outs = {
        "pred": ((2, PW * CH), BF16),
        "text_out": ((4, D), BF16),
        "grad_down": ((HD, D), BF16),
        "grad_up": ((D, HD), BF16),
        "grad_conv": ((288, HD), F32),
        "grad_out": ((CH, HD), F32),
    }
    scratch = {
        "conv_all": ((4, 80, HD), BF16),
        "gain_row": ((1, D), F32),
        "pg": ((32, CH), F32),
        "pred_rows": ((2, PW * CH), F32),
        "every_u": ((2, 64, 32, HD), BF16),
        "every_d": ((2, 64, 32, HD), BF16),
        "dn": ((HD, D), BF16),
        "up": ((D, HD), BF16),
        "wq": ((D, 512), BF16),
        "wk": ((D, 512), BF16),
        "wv": ((D, 512), BF16),
        "wo": ((512, D), BF16),
        "lat_in": ((8, 2, PW * CH), BF16),
        "text_in": ((8, 4, D), BF16),
        "tgrad_in": ((8, 4, D), BF16),
        "own_off": ((8, HD), F32),
        "offs": ((16, 8, HD), F32),
        "row_lat": ((PH, PW * CH), BF16),
        "rows_lat": ((PH, PW * CH), F32),
        "lat_all": ((16, PH, PW * CH), BF16),
        "rows_text": ((TXT, D), F32),
        "rows_grad": ((TXT, D), F32),
        "wd": ((HD, 256), BF16),
        "wu": ((HD, HD), BF16),
        "mix": ((HD, 384), BF16),
        "nt": ((HD, HD), BF16),
        "kv_out": ((4, TXT, 256), BF16),
        "qd_out": ((4, TXT, HD), BF16),
        "kv_in": ((16, TXT, 256), BF16),
        "qd_in": ((4, TXT, HD), BF16),
        "d_out": ((4, TXT, HD), BF16),
        "d_in": ((4, TXT, HD), BF16),
        "phase": ((2, 16, HD), F32),
        "bias_tt": ((512, 128), F32),
        "bias_ti": ((512, HD), F32),
        "vis": ((8, HD), F32),
        "wpad": ((384, HD), F32),
        "wide": ((3, 256, 640), F32),
        "patches": ((16, 256, 384), BF16),
        "da": ((16, 256, HD), BF16),
        "sp": ((16, 256, HD), BF16),
        "da_own": ((1024, HD), BF16),
        "k": ((4096, HD), BF16),
        "v": ((4096, HD), BF16),
        "vt": ((HD, 4096), BF16),
        "q": ((1152, HD), BF16),
        "kt": ((512, HD), BF16),
        "vtx": ((512, HD), BF16),
        "vtt": ((HD, 512), BF16),
        "e_img": ((12, 512, 512), BF16),
        "m_img": ((12, 8, 512), F32),
        "e_txt": ((2, 512, 512), BF16),
        "m_txt": ((2, 8, 512), F32),
        "e_q": ((9, 512, 128), BF16),
        "m_q": ((9, 8, 128), F32),
        "lse": ((3, 8, 512), F32),
        "att": ((1152, HD), BF16),
        "reorder": ((IMG, HD), F32),
        "part": ((32, 32, HD), BF16),
        "part_in": ((32, 32, HD), BF16),
        "att_txt": ((4, TXT, HD), BF16),
        "atx": ((4, TXT, HD), BF16),
        "gown": ((32, HD), BF16),
        "gall": ((32, 32, HD), BF16),
        "gup": ((CH, HD), F32),
        "order": ((1024, HD), F32),
        "gpu": ((1024, HD), BF16),
        "do": ((1152, HD), BF16),
        "dk": ((4096, HD), F32),
        "dv": ((4096, HD), F32),
        "dq": ((4, IMG, HD), F32),
        "dqs": ((512, HD), F32),
        "ex": ((4, IMG, HD), F32),
        "dpre": ((16, IMG, HD), BF16),
        "grads": ((1024, 384), BF16),
        "small_u": ((HD, 384), F32),
        "low_u": ((4, 32, 384), BF16),
        "low_u_in": ((4, 32, 384), BF16),
        "small": ((HD, 512), F32),
        "low_d": ((4, 32, 512), BF16),
        "low_d_in": ((4, 32, 512), BF16),
        "wide_u": ((32, 32, HD), BF16),
        "wide_u_in": ((32, 32, HD), BF16),
        "base_d": ((32, D), F32),
        "wide_d": ((32, 32, HD), BF16),
        "wide_d_in": ((32, 32, HD), BF16),
        "mixed": ((8, 4, D), BF16),
        "mixed_in": ((8, 4, D), BF16),
        "conv": ((4, 80, HD), BF16),
        "conv_in": ((4, 80, HD), BF16),
        "conv_a": ((80, HD), BF16),
        "conv_sx": ((8, 80, HD), BF16),
        "conv_b": ((80, HD), BF16),
        "conv_gr": ((4, 80, HD), BF16),
        "conv_c": ((80, HD), BF16),
    }
    sems = {"local": (6,), "s_wide_u": (2, 8), "s_wide_d": (2, 8)}
    for name in (
        ("lat", "off", "text", "do", "tgrad", "lats", "kv", "qd", "part", "atx", "up", "hu", "su")
        + ("mix", "hd", "sd", "c1", "c2", "c3", "c4")
    ):
        sems["s_" + name] = (2,)
    names = list(inputs) + list(outs) + list(scratch) + list(sems)
    hbm = {"w_down", "w_up", "w_query", "w_key", "w_value", "w_out"}
    specs = []
    for name in inputs:
        kind = pl.ANY if name in hbm else pltpu.SMEM if name == "offset" else pltpu.VMEM
        specs.append(pl.BlockSpec(memory_space=kind))
    return pl.pallas_call(
        functools.partial(whole_kernel, names),
        out_shape=[sds(*v) for v in outs.values()],
        in_specs=specs,
        out_specs=vmem(len(outs)),
        scratch_shapes=[space(*v) for v in scratch.values()] + [dma(v) for v in sems.values()],
        compiler_params=pltpu.CompilerParams(
            collective_id=cid, has_side_effects=True, vmem_limit_bytes=61 * 2**20
        ),
    )(*inputs.values())


def results_kernel(pred, text, down, up, conv, out, *results):
    for src, dst in zip((pred, text), results[:2]):
        dst[0] = src[...]
    for src, dst in zip((down, up, conv), results[2:5]):
        dst[...] = src[...].astype(F32)
    results[5][...] = out[...]


def results(*arrays):
    sds = jax.ShapeDtypeStruct
    shapes = [
        sds((1, 2, PW * CH), BF16),
        sds((1, 4, D), BF16),
        sds((HD, D), F32),
        sds((D, HD), F32),
        sds((288, HD), F32),
        sds((CH, HD), F32),
    ]
    return pl.pallas_call(
        results_kernel,
        out_shape=shapes,
        in_specs=vmem(6),
        out_specs=vmem(6),
        compiler_params=pltpu.CompilerParams(vmem_limit_bytes=32 * 2**20),
    )(*arrays)


def rope_base():
    half = HD // 2
    freq = np.exp(-(2.0 * np.arange(half) / HD) * math.log(ROPE_BASE))
    slot = np.arange(IMG)
    position = (slot % PH) * PW + slot // PH
    angle = position[:, None] * freq[None, :]
    cosine = np.concatenate([np.cos(angle), np.cos(angle)], axis=1)
    sine = np.concatenate([-np.sin(angle), np.sin(angle)], axis=1)
    return jnp.asarray(np.stack([cosine, sine]).astype(np.float32))


def shards(
    text_tokens,
    latent,
    image_offset,
    norm_gain,
    w_query,
    w_key,
    w_value,
    w_out,
    w_down_conv,
    w_down_proj,
    w_up_proj,
    w_up_out,
    pred_grad,
    text_grad,
):
    pred, text_out, grad_down_proj, grad_up_proj, grad_conv, grad_out = whole(
        {
            "offset": image_offset,
            "text": text_tokens[0],
            "tgrad": text_grad[0],
            "lat": latent[0],
            "gain": norm_gain,
            "pgrad": pred_grad[0],
            "wconv": w_down_conv,
            "w_uo": w_up_out.T,
            "base": rope_base(),
            "w_down": w_down_proj,
            "w_up": w_up_proj,
            "w_query": w_query,
            "w_key": w_key,
            "w_value": w_value,
            "w_out": w_out,
        },
        1,
    )
    pred, text_out, grad_down_proj, grad_up_proj, grad_conv, grad_out = results(
        pred, text_out, grad_down_proj, grad_up_proj, grad_conv, grad_out
    )
    return pred, text_out, grad_conv, grad_down_proj, grad_up_proj, grad_out.T


def solution(mesh):
    placed = (
        P("sy", "sx", None),
        P("sy", "sx", None),
        P("sy"),
        P(),
        P(None, "sx"),
        P(None, "sx"),
        P(None, "sx"),
        P("sx", None),
        P(),
        P(),
        P(),
        P(),
        P("sy", "sx", None),
        P("sy", "sx", None),
    )
    return jax.shard_map(
        shards,
        mesh=mesh,
        in_specs=placed,
        out_specs=(P("sy", "sx", None), P("sy", "sx", None), P(), P(), P(), P()),
        check_vma=False,
    )
```

```python
import functools
import math
import types

import jax
import jax.numpy as jnp
import numpy as np
from jax import lax
from jax.experimental import pallas as pl
from jax.experimental.pallas import tpu as pltpu
from jax.sharding import PartitionSpec as P

MESH = pl.DeviceIdType.MESH
F32 = jnp.float32
BF16 = jnp.bfloat16
HD = 128
SB = 288
TXT = 32
IMG = 256
PH = 16
PW = 16
CH = 32
D = 4096
EPS = 1e-05
NEG = -1e30
LOG2E = math.log2(math.e)
SCALE = HD ** (-0.5)
ROPE_BASE = 500000.0
SIZES = {"sx": 8, "sy": 16, "group": 4, "head": 4, "team": 32}
NT = (((1,), (1,)), ((), ()))
TN = (((0,), (0,)), ((), ()))


def dot(a, b, dims=(((1,), (0,)), ((), ()))):
    return lax.dot_general(a, b, dims, preferred_element_type=F32)


def vmem(count):
    return [pl.BlockSpec(memory_space=pltpu.VMEM)] * count


def mod(a, n):
    return a % n if isinstance(a, int) else lax.rem(a, n)


def div(a, n):
    return a // n if isinstance(a, int) else lax.div(a, n)


def sy_of(g, i):
    if isinstance(i, int):
        return 2 * g + i if i < 2 else 12 - 2 * g + i
    return jnp.where(i < 2, 2 * g + i, 12 - 2 * g + i)


def split_sy(sy):
    low = sy < 8
    g = jnp.where(low, div(sy, 2), div(15 - sy, 2))
    i = mod(sy, 2) + jnp.where(low, 0, 2)
    return g, i


def ring(kind):
    sx = lax.axis_index("sx")
    sy = lax.axis_index("sy")
    g, i = split_sy(sy)
    if kind == "sx":
        return sx, lambda o: (mod(sx + o, 8), sy, mod(sx + o, 8))
    if kind == "sy":
        return sy, lambda o: (sx, mod(sy + o, 16), mod(sy + o, 16))
    if kind == "group":
        return i, lambda o: (sx, sy_of(g, mod(i + o, 4)), mod(i + o, 4))
    if kind == "head":
        return g, lambda o: (sx, sy_of(mod(g + o, 4), i), mod(g + o, 4))
    e = i * 8 + sx

    def peer(o):
        f = mod(e + o, 32)
        return mod(f, 8), sy_of(g, div(f, 8)), f

    return e, peer


def remote(src, dst, send, recv, to):
    copy = pltpu.make_async_remote_copy(
        src_ref=src,
        dst_ref=dst,
        send_sem=send,
        recv_sem=recv,
        device_id=to,
        device_id_type=MESH,
    )
    copy.start()
    return copy


class Fan:
    def __init__(self, kind, source, land, sems, slot_of=None):
        own, peer = ring(kind)
        self.land = land.at[pl.ds(0, SIZES[kind] - 1)]
        self.sems = sems

        @pl.loop(1, SIZES[kind])
        def _(o):
            tx, ty, to = peer(o)
            src = source if slot_of is None else source.at[slot_of(ty, to)]
            remote(src, land.at[own], sems.at[0], sems.at[1], (tx, ty))

    def arrived(self):
        pltpu.make_async_copy(self.land, self.land, self.sems.at[1]).wait()

    def sent(self):
        pltpu.make_async_copy(self.land, self.land, self.sems.at[0]).wait()


class Team:
    def __init__(self, source, land, sems):
        sy = lax.axis_index("sy")
        self.g, i = split_sy(sy)
        self.own = i * 8 + lax.axis_index("sx")
        self.source = source
        self.slots = land
        self.land = land.at[pl.ds(0, 31)]
        self.sems = sems

    def push(self, f):
        @pl.when(f != self.own)
        def _():
            to = (mod(f, 8), sy_of(self.g, div(f, 8)))
            remote(
                self.source.at[f], self.slots.at[self.own], self.sems.at[0], self.sems.at[1], to
            )

    def keep(self):
        self.slots[self.own] = self.source[self.own]

    arrived = Fan.arrived
    sent = Fan.sent


def sigmoid(v):
    return 1.0 / (1.0 + jnp.exp(-v))


def turn(v, cosine, sine):
    return v * cosine + pltpu.roll(v, 64, 1) * sine


def trig(shape, position):
    lane = lax.broadcasted_iota(jnp.int32, shape, 1)
    step = (lane % 64).astype(F32)
    angle = position * jnp.exp(step * (-2.0 / HD * math.log(ROPE_BASE)))
    sine = jnp.sin(angle)
    return jnp.cos(angle), jnp.where(lane < 64, -sine, sine)


def tables(j, phase_ref, base_ref):
    pc = phase_ref[0, pl.ds(j, 1), :]
    ps = phase_ref[1, pl.ds(j, 1), :]
    bc = base_ref[0]
    bs = base_ref[1]
    return pc * bc - ps * bs, ps * bc + pc * bs


def row_sum(v):
    return dot(v.astype(BF16), jnp.ones((HD, HD), BF16))


def row_scale(da, wd):
    both = dot(da, wd)
    dawd = both[:, :HD] + both[:, HD:]
    return dawd, lax.rsqrt(row_sum(dawd * da.astype(F32)) * (1.0 / D) + EPS)


def lanes(column):
    return column.T[:1, :]


def place(x, y, z, core):
    return 2 * x + mod(z, 2), 4 * y + 2 * div(z, 2) + core


class Spread:
    def __init__(self, every, sems):
        self.every = every
        self.sems = sems
        sx = lax.axis_index("sx")
        sy = lax.axis_index("sy")
        self.core = mod(sy, 2)
        x = div(sx, 2)
        y = div(sy, 4)
        z = 2 * mod(div(sy, 2), 2) + mod(sx, 2)
        self.even = self.core == 0
        self.p1 = jnp.where(self.even, x, z)
        self.p2 = jnp.where(self.even, y, x)
        self.p3 = jnp.where(self.even, z, y)
        self.twin = place(x, y, z, 1 - self.core)
        self.here = every.at[self.core]
        self.spot = (self.p3 * 4 + self.p2) * 4 + self.p1
        self.live = []

    def chip(self, a, b, c):
        a = mod(a, 4)
        b = mod(b, 4)
        c = mod(c, 4)
        even = self.even
        return place(
            jnp.where(even, a, b), jnp.where(even, b, c), jnp.where(even, c, a), self.core
        )

    def send(self, ref, n, to):
        copy = remote(ref, ref, self.sems.at[0, n], self.sems.at[1, n], to)
        self.live.append(copy)
        return copy

    def slab(self, p):
        return self.here.at[pl.ds(mod(p, 4) * 16, 16)]

    def plane(self, block):
        self.every[self.core, self.spot] = block
        mine = self.here.at[self.spot]

        @pl.loop(1, 16)
        def _(o):
            to = self.chip(self.p1 + mod(o, 4), self.p2 + div(o, 4), self.p3)
            remote(mine, mine, self.sems.at[0, 0], self.sems.at[1, 0], to)

    def slabs(self):
        plane = self.here.at[pl.ds(0, 15)]
        pltpu.make_async_copy(plane, plane, self.sems.at[1, 0]).wait()
        own = self.slab(self.p3)
        self.wave = [self.send(own, o, self.chip(self.p1, self.p2, self.p3 + o)) for o in (1, 3, 2)]
        self.twins = [self.send(own, 4, self.twin)]

    def pass_on(self):
        for o, copy in zip((1, 3, 2), self.wave):
            copy.wait_recv()
            self.twins.append(self.send(self.slab(self.p3 + 4 - o), 4 + o, self.twin))

    def arrived(self):
        for copy in self.twins:
            copy.wait_recv()

    def sent(self):
        plane = self.here.at[pl.ds(0, 15)]
        pltpu.make_async_copy(plane, plane, self.sems.at[0, 0]).wait()
        for copy in self.live:
            copy.wait_send()


def greet(wide):
    barrier = pltpu.get_barrier_semaphore()
    for kind in ("team", "sy"):
        _, peer = ring(kind)

        @pl.loop(1, SIZES[kind])
        def _(o):
            tx, ty, _ = peer(o)
            pl.semaphore_signal(barrier, inc=1, device_id=(tx, ty), device_id_type=MESH)

    @pl.loop(1, 16)
    def _(o):
        to = wide.chip(wide.p1 + mod(o, 4), wide.p2 + div(o, 4), wide.p3)
        pl.semaphore_signal(barrier, inc=1, device_id=to, device_id_type=MESH)

    @pl.loop(1, 4)
    def _(o):
        to = wide.chip(wide.p1, wide.p2, wide.p3 + o)
        pl.semaphore_signal(barrier, inc=1, device_id=to, device_id_type=MESH)

    return lambda: pl.semaphore_wait(barrier, 31 + 15 + 15 + 3)


def masks(r, g, members):
    block = lax.broadcasted_iota(jnp.int32, (16, HD), 0).astype(F32)
    cosine, sine = trig((16, HD), block * float(SB) + jnp.max(r.offs[...], axis=1))
    r.phase[0] = cosine
    r.phase[1] = sine
    starts = [r.offs[b][:1, :] for b in members]
    row = lax.broadcasted_iota(jnp.int32, (512, TXT), 0)
    query = lax.broadcasted_iota(jnp.int32, (512, TXT), 1)
    for m in range(4):
        b = members[m]
        seen = (row // TXT < b) | ((row // TXT == b) & (row % TXT <= query))
        r.bias_tt[:, m * TXT : (m + 1) * TXT] = jnp.where(seen, 0.0, NEG)
    lane = lax.broadcasted_iota(jnp.int32, (8, HD), 1)
    start = starts[0]
    owner = jnp.full((8, HD), members[0], jnp.int32)
    for m in range(1, 4):
        start = jnp.where(lane // TXT == m, starts[m], start)
        owner = jnp.where(lane // TXT == m, members[m], owner)
    late = jnp.where((lane % TXT).astype(F32) >= start, 1.0, 0.0)
    r.vis[...] = late + owner.astype(F32)
    lane = lax.broadcasted_iota(jnp.int32, (512, HD), 1)
    row = lax.broadcasted_iota(jnp.int32, (512, HD), 0)
    start = jnp.broadcast_to(starts[0], (512, HD))
    owner = jnp.full((512, HD), members[0], jnp.int32)
    for m in range(1, 4):
        start = jnp.where(lane == m, starts[m], start)
        owner = jnp.where(lane == m, members[m], owner)
    seen = (row // TXT < owner) | ((row // TXT == owner) & ((row % TXT).astype(F32) < start))
    r.bias_ti[...] = jnp.where(seen, 0.0, NEG)


def down_block(r):
    r.wpad[...] = jnp.zeros_like(r.wpad)
    for tap in range(3):
        r.wpad[tap * 128 : tap * 128 + 96, :] = r.wconv[tap * 96 : tap * 96 + 96, :].astype(F32)
    mid = r.lat_all[...].reshape(256, PW * CH).astype(F32)
    mid = pltpu.roll(jnp.concatenate([mid, jnp.zeros((256, HD), F32)], axis=1), CH, 1)
    row = lax.broadcasted_iota(jnp.int32, mid.shape, 0) % PH
    r.wide[0] = jnp.where(row == 0, 0.0, pltpu.roll(mid, 1, 0))
    r.wide[1] = mid
    r.wide[2] = jnp.where(row == PH - 1, 0.0, pltpu.roll(mid, 16 * PH - 1, 0))
    weight = r.wpad[...].astype(BF16)
    for c in range(PW):
        for tap in range(3):
            r.patches[c, :, tap * 128 : tap * 128 + 128] = r.wide[
                tap, :, c * CH : c * CH + 128
            ].astype(BF16)
        pre = dot(r.patches[c], weight)
        sig = sigmoid(pre)
        r.da[:, c * PH : c * PH + PH, :] = (pre * sig).astype(BF16).reshape(16, PH, HD)
        r.sp[:, c * PH : c * PH + PH, :] = (
            (sig * (1.0 + pre * (1.0 - sig))).astype(BF16).reshape(16, PH, HD)
        )


def project(r, members):
    mix_kv = r.mix[:, HD:]
    mix_q = r.mix[:, :HD]
    wd = r.wd[...]

    @pl.loop(0, 4)
    def _(n):
        da = r.da[pl.ds(4 * n, 4)].reshape(4 * IMG, HD)
        _, inv = row_scale(da, wd)
        scaled = (da.astype(F32) * inv).astype(BF16)
        kv = dot(scaled, mix_kv)
        whole = pl.ds(pl.multiple_of(n * 1024, 1024), 1024)
        r.vt[:, whole] = dot(mix_kv[:, HD:], scaled, (((0,), (1,)), ((), ()))).astype(BF16)
        for m in range(4):
            j = 4 * n + m
            cosine, sine = tables(j, r.phase, r.base)
            rows = pl.ds(pl.multiple_of(j * IMG, IMG), IMG)
            part = kv[m * IMG : (m + 1) * IMG, :]
            r.k[rows, :] = turn(part[:, :HD], cosine, sine).astype(BF16)
            r.v[rows, :] = part[:, HD:].astype(BF16)

    for m in range(4):
        r.da_own[m * IMG : (m + 1) * IMG, :] = r.da[members[m]]
    da = r.da_own[...]
    _, inv = row_scale(da, wd)
    queries = dot((da.astype(F32) * inv).astype(BF16), mix_q) * (SCALE * LOG2E)
    for m in range(4):
        rows = slice(m * IMG, (m + 1) * IMG)
        cosine, sine = tables(members[m], r.phase, r.base)
        r.q[rows, :] = turn(queries[rows, :], cosine, sine).astype(BF16)


def tile_rows(j):
    return pl.ds(pl.multiple_of(j * 512, 512), 512)


def absorb(state, scores, vt, e_ref, m_ref):
    top = jnp.max(scores, axis=0, keepdims=True)
    new = top if state is None else jnp.maximum(state[0], top)
    raised = jnp.exp2(scores - new)
    low = raised.astype(BF16)
    e_ref[...] = low
    m_ref[...] = jnp.broadcast_to(new, m_ref.shape)
    total = jnp.sum(raised, axis=0, keepdims=True)
    mixed = dot(vt, low)
    if state is None:
        return new, total, mixed
    old = jnp.exp2(state[0] - new)
    return new, state[1] * old + total, state[2] * old + mixed


def conclude(r, p, width, state):
    peak, total, acc = state
    r.att[p * 512 : p * 512 + width, :] = (acc / total).T.astype(BF16)
    r.lse[p, :, :width] = jnp.broadcast_to(peak + jnp.log2(total), (8, width))


def diagonal_mask(scores):
    bottom = lax.broadcasted_iota(jnp.int32, scores.shape, 0) >= IMG
    left = lax.broadcasted_iota(jnp.int32, scores.shape, 1) < IMG
    return jnp.where(bottom & left, NEG, scores)


def attend_images(r, p, diagonal, text_ready):
    q = r.q[p * 512 : p * 512 + 512, :]
    base = 4 * p

    def tile(j):
        return dot(r.k[tile_rows(j), :], q, NT)

    state = absorb(
        None,
        diagonal_mask(tile(diagonal)),
        r.vt[:, tile_rows(diagonal)],
        r.e_img.at[base + diagonal],
        r.m_img.at[base + diagonal],
    )

    def body(j, state):
        return absorb(
            state, tile(j), r.vt[:, tile_rows(j)], r.e_img.at[base + j], r.m_img.at[base + j]
        )

    state = lax.fori_loop(0, diagonal, body, state)
    text_ready()
    scores = dot(r.kt[...], q, NT)
    bias = jnp.concatenate(
        [
            jnp.broadcast_to(r.bias_ti[:, 2 * p + half : 2 * p + half + 1], (512, IMG))
            for half in range(2)
        ],
        axis=1,
    )
    scores = jnp.where(bias < 0.0, NEG, scores)
    state = absorb(state, scores, r.vtt[...], r.e_txt.at[p], r.m_txt.at[p])
    conclude(r, p, 512, state)


def attend_text(r, count, kept):
    q = r.q[1024:, :]
    vis = r.vis[:1, :]
    scores = jnp.where(r.bias_tt[...] < 0.0, NEG, dot(r.kt[...], q, NT))
    state = absorb(None, scores, r.vtt[...], r.e_q.at[8], r.m_q.at[8])

    def body(j, state):
        scores = dot(r.k[tile_rows(j), :], q, NT)
        block = 2 * j + (lax.broadcasted_iota(jnp.int32, scores.shape, 0) >= IMG).astype(jnp.int32)
        scores = jnp.where(block.astype(F32) < vis, scores, NEG)
        return absorb(state, scores, r.vt[:, tile_rows(j)], r.e_q.at[j], r.m_q.at[j])

    conclude(r, 2, 128, lax.fori_loop(0, count, body, state))


def normalise(e_ref, m_ref, lse):
    factor = jnp.exp2(m_ref[:1, :] - lse)
    e_ref[...] = (e_ref[...].astype(F32) * factor).astype(BF16)


def backward_rows(r, p, width):
    rows = slice(p * 512, p * 512 + width)
    q = r.q[rows, :]
    do = r.do[rows, :]
    sums = jnp.sum(do.astype(F32) * r.att[rows, :].astype(F32), axis=1, keepdims=True)
    return q, do, lanes(jnp.broadcast_to(sums, (width, HD)))


def backward_images(r, p, diagonal, members):
    q, do, delta = backward_rows(r, p, 512)
    base = 4 * p

    probs = r.e_txt[p].astype(F32)
    grad = (probs * (dot(r.vtx[...], do, NT) - delta)).astype(BF16)
    r.dqs[...] = dot(grad, r.kt[...], TN)

    @pl.loop(0, diagonal + 1)
    def _(j):
        at = tile_rows(j)
        keys = r.k[at, :]
        probs = r.e_img[base + j]
        grad = (probs.astype(F32) * (dot(r.v[at, :], do, NT) - delta)).astype(BF16)
        r.dv[at, :] += dot(probs, do)
        r.dk[at, :] += dot(grad, q)
        r.dqs[...] += dot(grad, keys, TN)

    for half in range(2):
        r.dq[2 * p + half] = r.dqs[half * IMG : (half + 1) * IMG, :]


def backward_text(r, count):
    q, do, delta = backward_rows(r, 2, 128)

    @pl.loop(0, count)
    def _(j):
        at = tile_rows(j)
        probs = r.e_q[j]
        grad = (probs.astype(F32) * (dot(r.v[at, :], do, NT) - delta)).astype(BF16)
        r.dv[at, :] += dot(probs, do)
        r.dk[at, :] += dot(grad, q)


def image_grads(r, g):
    wd = r.wd[...]
    mix = r.mix[...]
    r.small[...] = jnp.zeros_like(r.small)

    @pl.loop(0, 4)
    def _(n):
        da = r.da[pl.ds(4 * n, 4)].reshape(4 * IMG, HD)
        da_wide = da.astype(F32)
        dawd, inv = row_scale(da, wd)
        extra = []
        for k in range(4):
            j = 4 * n + k
            group, m = split_sy(j)
            ours = (group == g).astype(F32)
            cosine, sine = tables(j, r.phase, r.base)
            at = pl.ds(pl.multiple_of(j * IMG, IMG), IMG)
            rows = slice(k * IMG, (k + 1) * IMG)
            gq = turn(r.dq[m] * (ours * SCALE), cosine, -sine)
            gk = turn(r.dk[at, :] * (1.0 / LOG2E), cosine, -sine)
            r.grads[rows, :HD] = gq.astype(BF16)
            r.grads[rows, HD : 2 * HD] = gk.astype(BF16)
            r.grads[rows, 2 * HD :] = r.dv[at, :].astype(BF16)
            extra.append(r.ex[m] * ours)
        grads = r.grads[...]
        back = dot(grads, mix, NT)
        cube = (inv * inv * inv) * (row_sum(back * da_wide) * (1.0 / D))
        slope = r.sp[pl.ds(4 * n, 4)].reshape(4 * IMG, HD).astype(F32)
        grad = (inv * back - cube * dawd + jnp.concatenate(extra, axis=0)) * slope
        r.dpre[pl.ds(4 * n, 4)] = grad.astype(BF16).reshape(4, IMG, HD)
        r.small[:, :384] += dot((da_wide * inv).astype(BF16), grads, TN)
        r.small[:, 384:] += dot((da_wide * cube).astype(BF16), da, TN)


def conv_grad(r):
    total = jnp.zeros((384, HD), F32)
    for c in range(PW):
        grad = r.dpre[:, c * PH : c * PH + PH, :].reshape(256, HD)
        total = total + dot(r.patches[c], grad, TN)
    rows = [total[tap * 128 : tap * 128 + 96, :] for tap in range(3)] + [r.gup[...]]
    whole = jnp.concatenate(rows, axis=0).astype(BF16)
    for n in range(4):
        r.conv[n] = whole[80 * n : 80 * n + 80, :]


def block_of(group, e):
    sx = e % 8
    sy = sy_of(group, e // 8)
    x = sx // 2
    y = sy // 4
    z = 2 * ((sy // 2) % 2) + sx % 2
    core = sy % 2
    return core, (z * 4 + y) * 4 + x if core == 0 else (y * 4 + x) * 4 + z


def lay_up(r):
    for e in range(32):
        cols = [r.every_u[block_of(group, e)].astype(F32) for group in range(4)]
        r.grad_up[e * HD : (e + 1) * HD, :] = jnp.concatenate(cols, axis=0).T.astype(BF16)


def lay_down(r):
    for e in range(32):
        for group in range(4):
            r.grad_down[32 * group : 32 * group + 32, e * HD : (e + 1) * HD] = r.every_d[
                block_of(group, e)
            ]


def whole_kernel(names, *refs):
    r = types.SimpleNamespace(**dict(zip(names, refs)))
    sx = lax.axis_index("sx")
    sy = lax.axis_index("sy")
    g, head = split_sy(sy)
    members = [sy_of(g, m) for m in range(4)]
    mine = pl.ds(pl.multiple_of(head * HD, HD), HD)
    loads = []
    for at, (src, dst) in enumerate(
        [
            (r.w_down, r.dn),
            (r.w_up, r.up),
            (r.w_query, r.wq),
            (r.w_key, r.wk),
            (r.w_value, r.wv),
            (r.w_out, r.wo),
        ]
    ):
        copy = pltpu.make_async_copy(src, dst, r.local.at[at])
        copy.start()
        loads.append(copy)
    wide_u = Spread(r.every_u, r.s_wide_u)
    wide_d = Spread(r.every_d, r.s_wide_d)
    all_here = greet(wide_u)
    r.own_off[...] = jnp.full((8, HD), r.offset[0].astype(F32))
    for k in range(2):
        row = r.pgrad[...].astype(F32)[k : k + 1, :]
        for c in range(PW):
            r.pg[k * PW + c : k * PW + c + 1, :] = row[:, c * CH : c * CH + CH]
    gain = r.gain[...].astype(F32).reshape(1, D)
    r.gain_row[...] = gain
    loads[0].wait()
    loads[1].wait()
    down = r.dn[...]
    both = dot(down, down, NT)
    high = both.astype(BF16)
    r.wd[:, :HD] = high
    r.wd[:, HD:] = (both - high.astype(F32)).astype(BF16)
    r.wu[...] = dot(down, r.up[...]).astype(BF16)
    scaled = (down.astype(F32) * gain).astype(BF16)
    all_here()

    lat = Fan("sx", r.lat, r.lat_in, r.s_lat)
    text = Fan("sx", r.text, r.text_in, r.s_text)
    offs = Fan("sy", r.own_off, r.offs, r.s_off)
    r.offs[sy] = r.own_off[...]
    r.lat_in[sx] = r.lat[...]
    r.text_in[sx] = r.text[...]

    lat.arrived()
    for n in range(8):
        r.rows_lat[2 * n : 2 * n + 2, :] = r.lat_in[n].astype(F32)
    r.row_lat[...] = r.rows_lat[...].astype(BF16)
    lats = Fan("sy", r.row_lat, r.lat_all, r.s_lats)
    r.lat_all[sy] = r.row_lat[...]
    for n, weight in enumerate([r.wq, r.wk, r.wv]):
        loads[2 + n].wait()
        r.mix[:, n * HD : (n + 1) * HD] = dot(scaled, weight[:, mine]).astype(BF16)
    loads[5].wait()
    r.nt[...] = dot(r.up[...], r.wo[mine, :], (((0,), (1,)), ((), ()))).astype(BF16)

    text.arrived()
    for n in range(8):
        r.rows_text[4 * n : 4 * n + 4, :] = r.text_in[n].astype(F32)
    wide = r.rows_text[...]
    inverse = lax.rsqrt(jnp.mean(wide * wide, axis=1, keepdims=True) + EPS)
    normed = (wide * inverse * gain).astype(BF16)
    token = lax.broadcasted_iota(jnp.int32, (TXT, HD), 0).astype(F32)
    shift = jnp.where(token >= r.own_off[:1, :], float(IMG), 0.0)
    cosine, sine = trig((TXT, HD), token + shift + (sy * SB).astype(F32))
    query = dot(normed, r.wq[...])
    key = dot(normed, r.wk[...])
    value = dot(normed, r.wv[...])
    for h in range(4):
        at = slice(h * HD, (h + 1) * HD)
        r.kv_out[h, :, :HD] = turn(key[:, at], cosine, sine).astype(BF16)
        r.kv_out[h, :, HD:] = value[:, at].astype(BF16)
        turned = turn(query[:, at], cosine, sine)
        r.qd_out[h] = (turned * (SCALE * LOG2E)).astype(BF16)
    kvs = Fan("sy", r.kv_out, r.kv_in, r.s_kv, lambda ty, to: split_sy(ty)[1])
    qds = Fan("group", r.qd_out, r.qd_in, r.s_qd, lambda ty, to: to)
    r.kv_in[sy] = r.kv_out[head]
    r.qd_in[head] = r.qd_out[head]

    offs.arrived()
    masks(r, g, members)

    lats.arrived()
    tgrad = Fan("sx", r.tgrad, r.tgrad_in, r.s_tgrad)
    r.tgrad_in[sx] = r.tgrad[...]
    down_block(r)

    project(r, members)

    def text_ready():
        kvs.arrived()
        qds.arrived()
        kv = r.kv_in[...].reshape(512, 256)
        r.kt[...] = kv[:, :HD]
        r.vtx[...] = kv[:, HD:]
        r.vtt[...] = kv[:, HD:].astype(F32).T.astype(BF16)
        r.q[1024:, :] = r.qd_in[...].reshape(128, HD)

    def add_part(m):
        r.reorder[...] = dot(r.att[m * IMG : (m + 1) * IMG, :], r.nt[...], NT) + dot(
            r.da_own[m * IMG : (m + 1) * IMG, :], r.wu[...]
        ) * (1.0 / 32.0)
        for n in range(8):
            for k in range(2):
                r.part[8 * m + n, k * PW : (k + 1) * PW, :] = r.reorder[
                    pl.ds(2 * n + k, PW, stride=PH), :
                ].astype(BF16)

    parts = Team(r.part, r.part_in, r.s_part)
    e = parts.own
    attend_images(r, 1, 7 - g, text_ready)
    add_part(2)
    add_part(3)

    @pl.loop(0, 16)
    def _(o):
        parts.push(16 + mod(e + o, 16))

    attend_images(r, 0, g, lambda: None)
    add_part(0)
    add_part(1)

    @pl.loop(0, 16)
    def _(o):
        parts.push(mod(e + o, 16))

    parts.keep()

    tgrad.arrived()
    for n in range(8):
        r.rows_grad[4 * n : 4 * n + 4, :] = r.tgrad_in[n].astype(F32)
    outer = dot(r.rows_grad[...].astype(BF16), r.wo[...], NT)
    for h in range(4):
        r.d_out[h] = outer[:, h * HD : (h + 1) * HD].astype(BF16)
    outers = Fan("group", r.d_out, r.d_in, r.s_do, lambda ty, to: to)
    r.d_in[head] = r.d_out[head]
    attend_text(r, 8 - g, None)
    for m in range(4):
        r.att_txt[m] = r.att[1024 + m * TXT : 1024 + (m + 1) * TXT, :]
    atx = Fan("group", r.att_txt, r.atx, r.s_atx, lambda ty, to: to)
    r.atx[head] = r.att_txt[head]
    r.dk[...] = jnp.zeros_like(r.dk)
    r.dv[...] = jnp.zeros_like(r.dv)
    parts.arrived()
    pre = jnp.sum(r.part_in[...].astype(F32), axis=0)
    sig = sigmoid(pre)
    act = (pre * sig).astype(BF16)
    slope = sig * (1.0 + pre * (1.0 - sig))
    pgrad = r.pg[...].astype(BF16)
    r.gown[...] = (dot(pgrad, r.w_uo[...]) * slope).astype(BF16)
    ups = Fan("team", r.gown, r.gall, r.s_up)
    r.gall[e] = r.gown[...]
    pred = dot(act, r.w_uo[...], NT)
    for k in range(2):
        for c in range(PW):
            r.pred_rows[k : k + 1, c * CH : c * CH + CH] = pred[k * PW + c : k * PW + c + 1, :]
    r.pred[...] = r.pred_rows[...].astype(BF16)
    r.gup[...] = dot(pgrad, act, TN)
    for p, diagonal in ((0, g), (1, 7 - g)):
        lse = r.lse[p, :1, :]

        @pl.loop(0, diagonal + 1)
        def _(j):
            normalise(r.e_img.at[4 * p + j], r.m_img.at[4 * p + j], lse)

        normalise(r.e_txt.at[p], r.m_txt.at[p], lse)

    @pl.loop(0, 8 - g)
    def _(j):
        normalise(r.e_q.at[j], r.m_q.at[j], r.lse[2, :1, :HD])

    outers.arrived()
    r.do[1024:, :] = r.d_in[...].reshape(128, HD)
    backward_text(r, 8 - g)

    ups.arrived()
    for m in range(4):
        for n in range(8):
            nat = r.gall[8 * m + n].astype(F32)
            for k in range(2):
                r.order[pl.ds(m * IMG + 2 * n + k, PW, stride=PH), :] = nat[
                    k * PW : (k + 1) * PW, :
                ]
    r.gpu[...] = r.order[...].astype(BF16)
    r.do[:1024, :] = dot(r.gpu[...], r.nt[...]).astype(BF16)

    gpu = r.gpu[...]
    grad = dot(gpu, r.wu[...], NT) * (1.0 / 32.0)
    for m in range(4):
        r.ex[m] = grad[m * IMG : (m + 1) * IMG, :]
    own = r.da_own[...]
    r.small_u[:, :HD] = dot(gpu, r.att[:1024, :], TN)
    r.small_u[:, HD : 2 * HD] = dot(gpu, own, TN) * (1.0 / 32.0)
    r.small_u[:, 2 * HD :] = dot(own, gpu, TN) * (1.0 / 32.0)
    for n in range(4):
        r.low_u[n] = r.small_u[32 * n : 32 * n + 32, :].astype(BF16)
    heads_u = Fan("head", r.low_u, r.low_u_in, r.s_hu, lambda ty, to: to)
    r.low_u_in[g] = r.low_u[g]

    backward_images(r, 0, g, members)

    atx.arrived()
    joined = jnp.concatenate([r.atx[h] for h in range(4)], axis=1)

    @pl.loop(0, 8)
    def _(c):
        at = pl.ds(pl.multiple_of(c * 512, 512), 512)
        out = dot(joined, r.wo[:, at])
        for n in range(8):
            r.mixed[n, :, at] = out[4 * n : 4 * n + 4, :].astype(BF16)

    heads_u.arrived()
    low_u = jnp.sum(r.low_u_in[...].astype(F32), axis=0).astype(BF16)

    sums_u = Team(r.wide_u, r.wide_u_in, r.s_su)

    @pl.loop(0, 8)
    def _(n):
        c = mod(n + div(e, 4), 8)
        at = pl.ds(pl.multiple_of(c * 512, 512), 512)
        grad = dot(low_u[:, :HD], r.wo[mine, at]) + dot(low_u[:, HD : 2 * HD], r.dn[:, at])
        for k in range(4):
            r.wide_u[4 * c + k] = grad[:, k * HD : (k + 1) * HD].astype(BF16)
            sums_u.push(4 * c + k)

    sums_u.keep()
    mixes = Fan("sx", r.mixed, r.mixed_in, r.s_mix, lambda ty, to: to)
    r.mixed_in[sx] = r.mixed[sx]

    backward_images(r, 1, 7 - g, members)

    sums_u.arrived()
    wide_u.plane(jnp.sum(r.wide_u_in[...].astype(F32), axis=0).astype(BF16))
    image_grads(r, g)

    for n in range(4):
        r.low_d[n] = r.small[32 * n : 32 * n + 32, :].astype(BF16)
    heads_d = Fan("head", r.low_d, r.low_d_in, r.s_hd, lambda ty, to: to)
    r.low_d_in[g] = r.low_d[g]
    conv_grad(r)
    convs = Fan("head", r.conv, r.conv_in, r.s_c1, lambda ty, to: to)
    r.conv_in[g] = r.conv[g]

    @pl.loop(0, 8)
    def _(c):
        at = pl.ds(pl.multiple_of(c * 512, 512), 512)
        r.base_d[:, at] = dot(low_u[:, 2 * HD :], r.up[at, :], NT)

    heads_d.arrived()
    low = jnp.sum(r.low_d_in[...].astype(F32), axis=0).astype(BF16)

    sums_d = Team(r.wide_d, r.wide_d_in, r.s_sd)

    @pl.loop(0, 8)
    def _(n):
        c = mod(n + div(e, 4), 8)
        at = pl.ds(pl.multiple_of(c * 512, 512), 512)
        grad = dot(low[:, :HD], r.wq[at, mine], NT)
        grad = grad + dot(low[:, HD : 2 * HD], r.wk[at, mine], NT)
        grad = grad + dot(low[:, 2 * HD : 3 * HD], r.wv[at, mine], NT)
        grad = grad * r.gain_row[:, at]
        grad = grad + r.base_d[:, at]
        grad = grad - dot(low[:, 3 * HD :], r.dn[:, at])
        for k in range(4):
            r.wide_d[4 * c + k] = grad[:, k * HD : (k + 1) * HD].astype(BF16)
            sums_d.push(4 * c + k)

    sums_d.keep()
    wide_u.slabs()
    convs.arrived()
    r.conv_a[...] = jnp.sum(r.conv_in[...].astype(F32), axis=0).astype(BF16)
    beside = Fan("sx", r.conv_a, r.conv_sx, r.s_c2)
    r.conv_sx[sx] = r.conv_a[...]
    mixes.arrived()
    total = r.text[...].astype(F32)
    for n in range(8):
        total = total + r.mixed_in[n].astype(F32)
    r.text_out[...] = total.astype(BF16)
    sums_d.arrived()
    wide_d.plane(jnp.sum(r.wide_d_in[...].astype(F32), axis=0).astype(BF16))
    beside.arrived()
    r.conv_b[...] = jnp.sum(r.conv_sx[...].astype(F32), axis=0).astype(BF16)
    along = Fan("group", r.conv_b, r.conv_gr, r.s_c3)
    r.conv_gr[head] = r.conv_b[...]
    wide_u.pass_on()
    wide_d.slabs()
    along.arrived()
    r.conv_c[...] = jnp.sum(r.conv_gr[...].astype(F32), axis=0).astype(BF16)
    across = Fan("head", r.conv_c, r.conv_all, r.s_c4)
    r.conv_all[g] = r.conv_c[...]
    wide_u.arrived()
    lay_up(r)
    wide_d.pass_on()
    across.arrived()
    for n in range(3):
        r.grad_conv[80 * n : 80 * n + 80, :] = r.conv_all[n].astype(F32)
    rest = r.conv_all[3].astype(F32)
    r.grad_conv[240:, :] = rest[:48, :]
    r.grad_out[...] = rest[48:, :]
    wide_d.arrived()
    lay_down(r)
    for fan in (
        lat,
        offs,
        text,
        tgrad,
        lats,
        kvs,
        qds,
        outers,
        parts,
        atx,
        ups,
        heads_u,
        sums_u,
        mixes,
        heads_d,
        convs,
        sums_d,
        beside,
        along,
        across,
    ):
        fan.sent()
    wide_u.sent()
    wide_d.sent()


def whole(inputs, cid):
    sds = jax.ShapeDtypeStruct
    dma = pltpu.SemaphoreType.DMA
    space = pltpu.VMEM
    outs = {
        "pred": ((2, PW * CH), BF16),
        "text_out": ((4, D), BF16),
        "grad_down": ((HD, D), BF16),
        "grad_up": ((D, HD), BF16),
        "grad_conv": ((288, HD), F32),
        "grad_out": ((CH, HD), F32),
    }
    scratch = {
        "conv_all": ((4, 80, HD), BF16),
        "gain_row": ((1, D), F32),
        "pg": ((32, CH), F32),
        "pred_rows": ((2, PW * CH), F32),
        "every_u": ((2, 64, 32, HD), BF16),
        "every_d": ((2, 64, 32, HD), BF16),
        "dn": ((HD, D), BF16),
        "up": ((D, HD), BF16),
        "wq": ((D, 512), BF16),
        "wk": ((D, 512), BF16),
        "wv": ((D, 512), BF16),
        "wo": ((512, D), BF16),
        "lat_in": ((8, 2, PW * CH), BF16),
        "text_in": ((8, 4, D), BF16),
        "tgrad_in": ((8, 4, D), BF16),
        "own_off": ((8, HD), F32),
        "offs": ((16, 8, HD), F32),
        "row_lat": ((PH, PW * CH), BF16),
        "rows_lat": ((PH, PW * CH), F32),
        "lat_all": ((16, PH, PW * CH), BF16),
        "rows_text": ((TXT, D), F32),
        "rows_grad": ((TXT, D), F32),
        "wd": ((HD, 256), BF16),
        "wu": ((HD, HD), BF16),
        "mix": ((HD, 384), BF16),
        "nt": ((HD, HD), BF16),
        "kv_out": ((4, TXT, 256), BF16),
        "qd_out": ((4, TXT, HD), BF16),
        "kv_in": ((16, TXT, 256), BF16),
        "qd_in": ((4, TXT, HD), BF16),
        "d_out": ((4, TXT, HD), BF16),
        "d_in": ((4, TXT, HD), BF16),
        "phase": ((2, 16, HD), F32),
        "bias_tt": ((512, 128), F32),
        "bias_ti": ((512, HD), F32),
        "vis": ((8, HD), F32),
        "wpad": ((384, HD), F32),
        "wide": ((3, 256, 640), F32),
        "patches": ((16, 256, 384), BF16),
        "da": ((16, 256, HD), BF16),
        "sp": ((16, 256, HD), BF16),
        "da_own": ((1024, HD), BF16),
        "k": ((4096, HD), BF16),
        "v": ((4096, HD), BF16),
        "vt": ((HD, 4096), BF16),
        "q": ((1152, HD), BF16),
        "kt": ((512, HD), BF16),
        "vtx": ((512, HD), BF16),
        "vtt": ((HD, 512), BF16),
        "e_img": ((12, 512, 512), BF16),
        "m_img": ((12, 8, 512), F32),
        "e_txt": ((2, 512, 512), BF16),
        "m_txt": ((2, 8, 512), F32),
        "e_q": ((9, 512, 128), BF16),
        "m_q": ((9, 8, 128), F32),
        "lse": ((3, 8, 512), F32),
        "att": ((1152, HD), BF16),
        "reorder": ((IMG, HD), F32),
        "part": ((32, 32, HD), BF16),
        "part_in": ((32, 32, HD), BF16),
        "att_txt": ((4, TXT, HD), BF16),
        "atx": ((4, TXT, HD), BF16),
        "gown": ((32, HD), BF16),
        "gall": ((32, 32, HD), BF16),
        "gup": ((CH, HD), F32),
        "order": ((1024, HD), F32),
        "gpu": ((1024, HD), BF16),
        "do": ((1152, HD), BF16),
        "dk": ((4096, HD), F32),
        "dv": ((4096, HD), F32),
        "dq": ((4, IMG, HD), F32),
        "dqs": ((512, HD), F32),
        "ex": ((4, IMG, HD), F32),
        "dpre": ((16, IMG, HD), BF16),
        "grads": ((1024, 384), BF16),
        "small_u": ((HD, 384), F32),
        "low_u": ((4, 32, 384), BF16),
        "low_u_in": ((4, 32, 384), BF16),
        "small": ((HD, 512), F32),
        "low_d": ((4, 32, 512), BF16),
        "low_d_in": ((4, 32, 512), BF16),
        "wide_u": ((32, 32, HD), BF16),
        "wide_u_in": ((32, 32, HD), BF16),
        "base_d": ((32, D), F32),
        "wide_d": ((32, 32, HD), BF16),
        "wide_d_in": ((32, 32, HD), BF16),
        "mixed": ((8, 4, D), BF16),
        "mixed_in": ((8, 4, D), BF16),
        "conv": ((4, 80, HD), BF16),
        "conv_in": ((4, 80, HD), BF16),
        "conv_a": ((80, HD), BF16),
        "conv_sx": ((8, 80, HD), BF16),
        "conv_b": ((80, HD), BF16),
        "conv_gr": ((4, 80, HD), BF16),
        "conv_c": ((80, HD), BF16),
    }
    sems = {"local": (6,), "s_wide_u": (2, 8), "s_wide_d": (2, 8)}
    for name in (
        ("lat", "off", "text", "do", "tgrad", "lats", "kv", "qd", "part", "atx", "up", "hu", "su")
        + ("mix", "hd", "sd", "c1", "c2", "c3", "c4")
    ):
        sems["s_" + name] = (2,)
    names = list(inputs) + list(outs) + list(scratch) + list(sems)
    hbm = {"w_down", "w_up", "w_query", "w_key", "w_value", "w_out"}
    specs = []
    for name in inputs:
        kind = pl.ANY if name in hbm else pltpu.SMEM if name == "offset" else pltpu.VMEM
        specs.append(pl.BlockSpec(memory_space=kind))
    return pl.pallas_call(
        functools.partial(whole_kernel, names),
        out_shape=[sds(*v) for v in outs.values()],
        in_specs=specs,
        out_specs=vmem(len(outs)),
        scratch_shapes=[space(*v) for v in scratch.values()] + [dma(v) for v in sems.values()],
        compiler_params=pltpu.CompilerParams(
            collective_id=cid, has_side_effects=True, vmem_limit_bytes=61 * 2**20
        ),
    )(*inputs.values())


def results_kernel(pred, text, down, up, conv, out, *results):
    for src, dst in zip((pred, text), results[:2]):
        dst[0] = src[...]
    for src, dst in zip((down, up, conv), results[2:5]):
        dst[...] = src[...].astype(F32)
    results[5][...] = out[...]


def results(*arrays):
    sds = jax.ShapeDtypeStruct
    shapes = [
        sds((1, 2, PW * CH), BF16),
        sds((1, 4, D), BF16),
        sds((HD, D), F32),
        sds((D, HD), F32),
        sds((288, HD), F32),
        sds((CH, HD), F32),
    ]
    return pl.pallas_call(
        results_kernel,
        out_shape=shapes,
        in_specs=vmem(6),
        out_specs=vmem(6),
        compiler_params=pltpu.CompilerParams(vmem_limit_bytes=60 * 2**20),
    )(*arrays)


def rope_base():
    half = HD // 2
    freq = np.exp(-(2.0 * np.arange(half) / HD) * math.log(ROPE_BASE))
    slot = np.arange(IMG)
    position = (slot % PH) * PW + slot // PH
    angle = position[:, None] * freq[None, :]
    cosine = np.concatenate([np.cos(angle), np.cos(angle)], axis=1)
    sine = np.concatenate([-np.sin(angle), np.sin(angle)], axis=1)
    return jnp.asarray(np.stack([cosine, sine]).astype(np.float32))


def shards(
    text_tokens,
    latent,
    image_offset,
    norm_gain,
    w_query,
    w_key,
    w_value,
    w_out,
    w_down_conv,
    w_down_proj,
    w_up_proj,
    w_up_out,
    pred_grad,
    text_grad,
):
    pred, text_out, grad_down_proj, grad_up_proj, grad_conv, grad_out = whole(
        {
            "offset": image_offset,
            "text": text_tokens[0],
            "tgrad": text_grad[0],
            "lat": latent[0],
            "gain": norm_gain,
            "pgrad": pred_grad[0],
            "wconv": w_down_conv,
            "w_uo": w_up_out.T,
            "base": rope_base(),
            "w_down": w_down_proj,
            "w_up": w_up_proj,
            "w_query": w_query,
            "w_key": w_key,
            "w_value": w_value,
            "w_out": w_out,
        },
        1,
    )
    pred, text_out, grad_down_proj, grad_up_proj, grad_conv, grad_out = results(
        pred, text_out, grad_down_proj, grad_up_proj, grad_conv, grad_out
    )
    return pred, text_out, grad_conv, grad_down_proj, grad_up_proj, grad_out.T


def solution(mesh):
    placed = (
        P("sy", "sx", None),
        P("sy", "sx", None),
        P("sy"),
        P(),
        P(None, "sx"),
        P(None, "sx"),
        P(None, "sx"),
        P("sx", None),
        P(),
        P(),
        P(),
        P(),
        P("sy", "sx", None),
        P("sy", "sx", None),
    )
    return jax.shard_map(
        shards,
        mesh=mesh,
        in_specs=placed,
        out_specs=(P("sy", "sx", None), P("sy", "sx", None), P(), P(), P(), P()),
        check_vma=False,
    )
```

```python
import functools
import math
import types

import jax
import jax.numpy as jnp
import numpy as np
from jax import lax
from jax.experimental import pallas as pl
from jax.experimental.pallas import tpu as pltpu
from jax.sharding import PartitionSpec as P

MESH = pl.DeviceIdType.MESH
F32 = jnp.float32
BF16 = jnp.bfloat16
HD = 128
SB = 288
TXT = 32
IMG = 256
PH = 16
PW = 16
CH = 32
D = 4096
EPS = 1e-05
NEG = -1e30
LOG2E = math.log2(math.e)
SCALE = HD ** (-0.5)
ROPE_BASE = 500000.0
SIZES = {"sx": 8, "sy": 16, "group": 4, "head": 4, "team": 32}
NT = (((1,), (1,)), ((), ()))
TN = (((0,), (0,)), ((), ()))


def dot(a, b, dims=(((1,), (0,)), ((), ()))):
    return lax.dot_general(a, b, dims, preferred_element_type=F32)


def vmem(count):
    return [pl.BlockSpec(memory_space=pltpu.VMEM)] * count


def mod(a, n):
    return a % n if isinstance(a, int) else lax.rem(a, n)


def div(a, n):
    return a // n if isinstance(a, int) else lax.div(a, n)


def sy_of(g, i):
    if isinstance(i, int):
        return 2 * g + i if i < 2 else 12 - 2 * g + i
    return jnp.where(i < 2, 2 * g + i, 12 - 2 * g + i)


def split_sy(sy):
    low = sy < 8
    g = jnp.where(low, div(sy, 2), div(15 - sy, 2))
    i = mod(sy, 2) + jnp.where(low, 0, 2)
    return g, i


def ring(kind):
    sx = lax.axis_index("sx")
    sy = lax.axis_index("sy")
    g, i = split_sy(sy)
    if kind == "sx":
        return sx, lambda o: (mod(sx + o, 8), sy, mod(sx + o, 8))
    if kind == "sy":
        return sy, lambda o: (sx, mod(sy + o, 16), mod(sy + o, 16))
    if kind == "group":
        return i, lambda o: (sx, sy_of(g, mod(i + o, 4)), mod(i + o, 4))
    if kind == "head":
        return g, lambda o: (sx, sy_of(mod(g + o, 4), i), mod(g + o, 4))
    e = i * 8 + sx

    def peer(o):
        f = mod(e + o, 32)
        return mod(f, 8), sy_of(g, div(f, 8)), f

    return e, peer


def remote(src, dst, send, recv, to):
    copy = pltpu.make_async_remote_copy(
        src_ref=src,
        dst_ref=dst,
        send_sem=send,
        recv_sem=recv,
        device_id=to,
        device_id_type=MESH,
    )
    copy.start()
    return copy


class Fan:
    def __init__(self, kind, source, land, sems, slot_of=None):
        own, peer = ring(kind)
        self.land = land.at[pl.ds(0, SIZES[kind] - 1)]
        self.sems = sems

        @pl.loop(1, SIZES[kind])
        def _(o):
            tx, ty, to = peer(o)
            src = source if slot_of is None else source.at[slot_of(ty, to)]
            remote(src, land.at[own], sems.at[0], sems.at[1], (tx, ty))

    def arrived(self):
        pltpu.make_async_copy(self.land, self.land, self.sems.at[1]).wait()

    def sent(self):
        pltpu.make_async_copy(self.land, self.land, self.sems.at[0]).wait()


class Team:
    def __init__(self, source, land, sems):
        sy = lax.axis_index("sy")
        self.g, i = split_sy(sy)
        self.own = i * 8 + lax.axis_index("sx")
        self.source = source
        self.slots = land
        self.land = land.at[pl.ds(0, 31)]
        self.sems = sems

    def push(self, f):
        @pl.when(f != self.own)
        def _():
            to = (mod(f, 8), sy_of(self.g, div(f, 8)))
            remote(
                self.source.at[f], self.slots.at[self.own], self.sems.at[0], self.sems.at[1], to
            )

    def keep(self):
        self.slots[self.own] = self.source[self.own]

    arrived = Fan.arrived
    sent = Fan.sent


def sigmoid(v):
    return 1.0 / (1.0 + jnp.exp(-v))


def turn(v, cosine, sine):
    return v * cosine + pltpu.roll(v, 64, 1) * sine


def trig(shape, position):
    lane = lax.broadcasted_iota(jnp.int32, shape, 1)
    step = (lane % 64).astype(F32)
    angle = position * jnp.exp(step * (-2.0 / HD * math.log(ROPE_BASE)))
    sine = jnp.sin(angle)
    return jnp.cos(angle), jnp.where(lane < 64, -sine, sine)


def tables(j, phase_ref, base_ref):
    pc = phase_ref[0, pl.ds(j, 1), :]
    ps = phase_ref[1, pl.ds(j, 1), :]
    bc = base_ref[0]
    bs = base_ref[1]
    return pc * bc - ps * bs, ps * bc + pc * bs


def row_sum(v):
    return dot(v.astype(BF16), jnp.ones((HD, HD), BF16))


def row_scale(da, wd):
    both = dot(da, wd)
    dawd = both[:, :HD] + both[:, HD:]
    return dawd, lax.rsqrt(row_sum(dawd * da.astype(F32)) * (1.0 / D) + EPS)


def lanes(column):
    return column.T[:1, :]


def place(x, y, z, core):
    return 2 * x + mod(z, 2), 4 * y + 2 * div(z, 2) + core


class Spread:
    def __init__(self, every, sems):
        self.every = every
        self.sems = sems
        sx = lax.axis_index("sx")
        sy = lax.axis_index("sy")
        self.core = mod(sy, 2)
        x = div(sx, 2)
        y = div(sy, 4)
        z = 2 * mod(div(sy, 2), 2) + mod(sx, 2)
        self.even = self.core == 0
        self.p1 = jnp.where(self.even, x, z)
        self.p2 = jnp.where(self.even, y, x)
        self.p3 = jnp.where(self.even, z, y)
        self.twin = place(x, y, z, 1 - self.core)
        self.here = every.at[self.core]
        self.spot = (self.p3 * 4 + self.p2) * 4 + self.p1
        self.live = []

    def chip(self, a, b, c):
        a = mod(a, 4)
        b = mod(b, 4)
        c = mod(c, 4)
        even = self.even
        return place(
            jnp.where(even, a, b), jnp.where(even, b, c), jnp.where(even, c, a), self.core
        )

    def send(self, ref, n, to):
        copy = remote(ref, ref, self.sems.at[0, n], self.sems.at[1, n], to)
        self.live.append(copy)
        return copy

    def slab(self, p):
        return self.here.at[pl.ds(mod(p, 4) * 16, 16)]

    def plane(self, block):
        self.every[self.core, self.spot] = block
        mine = self.here.at[self.spot]

        @pl.loop(1, 16)
        def _(o):
            to = self.chip(self.p1 + mod(o, 4), self.p2 + div(o, 4), self.p3)
            remote(mine, mine, self.sems.at[0, 0], self.sems.at[1, 0], to)

    def slabs(self):
        plane = self.here.at[pl.ds(0, 15)]
        pltpu.make_async_copy(plane, plane, self.sems.at[1, 0]).wait()
        own = self.slab(self.p3)
        self.wave = [self.send(own, o, self.chip(self.p1, self.p2, self.p3 + o)) for o in (1, 3, 2)]
        self.twins = [self.send(own, 4, self.twin)]

    def pass_on(self):
        for o, copy in zip((1, 3, 2), self.wave):
            copy.wait_recv()
            self.twins.append(self.send(self.slab(self.p3 + 4 - o), 4 + o, self.twin))

    def arrived(self):
        for copy in self.twins:
            copy.wait_recv()

    def sent(self):
        plane = self.here.at[pl.ds(0, 15)]
        pltpu.make_async_copy(plane, plane, self.sems.at[0, 0]).wait()
        for copy in self.live:
            copy.wait_send()


def greet(wide):
    barrier = pltpu.get_barrier_semaphore()
    for kind in ("team", "sy"):
        _, peer = ring(kind)

        @pl.loop(1, SIZES[kind])
        def _(o):
            tx, ty, _ = peer(o)
            pl.semaphore_signal(barrier, inc=1, device_id=(tx, ty), device_id_type=MESH)

    @pl.loop(1, 16)
    def _(o):
        to = wide.chip(wide.p1 + mod(o, 4), wide.p2 + div(o, 4), wide.p3)
        pl.semaphore_signal(barrier, inc=1, device_id=to, device_id_type=MESH)

    @pl.loop(1, 4)
    def _(o):
        to = wide.chip(wide.p1, wide.p2, wide.p3 + o)
        pl.semaphore_signal(barrier, inc=1, device_id=to, device_id_type=MESH)

    return lambda: pl.semaphore_wait(barrier, 31 + 15 + 15 + 3)


def masks(r, g, members):
    block = lax.broadcasted_iota(jnp.int32, (16, HD), 0).astype(F32)
    cosine, sine = trig((16, HD), block * float(SB) + jnp.max(r.offs[...], axis=1))
    r.phase[0] = cosine
    r.phase[1] = sine
    starts = [r.offs[b][:1, :] for b in members]
    row = lax.broadcasted_iota(jnp.int32, (512, TXT), 0)
    query = lax.broadcasted_iota(jnp.int32, (512, TXT), 1)
    for m in range(4):
        b = members[m]
        seen = (row // TXT < b) | ((row // TXT == b) & (row % TXT <= query))
        r.bias_tt[:, m * TXT : (m + 1) * TXT] = jnp.where(seen, 0.0, NEG)
    lane = lax.broadcasted_iota(jnp.int32, (8, HD), 1)
    start = starts[0]
    owner = jnp.full((8, HD), members[0], jnp.int32)
    for m in range(1, 4):
        start = jnp.where(lane // TXT == m, starts[m], start)
        owner = jnp.where(lane // TXT == m, members[m], owner)
    late = jnp.where((lane % TXT).astype(F32) >= start, 1.0, 0.0)
    r.vis[...] = late + owner.astype(F32)
    lane = lax.broadcasted_iota(jnp.int32, (512, HD), 1)
    row = lax.broadcasted_iota(jnp.int32, (512, HD), 0)
    start = jnp.broadcast_to(starts[0], (512, HD))
    owner = jnp.full((512, HD), members[0], jnp.int32)
    for m in range(1, 4):
        start = jnp.where(lane == m, starts[m], start)
        owner = jnp.where(lane == m, members[m], owner)
    seen = (row // TXT < owner) | ((row // TXT == owner) & ((row % TXT).astype(F32) < start))
    r.bias_ti[...] = jnp.where(seen, 0.0, NEG)


def down_block(r):
    r.wpad[...] = jnp.zeros_like(r.wpad)
    for tap in range(3):
        r.wpad[tap * 128 : tap * 128 + 96, :] = r.wconv[tap * 96 : tap * 96 + 96, :].astype(F32)
    mid = r.lat_all[...].reshape(256, PW * CH).astype(F32)
    mid = pltpu.roll(jnp.concatenate([mid, jnp.zeros((256, HD), F32)], axis=1), CH, 1)
    row = lax.broadcasted_iota(jnp.int32, mid.shape, 0) % PH
    r.wide[0] = jnp.where(row == 0, 0.0, pltpu.roll(mid, 1, 0))
    r.wide[1] = mid
    r.wide[2] = jnp.where(row == PH - 1, 0.0, pltpu.roll(mid, 16 * PH - 1, 0))
    weight = r.wpad[...].astype(BF16)
    for c in range(PW):
        for tap in range(3):
            r.patches[c, :, tap * 128 : tap * 128 + 128] = r.wide[
                tap, :, c * CH : c * CH + 128
            ].astype(BF16)
        pre = dot(r.patches[c], weight)
        sig = sigmoid(pre)
        r.da[:, c * PH : c * PH + PH, :] = (pre * sig).astype(BF16).reshape(16, PH, HD)
        r.sp[:, c * PH : c * PH + PH, :] = (
            (sig * (1.0 + pre * (1.0 - sig))).astype(BF16).reshape(16, PH, HD)
        )


def project(r, members):
    mix_kv = r.mix[:, HD:]
    mix_q = r.mix[:, :HD]
    wd = r.wd[...]

    @pl.loop(0, 4)
    def _(n):
        da = r.da[pl.ds(4 * n, 4)].reshape(4 * IMG, HD)
        _, inv = row_scale(da, wd)
        scaled = (da.astype(F32) * inv).astype(BF16)
        kv = dot(scaled, mix_kv)
        whole = pl.ds(pl.multiple_of(n * 1024, 1024), 1024)
        r.vt[:, whole] = dot(mix_kv[:, HD:], scaled, (((0,), (1,)), ((), ()))).astype(BF16)
        for m in range(4):
            j = 4 * n + m
            cosine, sine = tables(j, r.phase, r.base)
            rows = pl.ds(pl.multiple_of(j * IMG, IMG), IMG)
            part = kv[m * IMG : (m + 1) * IMG, :]
            r.k[rows, :] = turn(part[:, :HD], cosine, sine).astype(BF16)
            r.v[rows, :] = part[:, HD:].astype(BF16)

    for m in range(4):
        r.da_own[m * IMG : (m + 1) * IMG, :] = r.da[members[m]]
    da = r.da_own[...]
    _, inv = row_scale(da, wd)
    queries = dot((da.astype(F32) * inv).astype(BF16), mix_q) * (SCALE * LOG2E)
    for m in range(4):
        rows = slice(m * IMG, (m + 1) * IMG)
        cosine, sine = tables(members[m], r.phase, r.base)
        r.q[rows, :] = turn(queries[rows, :], cosine, sine).astype(BF16)


def tile_rows(j):
    return pl.ds(pl.multiple_of(j * 512, 512), 512)


def absorb(state, scores, vt, e_ref, m_ref):
    top = jnp.max(scores, axis=0, keepdims=True)
    new = top if state is None else jnp.maximum(state[0], top)
    raised = jnp.exp2(scores - new)
    low = raised.astype(BF16)
    e_ref[...] = low
    m_ref[...] = jnp.broadcast_to(new, m_ref.shape)
    total = jnp.sum(raised, axis=0, keepdims=True)
    mixed = dot(vt, low)
    if state is None:
        return new, total, mixed
    old = jnp.exp2(state[0] - new)
    return new, state[1] * old + total, state[2] * old + mixed


def conclude(r, p, width, state):
    peak, total, acc = state
    r.att[p * 512 : p * 512 + width, :] = (acc / total).T.astype(BF16)
    r.lse[p, :, :width] = jnp.broadcast_to(peak + jnp.log2(total), (8, width))


def diagonal_mask(scores):
    bottom = lax.broadcasted_iota(jnp.int32, scores.shape, 0) >= IMG
    left = lax.broadcasted_iota(jnp.int32, scores.shape, 1) < IMG
    return jnp.where(bottom & left, NEG, scores)


def attend_images(r, p, diagonal, text_ready):
    q = r.q[p * 512 : p * 512 + 512, :]
    base = 4 * p

    def tile(j):
        return dot(r.k[tile_rows(j), :], q, NT)

    state = absorb(
        None,
        diagonal_mask(tile(diagonal)),
        r.vt[:, tile_rows(diagonal)],
        r.e_img.at[base + diagonal],
        r.m_img.at[base + diagonal],
    )

    def body(j, state):
        return absorb(
            state, tile(j), r.vt[:, tile_rows(j)], r.e_img.at[base + j], r.m_img.at[base + j]
        )

    state = lax.fori_loop(0, diagonal, body, state)
    text_ready()
    scores = dot(r.kt[...], q, NT)
    bias = jnp.concatenate(
        [
            jnp.broadcast_to(r.bias_ti[:, 2 * p + half : 2 * p + half + 1], (512, IMG))
            for half in range(2)
        ],
        axis=1,
    )
    scores = jnp.where(bias < 0.0, NEG, scores)
    state = absorb(state, scores, r.vtt[...], r.e_txt.at[p], r.m_txt.at[p])
    conclude(r, p, 512, state)


def attend_text(r, count, kept):
    q = r.q[1024:, :]
    vis = r.vis[:1, :]
    scores = jnp.where(r.bias_tt[...] < 0.0, NEG, dot(r.kt[...], q, NT))
    state = absorb(None, scores, r.vtt[...], r.e_q.at[8], r.m_q.at[8])

    def body(j, state):
        scores = dot(r.k[tile_rows(j), :], q, NT)
        block = 2 * j + (lax.broadcasted_iota(jnp.int32, scores.shape, 0) >= IMG).astype(jnp.int32)
        scores = jnp.where(block.astype(F32) < vis, scores, NEG)
        return absorb(state, scores, r.vt[:, tile_rows(j)], r.e_q.at[j], r.m_q.at[j])

    conclude(r, 2, 128, lax.fori_loop(0, count, body, state))


def normalise(e_ref, m_ref, lse):
    factor = jnp.exp2(m_ref[:1, :] - lse)
    e_ref[...] = (e_ref[...].astype(F32) * factor).astype(BF16)


def backward_rows(r, p, width):
    rows = slice(p * 512, p * 512 + width)
    q = r.q[rows, :]
    do = r.do[rows, :]
    sums = jnp.sum(do.astype(F32) * r.att[rows, :].astype(F32), axis=1, keepdims=True)
    return q, do, lanes(jnp.broadcast_to(sums, (width, HD)))


def backward_images(r, p, diagonal, members):
    q, do, delta = backward_rows(r, p, 512)
    base = 4 * p

    probs = r.e_txt[p].astype(F32)
    grad = (probs * (dot(r.vtx[...], do, NT) - delta)).astype(BF16)
    r.dqs[...] = dot(grad, r.kt[...], TN)

    @pl.loop(0, diagonal + 1)
    def _(j):
        at = tile_rows(j)
        keys = r.k[at, :]
        probs = r.e_img[base + j]
        grad = (probs.astype(F32) * (dot(r.v[at, :], do, NT) - delta)).astype(BF16)
        r.dv[at, :] += dot(probs, do)
        r.dk[at, :] += dot(grad, q)
        r.dqs[...] += dot(grad, keys, TN)

    for half in range(2):
        r.dq[2 * p + half] = r.dqs[half * IMG : (half + 1) * IMG, :]


def backward_text(r, count):
    q, do, delta = backward_rows(r, 2, 128)

    @pl.loop(0, count)
    def _(j):
        at = tile_rows(j)
        probs = r.e_q[j]
        grad = (probs.astype(F32) * (dot(r.v[at, :], do, NT) - delta)).astype(BF16)
        r.dv[at, :] += dot(probs, do)
        r.dk[at, :] += dot(grad, q)


def image_grads(r, g):
    wd = r.wd[...]
    mix = r.mix[...]
    r.small[...] = jnp.zeros_like(r.small)

    @pl.loop(0, 4)
    def _(n):
        da = r.da[pl.ds(4 * n, 4)].reshape(4 * IMG, HD)
        da_wide = da.astype(F32)
        dawd, inv = row_scale(da, wd)
        extra = []
        for k in range(4):
            j = 4 * n + k
            group, m = split_sy(j)
            ours = (group == g).astype(F32)
            cosine, sine = tables(j, r.phase, r.base)
            at = pl.ds(pl.multiple_of(j * IMG, IMG), IMG)
            rows = slice(k * IMG, (k + 1) * IMG)
            gq = turn(r.dq[m] * (ours * SCALE), cosine, -sine)
            gk = turn(r.dk[at, :] * (1.0 / LOG2E), cosine, -sine)
            r.grads[rows, :HD] = gq.astype(BF16)
            r.grads[rows, HD : 2 * HD] = gk.astype(BF16)
            r.grads[rows, 2 * HD :] = r.dv[at, :].astype(BF16)
            extra.append(r.ex[m] * ours)
        grads = r.grads[...]
        back = dot(grads, mix, NT)
        cube = (inv * inv * inv) * (row_sum(back * da_wide) * (1.0 / D))
        slope = r.sp[pl.ds(4 * n, 4)].reshape(4 * IMG, HD).astype(F32)
        grad = (inv * back - cube * dawd + jnp.concatenate(extra, axis=0)) * slope
        r.dpre[pl.ds(4 * n, 4)] = grad.astype(BF16).reshape(4, IMG, HD)
        r.small[:, :384] += dot((da_wide * inv).astype(BF16), grads, TN)
        r.small[:, 384:] += dot((da_wide * cube).astype(BF16), da, TN)


def conv_grad(r):
    total = jnp.zeros((384, HD), F32)
    for c in range(PW):
        grad = r.dpre[:, c * PH : c * PH + PH, :].reshape(256, HD)
        total = total + dot(r.patches[c], grad, TN)
    rows = [total[tap * 128 : tap * 128 + 96, :] for tap in range(3)] + [r.gup[...]]
    whole = jnp.concatenate(rows, axis=0).astype(BF16)
    for n in range(4):
        r.conv[n] = whole[80 * n : 80 * n + 80, :]


def block_of(group, e):
    sx = e % 8
    sy = sy_of(group, e // 8)
    x = sx // 2
    y = sy // 4
    z = 2 * ((sy // 2) % 2) + sx % 2
    core = sy % 2
    return core, (z * 4 + y) * 4 + x if core == 0 else (y * 4 + x) * 4 + z


def lay_up(r):
    for e in range(32):
        cols = [r.every_u[block_of(group, e)].astype(F32) for group in range(4)]
        r.grad_up[e * HD : (e + 1) * HD, :] = jnp.concatenate(cols, axis=0).T.astype(BF16)


def lay_down(r):
    for e in range(32):
        for group in range(4):
            r.grad_down[32 * group : 32 * group + 32, e * HD : (e + 1) * HD] = r.every_d[
                block_of(group, e)
            ]


def whole_kernel(names, *refs):
    r = types.SimpleNamespace(**dict(zip(names, refs)))
    sx = lax.axis_index("sx")
    sy = lax.axis_index("sy")
    g, head = split_sy(sy)
    members = [sy_of(g, m) for m in range(4)]
    mine = pl.ds(pl.multiple_of(head * HD, HD), HD)
    loads = []
    for at, (src, dst) in enumerate(
        [
            (r.w_down, r.dn),
            (r.w_up, r.up),
            (r.w_query, r.wq),
            (r.w_key, r.wk),
            (r.w_value, r.wv),
            (r.w_out, r.wo),
        ]
    ):
        copy = pltpu.make_async_copy(src, dst, r.local.at[at])
        copy.start()
        loads.append(copy)
    wide_u = Spread(r.every_u, r.s_wide_u)
    wide_d = Spread(r.every_d, r.s_wide_d)
    all_here = greet(wide_u)
    r.own_off[...] = jnp.full((8, HD), r.offset[0].astype(F32))
    for k in range(2):
        row = r.pgrad[...].astype(F32)[k : k + 1, :]
        for c in range(PW):
            r.pg[k * PW + c : k * PW + c + 1, :] = row[:, c * CH : c * CH + CH]
    gain = r.gain[...].astype(F32).reshape(1, D)
    r.gain_row[...] = gain
    loads[0].wait()
    loads[1].wait()
    down = r.dn[...]
    both = dot(down, down, NT)
    high = both.astype(BF16)
    r.wd[:, :HD] = high
    r.wd[:, HD:] = (both - high.astype(F32)).astype(BF16)
    r.wu[...] = dot(down, r.up[...]).astype(BF16)
    scaled = (down.astype(F32) * gain).astype(BF16)
    all_here()

    lat = Fan("sx", r.lat, r.lat_in, r.s_lat)
    text = Fan("sx", r.text, r.text_in, r.s_text)
    offs = Fan("sy", r.own_off, r.offs, r.s_off)
    r.offs[sy] = r.own_off[...]
    r.lat_in[sx] = r.lat[...]
    r.text_in[sx] = r.text[...]

    lat.arrived()
    for n in range(8):
        r.rows_lat[2 * n : 2 * n + 2, :] = r.lat_in[n].astype(F32)
    r.row_lat[...] = r.rows_lat[...].astype(BF16)
    lats = Fan("sy", r.row_lat, r.lat_all, r.s_lats)
    r.lat_all[sy] = r.row_lat[...]
    for n, weight in enumerate([r.wq, r.wk, r.wv]):
        loads[2 + n].wait()
        r.mix[:, n * HD : (n + 1) * HD] = dot(scaled, weight[:, mine]).astype(BF16)
    loads[5].wait()
    r.nt[...] = dot(r.up[...], r.wo[mine, :], (((0,), (1,)), ((), ()))).astype(BF16)

    text.arrived()
    for n in range(8):
        r.rows_text[4 * n : 4 * n + 4, :] = r.text_in[n].astype(F32)
    wide = r.rows_text[...]
    inverse = lax.rsqrt(jnp.mean(wide * wide, axis=1, keepdims=True) + EPS)
    normed = (wide * inverse * gain).astype(BF16)
    token = lax.broadcasted_iota(jnp.int32, (TXT, HD), 0).astype(F32)
    shift = jnp.where(token >= r.own_off[:1, :], float(IMG), 0.0)
    cosine, sine = trig((TXT, HD), token + shift + (sy * SB).astype(F32))
    query = dot(normed, r.wq[...])
    key = dot(normed, r.wk[...])
    value = dot(normed, r.wv[...])
    for h in range(4):
        at = slice(h * HD, (h + 1) * HD)
        r.kv_out[h, :, :HD] = turn(key[:, at], cosine, sine).astype(BF16)
        r.kv_out[h, :, HD:] = value[:, at].astype(BF16)
        turned = turn(query[:, at], cosine, sine)
        r.qd_out[h] = (turned * (SCALE * LOG2E)).astype(BF16)
    kvs = Fan("sy", r.kv_out, r.kv_in, r.s_kv, lambda ty, to: split_sy(ty)[1])
    qds = Fan("group", r.qd_out, r.qd_in, r.s_qd, lambda ty, to: to)
    r.kv_in[sy] = r.kv_out[head]
    r.qd_in[head] = r.qd_out[head]

    offs.arrived()
    masks(r, g, members)

    lats.arrived()
    tgrad = Fan("sx", r.tgrad, r.tgrad_in, r.s_tgrad)
    r.tgrad_in[sx] = r.tgrad[...]
    down_block(r)

    project(r, members)

    def text_ready():
        kvs.arrived()
        qds.arrived()
        kv = r.kv_in[...].reshape(512, 256)
        r.kt[...] = kv[:, :HD]
        r.vtx[...] = kv[:, HD:]
        r.vtt[...] = kv[:, HD:].astype(F32).T.astype(BF16)
        r.q[1024:, :] = r.qd_in[...].reshape(128, HD)

    def add_part(m):
        r.reorder[...] = dot(r.att[m * IMG : (m + 1) * IMG, :], r.nt[...], NT) + dot(
            r.da_own[m * IMG : (m + 1) * IMG, :], r.wu[...]
        ) * (1.0 / 32.0)
        for n in range(8):
            for k in range(2):
                r.part[8 * m + n, k * PW : (k + 1) * PW, :] = r.reorder[
                    pl.ds(2 * n + k, PW, stride=PH), :
                ].astype(BF16)

    parts = Team(r.part, r.part_in, r.s_part)
    e = parts.own
    attend_images(r, 1, 7 - g, text_ready)
    add_part(2)
    add_part(3)

    @pl.loop(0, 16)
    def _(o):
        parts.push(16 + mod(e + o, 16))

    attend_images(r, 0, g, lambda: None)
    add_part(0)
    add_part(1)

    @pl.loop(0, 16)
    def _(o):
        parts.push(mod(e + o, 16))

    parts.keep()

    tgrad.arrived()
    for n in range(8):
        r.rows_grad[4 * n : 4 * n + 4, :] = r.tgrad_in[n].astype(F32)
    outer = dot(r.rows_grad[...].astype(BF16), r.wo[...], NT)
    for h in range(4):
        r.d_out[h] = outer[:, h * HD : (h + 1) * HD].astype(BF16)
    outers = Fan("group", r.d_out, r.d_in, r.s_do, lambda ty, to: to)
    r.d_in[head] = r.d_out[head]
    attend_text(r, 8 - g, None)
    for m in range(4):
        r.att_txt[m] = r.att[1024 + m * TXT : 1024 + (m + 1) * TXT, :]
    atx = Fan("group", r.att_txt, r.atx, r.s_atx, lambda ty, to: to)
    r.atx[head] = r.att_txt[head]
    r.dk[...] = jnp.zeros_like(r.dk)
    r.dv[...] = jnp.zeros_like(r.dv)
    parts.arrived()
    pre = jnp.sum(r.part_in[...].astype(F32), axis=0)
    sig = sigmoid(pre)
    act = (pre * sig).astype(BF16)
    slope = sig * (1.0 + pre * (1.0 - sig))
    pgrad = r.pg[...].astype(BF16)
    r.gown[...] = (dot(pgrad, r.w_uo[...]) * slope).astype(BF16)
    ups = Fan("team", r.gown, r.gall, r.s_up)
    r.gall[e] = r.gown[...]
    pred = dot(act, r.w_uo[...], NT)
    for k in range(2):
        for c in range(PW):
            r.pred_rows[k : k + 1, c * CH : c * CH + CH] = pred[k * PW + c : k * PW + c + 1, :]
    r.pred[...] = r.pred_rows[...].astype(BF16)
    r.gup[...] = dot(pgrad, act, TN)
    for p, diagonal in ((0, g), (1, 7 - g)):
        lse = r.lse[p, :1, :]

        @pl.loop(0, diagonal + 1)
        def _(j):
            normalise(r.e_img.at[4 * p + j], r.m_img.at[4 * p + j], lse)

        normalise(r.e_txt.at[p], r.m_txt.at[p], lse)

    @pl.loop(0, 8 - g)
    def _(j):
        normalise(r.e_q.at[j], r.m_q.at[j], r.lse[2, :1, :HD])

    outers.arrived()
    r.do[1024:, :] = r.d_in[...].reshape(128, HD)
    backward_text(r, 8 - g)

    ups.arrived()
    for m in range(4):
        for n in range(8):
            nat = r.gall[8 * m + n].astype(F32)
            for k in range(2):
                r.order[pl.ds(m * IMG + 2 * n + k, PW, stride=PH), :] = nat[
                    k * PW : (k + 1) * PW, :
                ]
    r.gpu[...] = r.order[...].astype(BF16)
    r.do[:1024, :] = dot(r.gpu[...], r.nt[...]).astype(BF16)

    gpu = r.gpu[...]
    grad = dot(gpu, r.wu[...], NT) * (1.0 / 32.0)
    for m in range(4):
        r.ex[m] = grad[m * IMG : (m + 1) * IMG, :]
    own = r.da_own[...]
    r.small_u[:, :HD] = dot(gpu, r.att[:1024, :], TN)
    r.small_u[:, HD : 2 * HD] = dot(gpu, own, TN) * (1.0 / 32.0)
    r.small_u[:, 2 * HD :] = dot(own, gpu, TN) * (1.0 / 32.0)
    for n in range(4):
        r.low_u[n] = r.small_u[32 * n : 32 * n + 32, :].astype(BF16)
    heads_u = Fan("head", r.low_u, r.low_u_in, r.s_hu, lambda ty, to: to)
    r.low_u_in[g] = r.low_u[g]

    backward_images(r, 0, g, members)

    atx.arrived()
    joined = jnp.concatenate([r.atx[h] for h in range(4)], axis=1)

    @pl.loop(0, 8)
    def _(c):
        at = pl.ds(pl.multiple_of(c * 512, 512), 512)
        out = dot(joined, r.wo[:, at])
        for n in range(8):
            r.mixed[n, :, at] = out[4 * n : 4 * n + 4, :].astype(BF16)

    heads_u.arrived()
    low_u = jnp.sum(r.low_u_in[...].astype(F32), axis=0).astype(BF16)

    sums_u = Team(r.wide_u, r.wide_u_in, r.s_su)

    @pl.loop(0, 8)
    def _(n):
        c = mod(n + div(e, 4), 8)
        at = pl.ds(pl.multiple_of(c * 512, 512), 512)
        grad = dot(low_u[:, :HD], r.wo[mine, at]) + dot(low_u[:, HD : 2 * HD], r.dn[:, at])
        for k in range(4):
            r.wide_u[4 * c + k] = grad[:, k * HD : (k + 1) * HD].astype(BF16)
            sums_u.push(4 * c + k)

    sums_u.keep()
    mixes = Fan("sx", r.mixed, r.mixed_in, r.s_mix, lambda ty, to: to)
    r.mixed_in[sx] = r.mixed[sx]

    backward_images(r, 1, 7 - g, members)

    sums_u.arrived()
    wide_u.plane(jnp.sum(r.wide_u_in[...].astype(F32), axis=0).astype(BF16))
    image_grads(r, g)

    for n in range(4):
        r.low_d[n] = r.small[32 * n : 32 * n + 32, :].astype(BF16)
    heads_d = Fan("head", r.low_d, r.low_d_in, r.s_hd, lambda ty, to: to)
    r.low_d_in[g] = r.low_d[g]
    wide_u.slabs()
    conv_grad(r)
    convs = Fan("head", r.conv, r.conv_in, r.s_c1, lambda ty, to: to)
    r.conv_in[g] = r.conv[g]

    @pl.loop(0, 8)
    def _(c):
        at = pl.ds(pl.multiple_of(c * 512, 512), 512)
        r.base_d[:, at] = dot(low_u[:, 2 * HD :], r.up[at, :], NT)

    heads_d.arrived()
    low = jnp.sum(r.low_d_in[...].astype(F32), axis=0).astype(BF16)

    sums_d = Team(r.wide_d, r.wide_d_in, r.s_sd)

    @pl.loop(0, 8)
    def _(n):
        c = mod(n + div(e, 4), 8)
        at = pl.ds(pl.multiple_of(c * 512, 512), 512)
        grad = dot(low[:, :HD], r.wq[at, mine], NT)
        grad = grad + dot(low[:, HD : 2 * HD], r.wk[at, mine], NT)
        grad = grad + dot(low[:, 2 * HD : 3 * HD], r.wv[at, mine], NT)
        grad = grad * r.gain_row[:, at]
        grad = grad + r.base_d[:, at]
        grad = grad - dot(low[:, 3 * HD :], r.dn[:, at])
        for k in range(4):
            r.wide_d[4 * c + k] = grad[:, k * HD : (k + 1) * HD].astype(BF16)
            sums_d.push(4 * c + k)

    sums_d.keep()
    convs.arrived()
    r.conv_a[...] = jnp.sum(r.conv_in[...].astype(F32), axis=0).astype(BF16)
    beside = Fan("sx", r.conv_a, r.conv_sx, r.s_c2)
    r.conv_sx[sx] = r.conv_a[...]
    mixes.arrived()
    total = r.text[...].astype(F32)
    for n in range(8):
        total = total + r.mixed_in[n].astype(F32)
    r.text_out[...] = total.astype(BF16)
    sums_d.arrived()
    wide_d.plane(jnp.sum(r.wide_d_in[...].astype(F32), axis=0).astype(BF16))
    beside.arrived()
    r.conv_b[...] = jnp.sum(r.conv_sx[...].astype(F32), axis=0).astype(BF16)
    along = Fan("group", r.conv_b, r.conv_gr, r.s_c3)
    r.conv_gr[head] = r.conv_b[...]
    wide_d.slabs()
    wide_u.pass_on()
    along.arrived()
    r.conv_c[...] = jnp.sum(r.conv_gr[...].astype(F32), axis=0).astype(BF16)
    across = Fan("head", r.conv_c, r.conv_all, r.s_c4)
    r.conv_all[g] = r.conv_c[...]
    wide_u.arrived()
    lay_up(r)
    wide_d.pass_on()
    across.arrived()
    for n in range(3):
        r.grad_conv[80 * n : 80 * n + 80, :] = r.conv_all[n].astype(F32)
    rest = r.conv_all[3].astype(F32)
    r.grad_conv[240:, :] = rest[:48, :]
    r.grad_out[...] = rest[48:, :]
    wide_d.arrived()
    lay_down(r)
    for fan in (
        lat,
        offs,
        text,
        tgrad,
        lats,
        kvs,
        qds,
        outers,
        parts,
        atx,
        ups,
        heads_u,
        sums_u,
        mixes,
        heads_d,
        convs,
        sums_d,
        beside,
        along,
        across,
    ):
        fan.sent()
    wide_u.sent()
    wide_d.sent()


def whole(inputs, cid):
    sds = jax.ShapeDtypeStruct
    dma = pltpu.SemaphoreType.DMA
    space = pltpu.VMEM
    outs = {
        "pred": ((2, PW * CH), BF16),
        "text_out": ((4, D), BF16),
        "grad_down": ((HD, D), BF16),
        "grad_up": ((D, HD), BF16),
        "grad_conv": ((288, HD), F32),
        "grad_out": ((CH, HD), F32),
    }
    scratch = {
        "conv_all": ((4, 80, HD), BF16),
        "gain_row": ((1, D), F32),
        "pg": ((32, CH), F32),
        "pred_rows": ((2, PW * CH), F32),
        "every_u": ((2, 64, 32, HD), BF16),
        "every_d": ((2, 64, 32, HD), BF16),
        "dn": ((HD, D), BF16),
        "up": ((D, HD), BF16),
        "wq": ((D, 512), BF16),
        "wk": ((D, 512), BF16),
        "wv": ((D, 512), BF16),
        "wo": ((512, D), BF16),
        "lat_in": ((8, 2, PW * CH), BF16),
        "text_in": ((8, 4, D), BF16),
        "tgrad_in": ((8, 4, D), BF16),
        "own_off": ((8, HD), F32),
        "offs": ((16, 8, HD), F32),
        "row_lat": ((PH, PW * CH), BF16),
        "rows_lat": ((PH, PW * CH), F32),
        "lat_all": ((16, PH, PW * CH), BF16),
        "rows_text": ((TXT, D), F32),
        "rows_grad": ((TXT, D), F32),
        "wd": ((HD, 256), BF16),
        "wu": ((HD, HD), BF16),
        "mix": ((HD, 384), BF16),
        "nt": ((HD, HD), BF16),
        "kv_out": ((4, TXT, 256), BF16),
        "qd_out": ((4, TXT, HD), BF16),
        "kv_in": ((16, TXT, 256), BF16),
        "qd_in": ((4, TXT, HD), BF16),
        "d_out": ((4, TXT, HD), BF16),
        "d_in": ((4, TXT, HD), BF16),
        "phase": ((2, 16, HD), F32),
        "bias_tt": ((512, 128), F32),
        "bias_ti": ((512, HD), F32),
        "vis": ((8, HD), F32),
        "wpad": ((384, HD), F32),
        "wide": ((3, 256, 640), F32),
        "patches": ((16, 256, 384), BF16),
        "da": ((16, 256, HD), BF16),
        "sp": ((16, 256, HD), BF16),
        "da_own": ((1024, HD), BF16),
        "k": ((4096, HD), BF16),
        "v": ((4096, HD), BF16),
        "vt": ((HD, 4096), BF16),
        "q": ((1152, HD), BF16),
        "kt": ((512, HD), BF16),
        "vtx": ((512, HD), BF16),
        "vtt": ((HD, 512), BF16),
        "e_img": ((12, 512, 512), BF16),
        "m_img": ((12, 8, 512), F32),
        "e_txt": ((2, 512, 512), BF16),
        "m_txt": ((2, 8, 512), F32),
        "e_q": ((9, 512, 128), BF16),
        "m_q": ((9, 8, 128), F32),
        "lse": ((3, 8, 512), F32),
        "att": ((1152, HD), BF16),
        "reorder": ((IMG, HD), F32),
        "part": ((32, 32, HD), BF16),
        "part_in": ((32, 32, HD), BF16),
        "att_txt": ((4, TXT, HD), BF16),
        "atx": ((4, TXT, HD), BF16),
        "gown": ((32, HD), BF16),
        "gall": ((32, 32, HD), BF16),
        "gup": ((CH, HD), F32),
        "order": ((1024, HD), F32),
        "gpu": ((1024, HD), BF16),
        "do": ((1152, HD), BF16),
        "dk": ((4096, HD), F32),
        "dv": ((4096, HD), F32),
        "dq": ((4, IMG, HD), F32),
        "dqs": ((512, HD), F32),
        "ex": ((4, IMG, HD), F32),
        "dpre": ((16, IMG, HD), BF16),
        "grads": ((1024, 384), BF16),
        "small_u": ((HD, 384), F32),
        "low_u": ((4, 32, 384), BF16),
        "low_u_in": ((4, 32, 384), BF16),
        "small": ((HD, 512), F32),
        "low_d": ((4, 32, 512), BF16),
        "low_d_in": ((4, 32, 512), BF16),
        "wide_u": ((32, 32, HD), BF16),
        "wide_u_in": ((32, 32, HD), BF16),
        "base_d": ((32, D), F32),
        "wide_d": ((32, 32, HD), BF16),
        "wide_d_in": ((32, 32, HD), BF16),
        "mixed": ((8, 4, D), BF16),
        "mixed_in": ((8, 4, D), BF16),
        "conv": ((4, 80, HD), BF16),
        "conv_in": ((4, 80, HD), BF16),
        "conv_a": ((80, HD), BF16),
        "conv_sx": ((8, 80, HD), BF16),
        "conv_b": ((80, HD), BF16),
        "conv_gr": ((4, 80, HD), BF16),
        "conv_c": ((80, HD), BF16),
    }
    sems = {"local": (6,), "s_wide_u": (2, 8), "s_wide_d": (2, 8)}
    for name in (
        ("lat", "off", "text", "do", "tgrad", "lats", "kv", "qd", "part", "atx", "up", "hu", "su")
        + ("mix", "hd", "sd", "c1", "c2", "c3", "c4")
    ):
        sems["s_" + name] = (2,)
    names = list(inputs) + list(outs) + list(scratch) + list(sems)
    hbm = {"w_down", "w_up", "w_query", "w_key", "w_value", "w_out"}
    specs = []
    for name in inputs:
        kind = pl.ANY if name in hbm else pltpu.SMEM if name == "offset" else pltpu.VMEM
        specs.append(pl.BlockSpec(memory_space=kind))
    return pl.pallas_call(
        functools.partial(whole_kernel, names),
        out_shape=[sds(*v) for v in outs.values()],
        in_specs=specs,
        out_specs=vmem(len(outs)),
        scratch_shapes=[space(*v) for v in scratch.values()] + [dma(v) for v in sems.values()],
        compiler_params=pltpu.CompilerParams(
            collective_id=cid, has_side_effects=True, vmem_limit_bytes=61 * 2**20
        ),
    )(*inputs.values())


def results_kernel(pred, text, down, up, conv, out, *results):
    for src, dst in zip((pred, text), results[:2]):
        dst[0] = src[...]
    for src, dst in zip((down, up, conv), results[2:5]):
        dst[...] = src[...].astype(F32)
    results[5][...] = out[...]


def results(*arrays):
    sds = jax.ShapeDtypeStruct
    shapes = [
        sds((1, 2, PW * CH), BF16),
        sds((1, 4, D), BF16),
        sds((HD, D), F32),
        sds((D, HD), F32),
        sds((288, HD), F32),
        sds((CH, HD), F32),
    ]
    return pl.pallas_call(
        results_kernel,
        out_shape=shapes,
        in_specs=vmem(6),
        out_specs=vmem(6),
        compiler_params=pltpu.CompilerParams(vmem_limit_bytes=60 * 2**20),
    )(*arrays)


def rope_base():
    half = HD // 2
    freq = np.exp(-(2.0 * np.arange(half) / HD) * math.log(ROPE_BASE))
    slot = np.arange(IMG)
    position = (slot % PH) * PW + slot // PH
    angle = position[:, None] * freq[None, :]
    cosine = np.concatenate([np.cos(angle), np.cos(angle)], axis=1)
    sine = np.concatenate([-np.sin(angle), np.sin(angle)], axis=1)
    return jnp.asarray(np.stack([cosine, sine]).astype(np.float32))


def shards(
    text_tokens,
    latent,
    image_offset,
    norm_gain,
    w_query,
    w_key,
    w_value,
    w_out,
    w_down_conv,
    w_down_proj,
    w_up_proj,
    w_up_out,
    pred_grad,
    text_grad,
):
    pred, text_out, grad_down_proj, grad_up_proj, grad_conv, grad_out = whole(
        {
            "offset": image_offset,
            "text": text_tokens[0],
            "tgrad": text_grad[0],
            "lat": latent[0],
            "gain": norm_gain,
            "pgrad": pred_grad[0],
            "wconv": w_down_conv,
            "w_uo": w_up_out.T,
            "base": rope_base(),
            "w_down": w_down_proj,
            "w_up": w_up_proj,
            "w_query": w_query,
            "w_key": w_key,
            "w_value": w_value,
            "w_out": w_out,
        },
        1,
    )
    pred, text_out, grad_down_proj, grad_up_proj, grad_conv, grad_out = results(
        pred, text_out, grad_down_proj, grad_up_proj, grad_conv, grad_out
    )
    return pred, text_out, grad_conv, grad_down_proj, grad_up_proj, grad_out.T


def solution(mesh):
    placed = (
        P("sy", "sx", None),
        P("sy", "sx", None),
        P("sy"),
        P(),
        P(None, "sx"),
        P(None, "sx"),
        P(None, "sx"),
        P("sx", None),
        P(),
        P(),
        P(),
        P(),
        P("sy", "sx", None),
        P("sy", "sx", None),
    )
    return jax.shard_map(
        shards,
        mesh=mesh,
        in_specs=placed,
        out_specs=(P("sy", "sx", None), P("sy", "sx", None), P(), P(), P(), P()),
        check_vma=False,
    )
```
